128 devices in a mesh: batch: 32 (over y, x, core), blk: 4 (over z).
Axes of the slice: x: 4, y: 4, z: 4, core: 2. Of those that a mesh axis runs over, the one named last changes fastest.
Arguments:
- stream: bfloat16 [32, 2040, 768], P('batch', 'blk'), may hold values from -6 to 6
- cotangent: bfloat16 [32, 2040, 768], P('batch', 'blk'), may hold values from -6 to 6
- passes: int32 [32], P('batch'), may hold values from 2 to 5
- w_qkv: bfloat16 [768, 2304], replicated, may hold values from -0.3125 to 0.3125
- w_out: bfloat16 [768, 768], replicated, may hold values from -0.625 to 0.625
- w_up: bfloat16 [768, 3072], replicated, may hold values from -0.21875 to 0.21875
- w_down: bfloat16 [3072, 768], replicated, may hold values from -0.109375 to 0.109375
- ln_gains: float32 [768, 2], replicated, may hold values from 0.5 to 1.5
- pass_embed: float32 [768, 5], replicated, may hold values from -3 to 3
Outputs:
- layer_out: bfloat16 [32, 2040, 768], P('batch', 'blk')
- grad_stream: float32 [32, 2040, 768], P('batch', 'blk')
- grad_qkv: float32 [768, 2304], P('blk')
- grad_out: float32 [768, 768], P('blk')
- grad_up: float32 [768, 3072], P('blk')
- grad_down: float32 [3072, 768], P('blk')
- grad_gains: float32 [768, 2], P('blk')
- grad_pass: float32 [768, 5], P('blk')
The draws below stay inside these ranges and needn't reach their ends.
Inputs may be any that keep to these rules, and one draw needn't show every extreme that they name: `passes`: 2040 is a multiple of every sequence's pass count.
All inputs are finite; a program needn't handle non-finite values.
Results may differ from the reference program's by a relative error of at most 0.012.
Values may be sent and summed in bfloat16 or wider, within the bound.
No kernel may reach another device: no remote copies, remote signals or barrier semaphores. Data moves between devices by JAX's collectives and lax.ppermute only.
A program may use at most 320 MiB of HBM per device.

```python
import jax
import jax.numpy as jnp
from jax import lax

D = 768
HEADS = 12
HD = 64
FF = 3072
PASSES = 5
STREAM = 2040
SEQS = 32


def place_ends(array, key, low, largest):
    longest = array.shape.index(max(array.shape))
    spots = []
    for shift in (0, 1):
        where = [jax.random.randint(jax.random.fold_in(key, axis), (), 0, length) for axis, length in enumerate(array.shape)]
        where[longest] = (where[longest] + shift) % array.shape[longest]
        spots.append(tuple(where))
    return array.at[spots[0]].set(low).at[spots[1]].set(largest)


def level_of(key, shape, pieces, low, high):
    level, own = 1.0, jax.random.fold_in(key, 6)
    for dim, blocks in pieces:
        draws = jnp.exp(jax.random.uniform(jax.random.fold_in(own, dim), (blocks,), jnp.float32, low / len(pieces), high / len(pieces)))
        level = level * jnp.repeat(draws, shape[dim] // blocks).reshape([-1 if axis == dim else 1 for axis in range(len(shape))])
    return level


def gaussian(rng, dims, spread, bound, cuts=(), kind=jnp.bfloat16):
    values = spread * jax.random.normal(rng, dims, jnp.float32)
    if cuts:
        values = values * level_of(rng, dims, cuts, -0.22, 0.18)
    return jnp.clip(values, -bound, bound).astype(kind)


def setup_inputs(seed: int = 0) -> dict:
    key_list = jax.random.split(jax.random.key(seed), 10)
    return {
        "stream": gaussian(key_list[0], (SEQS, STREAM, D), 1.0, 6.0, ((0, 32), (1, 4))),
        "cotangent": gaussian(key_list[1], (SEQS, STREAM, D), 1.0, 6.0, ((0, 32), (1, 4))),
        "passes": place_ends(jax.random.randint(key_list[2], (SEQS,), 2, 6), jax.random.fold_in(key_list[2], 1), 2, 5).astype(jnp.int32),
        "w_qkv": gaussian(key_list[3], (D, 3 * D), (D // 2) ** -0.5, 0.3125),
        "w_out": gaussian(key_list[4], (D, D), (D // 8) ** -0.5, 0.625),
        "w_up": gaussian(key_list[5], (D, FF), D ** -0.5, 0.21875),
        "w_down": gaussian(key_list[6], (FF, D), FF ** -0.5, 0.109375),
        "ln_gains": jnp.clip(1.0 + 0.1 * jax.random.normal(key_list[7], (D, 2), jnp.float32), 0.5, 1.5),
        "pass_embed": gaussian(key_list[8], (D, PASSES), 0.5, 3.0, (), jnp.float32),
    }


@jax.custom_vjp
def low(v):
    return lax.optimization_barrier(v.astype(jnp.bfloat16)).astype(jnp.float32)

@jax.custom_vjp
def low_back(v):
    return v

def low_keep(v):
    return (low(v), None)

def low_pass(kept, grad):
    return (grad,)

def back_keep(v):
    return (v, None)

def back_low(kept, grad):
    return (low(grad),)
low.defvjp(low_keep, low_pass)
low_back.defvjp(back_keep, back_low)
HIGH = lax.Precision.HIGHEST
EPS = 1e-05

def layer_norm(values, gain):
    mean = lax.optimization_barrier(jnp.mean(values, axis=-1, keepdims=True))
    centred = values - mean
    inverse = lax.rsqrt(lax.optimization_barrier(jnp.mean(centred * centred, axis=-1, keepdims=True)) + EPS)
    return centred * inverse * gain

def sequence_forward(params, seq, count):
    w_qkv, w_out, w_up, w_down, ln_gains, pass_embed = params
    position = jnp.arange(STREAM, dtype=jnp.int32)
    which = position % count
    hidden = seq + jnp.take(pass_embed, which, axis=1).T
    normed = low(layer_norm(hidden, ln_gains[:, 0]))
    qkv = low_back(low(jnp.dot(normed, w_qkv, precision=HIGH)))
    query = qkv[:, :D].reshape(STREAM, HEADS, HD)
    key = qkv[:, D:2 * D].reshape(STREAM, HEADS, HD)
    value = qkv[:, 2 * D:].reshape(STREAM, HEADS, HD)
    raw = low_back(jnp.einsum('qhd,khd->hqk', query, key, precision=HIGH))
    scaled = raw * HD ** (-0.5)
    allowed = position[:, None] >= position[None, :]
    scaled = jnp.where(allowed[None], scaled, -1e+30)
    top = lax.optimization_barrier(jnp.max(scaled, axis=-1, keepdims=True))
    expd = jnp.exp(scaled - top)
    probs = expd / lax.optimization_barrier(jnp.sum(expd, axis=-1, keepdims=True))
    attended = jnp.einsum('hqk,khd->qhd', low(probs), value, precision=HIGH).reshape(STREAM, D)
    attended = low_back(low(attended))
    branch = low_back(jnp.dot(attended, w_out, precision=HIGH))
    middle = hidden + branch
    second = low(layer_norm(middle, ln_gains[:, 1]))
    upward = low_back(jnp.dot(second, w_up, precision=HIGH))
    active = low(jax.nn.gelu(upward))
    return middle + jnp.dot(active, w_down, precision=HIGH)

def reference(stream, cotangent, passes, w_qkv, w_out, w_up, w_down, ln_gains, pass_embed):
    params = tuple((p.astype(jnp.float32) for p in (w_qkv, w_out, w_up, w_down, ln_gains, pass_embed)))

    def one_sequence(totals, item):
        seq, cot, count = item
        result, pull = jax.vjp(lambda prm, values: sequence_forward(prm, values, count), params, seq.astype(jnp.float32))
        grads, grad_seq = pull(cot.astype(jnp.float32))
        totals = jax.tree.map(lambda left, right: left + right, totals, grads)
        return (totals, (result.astype(jnp.bfloat16), grad_seq))
    zeros = jax.tree.map(jnp.zeros_like, params)
    totals, (outputs, grad_stream) = lax.scan(one_sequence, zeros, (stream, cotangent, passes))
    return (outputs, grad_stream, totals[0], totals[1], totals[2], totals[3], totals[4], totals[5])
```

```python
import jax
import jax.numpy as jnp
from jax import lax
from jax.experimental import pallas as pl
from jax.experimental.pallas import tpu as pltpu
from jax.sharding import PartitionSpec as P

D = 768
HEADS = 12
HD = 64
FF = 3072
PASSES = 5
ROWS = 510
R = 512
EPS = 1e-05
NEG = -1e30
BF = jnp.bfloat16
F32 = jnp.float32
VM = pl.BlockSpec(memory_space=pltpu.VMEM)
SM = pl.BlockSpec(memory_space=pltpu.SMEM)
HB = pl.BlockSpec(memory_space=pl.ANY)
PARAMS = pltpu.CompilerParams(vmem_limit_bytes=56 * 1024 * 1024)


def shape(dims, kind=BF):
    return jax.ShapeDtypeStruct(dims, kind)


def dot(left, right):
    return jnp.dot(left, right, preferred_element_type=F32)


def dot_nt(left, right):
    return lax.dot_general(left, right, (((1,), (1,)), ((), ())), preferred_element_type=F32)


def normalize(values):
    mean = jnp.mean(values, axis=-1, keepdims=True)
    centred = values - mean
    inverse = lax.rsqrt(jnp.mean(centred * centred, axis=-1, keepdims=True) + EPS)
    return centred * inverse, inverse


def norm_back(grad, unit, inverse, gain):
    scaled = grad * gain
    first = jnp.mean(scaled, axis=-1, keepdims=True)
    second = jnp.mean(scaled * unit, axis=-1, keepdims=True)
    return inverse * (scaled - first - unit * second)


def pass_index(blk, count):
    row = lax.broadcasted_iota(jnp.int32, (R, 1), 0) + blk * ROWS
    turns = jnp.floor((row.astype(F32) + 0.5) / count.astype(F32)).astype(jnp.int32)
    return row - turns * count


def pieces_out(stage, outs, blk):
    for d, out in enumerate(outs):
        out[...] = stage[lax.rem(blk + d, 4)]


def project(normed, weights, stage, outs, blk):
    for part, weight in enumerate(weights):
        got = dot(normed, weight[...])
        if part == 0:
            got = got.astype(BF) * jnp.asarray(HD ** (-0.5), BF)
        turned = got.astype(BF).T
        for j in range(4):
            stage[j, 64 * part : 64 * part + 64, :] = turned[64 * j : 64 * j + 64]
    pieces_out(stage, outs, blk)


def first_kernel(blk_ref, count_ref, stream, embed, gains, wq, wk, wv, hidden, normed, turned, p0, p1, p2, p3, stage):
    blk = blk_ref[0]
    hidden[R - 8 : R, :] = jnp.zeros((8, D), F32)
    hidden[0:ROWS, :] = stream[0].astype(F32)
    which = pass_index(blk, count_ref[0])
    added = embed[0:1, :]
    for r in range(1, PASSES):
        added = jnp.where(which == r, embed[r : r + 1, :], added)
    values = hidden[...] + added
    hidden[...] = values
    unit, _ = normalize(values)
    row = lax.broadcasted_iota(jnp.int32, (R, 1), 0)
    low = jnp.where(row < ROWS, unit * gains[0:1, :], 0.0).astype(BF)
    normed[...] = low
    project(low, (wq, wk, wv), stage, (p0, p1, p2, p3), blk)
    turned[...] = low.T


def second_kernel(blk_ref, normed, wq1, wk1, wv1, wq2, wk2, wv2, a0, a1, a2, a3, b0, b1, b2, b3, stage, stage2):
    blk = blk_ref[0]
    low = normed[...]
    project(low, (wq1, wk1, wv1), stage, (a0, a1, a2, a3), blk)
    project(low, (wq2, wk2, wv2), stage2, (b0, b1, b2, b3), blk)


def load_heads(blk, parts, q_rows, k_rows, v_rows, k_cols):
    for d in range(4):
        s = lax.rem(blk + 4 - d, 4)
        piece = parts[d]
        q_rows[s, 0:64, :] = piece[0:64, :]
        k_rows[s, 0:64, :] = piece[64:128, :]
        v_rows[s] = piece[128:192, :]
    row = lax.broadcasted_iota(jnp.int32, (64, R), 0)
    col = lax.broadcasted_iota(jnp.int32, (64, R), 1)
    one = jnp.where(row == 0, 1.0, 0.0).astype(BF)
    off = jnp.where((row == 0) & (col >= ROWS), NEG, 0.0).astype(BF)
    for s in range(4):
        q_rows[s, 64:128, :] = one
        k_rows[s, 64:128, :] = off
    for s in range(4):
        k_cols[s] = k_rows[s].T


def causal():
    key = lax.broadcasted_iota(jnp.int32, (R, R), 0)
    query = lax.broadcasted_iota(jnp.int32, (R, R), 1)
    return key <= query


def attend_kernel(blk_ref, r0, r1, r2, r3, p0, p1, p2, p3, attended, spread, q_rows, k_rows, v_rows, k_cols, scores, stage):
    blk = blk_ref[0]
    load_heads(blk, (r0, r1, r2, r3), q_rows, k_rows, v_rows, k_cols)
    for i in range(4):
        top = None
        for j in range(i + 1):
            got = dot(k_cols[j], q_rows[i])
            if i == j:
                got = jnp.where(causal(), got, NEG)
            scores[j] = got
            best = jnp.max(got, axis=0, keepdims=True)
            top = best if top is None else jnp.maximum(top, best)
        total = jnp.zeros((1, R), F32)
        summed = jnp.zeros((HD, R), F32)
        for j in range(i + 1):
            raised = jnp.exp(scores[j] - top)
            total = total + jnp.sum(raised, axis=0, keepdims=True)
            summed = summed + dot(v_rows[j], raised.astype(BF))
        result = summed / total
        attended[i] = result
        spread[i] = top + jnp.log(total)
        stage[i] = result.astype(BF)
    pieces_out(stage, (p0, p1, p2, p3), blk)


def attend_back_kernel(
    last, blk_ref, r0, r1, r2, r3, g0, g1, g2, g3, attended, spread, a0, a1, a2, a3, *rest
):
    if last:
        prev0, prev1, p0, p1, p2, p3, grad, q_rows, k_rows, v_rows, k_cols, q_cols, v_cols, o_rows, o_cols, delta, dq, outs = rest
    else:
        p0, p1, p2, p3, grad, q_rows, k_rows, v_rows, k_cols, q_cols, v_cols, o_rows, o_cols, delta, dq, outs = rest
    blk = blk_ref[0]
    load_heads(blk, (r0, r1, r2, r3), q_rows, k_rows, v_rows, k_cols)
    for d, piece in enumerate((g0, g1, g2, g3)):
        o_rows[lax.rem(blk + 4 - d, 4)] = piece[...]
    for s in range(4):
        q_cols[s] = q_rows[s].T
        v_cols[s] = v_rows[s].T
        o_cols[s] = o_rows[s].T
        delta[s] = jnp.sum(o_rows[s].astype(F32) * attended[s], axis=0, keepdims=True)
        dq[s] = jnp.zeros((HD, R), F32)
    for j in range(4):
        dk = jnp.zeros((R, 2 * HD), F32)
        dv = jnp.zeros((R, HD), F32)
        for i in range(j, 4):
            got = dot(k_cols[j], q_rows[i])
            if i == j:
                got = jnp.where(causal(), got, NEG)
            probs = jnp.exp(got - spread[i])
            d_probs = dot(v_cols[j], o_rows[i])
            d_scores = (probs * (d_probs - delta[i])).astype(BF)
            dv = dv + dot(probs.astype(BF), o_cols[i])
            dk = dk + dot(d_scores, q_cols[i])
            dq[i] = dq[i] + dot(k_rows[j, 0:64, :], d_scores)
        outs[j, 0:64, :] = (dq[j] * HD ** (-0.5)).astype(BF)
        outs[j, 64:128, :] = dk[:, 0:64].astype(BF).T
        outs[j, 128:192, :] = dv.astype(BF).T
        outs[j, 192:256, :] = jnp.zeros((64, R), BF)
    for d, out in enumerate((p0, p1, p2, p3)):
        out[...] = outs[lax.rem(blk + d, 4), 0:192, :]
    made = jnp.zeros((D, 256), F32)
    for d, piece in enumerate((a0, a1, a2, a3)):
        s = lax.rem(blk + 4 - d, 4)
        made = made + dot(piece[...], outs[s].T)
    if last:
        grad[:, 0:192] = prev0[...]
        grad[:, 192:384] = prev1[...]
        grad[:, 384:576] = made[:, 0:192].astype(BF)
    else:
        grad[...] = made[:, 0:192].astype(BF)


def gelu_both(value):
    c = (2.0 / jnp.pi) ** 0.5
    square = value * value
    t = jnp.tanh(c * value * (1.0 + 0.044715 * square))
    cdf = 0.5 * (1.0 + t)
    slope = cdf + (0.5 * c) * value * (1.0 - t * t) * (1.0 + 3.0 * 0.044715 * square)
    return value * cdf, slope


CHUNK = 512


def ff_kernel(
    blk_ref, r0, r1, r2, r3, hidden, cot, gains, w_out, w_up, w_down,
    active, d_up, second, middle, o_turned, d_branch, d_middle, gain_term, p0, p1, p2, p3,
    dy, back, stage,
):
    step = pl.program_id(0)

    @pl.when(step == 0)
    def _():
        blk = blk_ref[0]
        for d, piece in enumerate((r0, r1, r2, r3)):
            s = lax.rem(blk + 4 - d, 4)
            for g in range(3):
                stage[4 * g + s] = piece[64 * g : 64 * g + 64, :]
        o_rows = stage[...].reshape(D, R)
        o_turned[...] = o_rows
        values = hidden[...] + dot(o_rows.T, w_out[...])
        middle[...] = values
        unit, _ = normalize(values)
        second[...] = (unit * gains[1:2, :]).astype(BF)
        back[R - 8 : R, :] = jnp.zeros((8, D), F32)
        back[0:ROWS, :] = cot[0].astype(F32)
        dy[...] = back[...].astype(BF)
        back[...] = jnp.zeros((R, D), F32)

    upward = dot(second[...], w_up[...])
    act, slope = gelu_both(upward)
    active[...] = act.astype(BF)
    d_active = dot_nt(dy[...], w_down[...])
    d_upward = (d_active * slope).astype(BF)
    d_up[...] = d_upward
    back[...] += dot_nt(d_upward, w_up[...])

    @pl.when(step == FF // CHUNK - 1)
    def _():
        blk = blk_ref[0]
        unit, inverse = normalize(middle[...])
        grad = back[...]
        gain_term[...] = jnp.sum(grad * unit, axis=0, keepdims=True)
        total = dy[...].astype(F32) + norm_back(grad, unit, inverse, gains[1:2, :])
        d_middle[...] = total
        low = total.astype(BF)
        d_branch[...] = low
        stage[...] = dot_nt(w_out[...], low).astype(BF).reshape(HEADS, HD, R)
        for d, out in enumerate((p0, p1, p2, p3)):
            j = lax.rem(blk + d, 4)
            for g in range(3):
                out[64 * g : 64 * g + 64, :] = stage[4 * g + j]


def ff_grad_kernel(sel_ref, active, d_up, second, cot, o_turned, d_branch, up_out, down_out, out_out, dy, second_turned, pad):
    step = pl.program_id(0)

    @pl.when(step == 0)
    def _():
        pad[R - 8 : R, :] = jnp.zeros((8, D), F32)
        pad[0:ROWS, :] = cot[0].astype(F32)
        dy[...] = pad[...].astype(BF)
        second_turned[...] = second[...].T
        half = dot(o_turned[...], d_branch[...]).astype(BF)
        for i in range(4):
            for n in range(16):
                if n < 12:
                    out_out[n // 4, n % 4, i] = half[192 * i + 16 * n : 192 * i + 16 * n + 16, :]
                else:
                    out_out[n // 4, n % 4, i] = jnp.zeros((16, 384), BF)

    up = dot(second_turned[...], d_up[...]).astype(BF)
    for i in range(4):
        for yy in range(4):
            up_out[yy, 0, i] = up[192 * i + 48 * yy : 192 * i + 48 * yy + 48, :]
    down = dot(active[...].T, dy[...]).astype(BF)
    for yy in range(4):
        for xx in range(4):
            r = 48 * (2 * yy + xx // 2)
            down_out[yy, xx, 0] = down[r : r + 48, 384 * (xx % 2) : 384 * (xx % 2) + 384]


def layer_out_kernel(middle, active, w_down, out, total):
    step = pl.program_id(0)

    @pl.when(step == 0)
    def _():
        total[...] = middle[...]

    total[...] += dot(active[...], w_down[...])

    @pl.when(step == FF // CHUNK - 1)
    def _():
        out[0] = total[0:ROWS, :].astype(BF)


def last_kernel(
    blk_ref, count_ref, a0, a1, a2, a3, b0, b1, b2, b3, c0, c1, c2, c3, hidden, d_middle, gain_term, gains, w_qkv,
    grad_stream, small, stage,
):
    blk = blk_ref[0]
    for g, group in enumerate(((a0, a1, a2, a3), (b0, b1, b2, b3), (c0, c1, c2, c3))):
        for d, piece in enumerate(group):
            s = lax.rem(blk + 4 - d, 4)
            for part in range(3):
                stage[12 * part + 4 * g + s] = piece[64 * part : 64 * part + 64, :]
    grad = dot(w_qkv[...], stage[...].reshape(3 * D, R)).T
    unit, inverse = normalize(hidden[...])
    total = d_middle[...] + norm_back(grad, unit, inverse, gains[0:1, :])
    grad_stream[0] = total[0:ROWS, :]
    row = lax.broadcasted_iota(jnp.int32, (R, 1), 0)
    which = jnp.where(row < ROWS, pass_index(blk, count_ref[0]), -1)
    small[0:1, :] = jnp.sum(grad * unit, axis=0, keepdims=True)
    small[1:2, :] = gain_term[...]
    for r in range(PASSES):
        small[2 + r : 3 + r, :] = jnp.sum(jnp.where(which == r, total, 0.0), axis=0, keepdims=True)
    small[7:8, :] = jnp.zeros((1, D), F32)


def shift(values, axis, d):
    if axis == "z":
        return lax.ppermute(values, "blk", [(i, (i + d) % 4) for i in range(4)])
    pairs = []
    for b in range(32):
        y, x, core = b // 8, (b // 2) % 4, b % 2
        if axis == "y":
            y = (y + d) % 4
        elif axis == "x":
            x = (x + d) % 4
        else:
            core = (core + d) % 2
        pairs.append((b, 8 * y + 2 * x + core))
    return lax.ppermute(values, "batch", pairs)


def spread_pieces(pieces, axis):
    return (pieces[0],) + tuple(shift(pieces[d], axis, d) for d in (1, 2, 3))


def pick(values, index, dim):
    return lax.dynamic_index_in_dim(values, index, dim, keepdims=False)


def scatter_sum(terms, where, axis, dim):
    pieces = []
    for d in range(4):
        index = lax.rem(where + d, 4)
        pieces.append(sum(pick(t, index, dim).astype(F32) for t in terms).astype(BF))
    return spread_pieces(pieces, axis)


def add(terms):
    return sum(t.astype(F32) for t in terms)


def sum_four(values, axis):
    one, two, three = (shift(values, axis, d).astype(F32) for d in (1, 2, 3))
    return (values.astype(F32) + two) + (one + three)


def gather(piece, where, axis):
    got = jnp.stack((piece,) + tuple(shift(piece, axis, d) for d in (1, 2, 3)))
    return jnp.take(got, lax.rem(where + 4 - jnp.arange(4, dtype=jnp.int32), 4), axis=0)


def gather_core(piece, core):
    other = shift(piece, "core", 1)
    return jnp.where(core == 0, jnp.stack((piece, other)), jnp.stack((other, piece)))


def weight_spec(column):
    return pl.BlockSpec((D, 256), lambda *_, column=column: (0, column))


def on_device(stream, cotangent, passes, w_qkv, w_out, w_up, w_down, ln_gains, pass_embed):
    z = lax.axis_index("blk")
    batch = lax.axis_index("batch")
    core, x, y = batch % 2, (batch // 2) % 4, batch // 8
    blk = z.astype(jnp.int32).reshape(1)
    gains = ln_gains.T
    embed = pass_embed.T
    piece = shape((192, R))
    full = shape((R, D))

    hidden, normed, turned, *sent = pl.pallas_call(
        first_kernel,
        grid=(1,),
        in_specs=[SM, SM, VM, VM, VM, weight_spec(0), weight_spec(3), weight_spec(6)],
        out_specs=[VM] * 7,
        out_shape=[shape((R, D), F32), full, shape((D, R))] + [piece] * 4,
        scratch_shapes=[pltpu.VMEM((4, 192, R), BF)],
        compiler_params=PARAMS,
        name="ln_qkv_first",
    )(blk, passes, stream, embed, gains, w_qkv, w_qkv, w_qkv)
    heads = [spread_pieces(sent, "z")]
    sent = pl.pallas_call(
        second_kernel,
        grid=(1,),
        in_specs=[SM, VM] + [weight_spec(c) for c in (1, 4, 7, 2, 5, 8)],
        out_specs=[VM] * 8,
        out_shape=[piece] * 8,
        scratch_shapes=[pltpu.VMEM((4, 192, R), BF)] * 2,
        compiler_params=PARAMS,
        name="qkv_rest",
    )(blk, normed, *([w_qkv] * 6))
    heads += [spread_pieces(sent[:4], "z"), spread_pieces(sent[4:], "z")]

    attended, spreads, sent = [], [], []
    for g in range(3):
        *parts, result, spread = pl.pallas_call(
            attend_kernel,
            in_specs=[SM] + [VM] * 4,
            out_specs=[VM] * 6,
            out_shape=[shape((HD, R))] * 4 + [shape((4, HD, R), F32), shape((4, 1, R), F32)],
            scratch_shapes=[
                pltpu.VMEM((4, 128, R), BF),
                pltpu.VMEM((4, 128, R), BF),
                pltpu.VMEM((4, HD, R), BF),
                pltpu.VMEM((4, R, 128), BF),
                pltpu.VMEM((4, R, R), F32),
                pltpu.VMEM((4, HD, R), BF),
            ],
            compiler_params=PARAMS,
            name="attend",
        )(blk, *heads[g])
        attended.append(result)
        spreads.append(spread)
        sent.append(parts)
    back_o = spread_pieces([jnp.concatenate([sent[g][d] for g in range(3)], axis=0) for d in range(4)], "z")
    turned_all = spread_pieces((turned, turned, turned, turned), "z")

    whole = pl.BlockSpec(memory_space=pltpu.VMEM)
    active, d_up, second, middle, o_turned, d_branch, d_middle, gain_term, *sent = pl.pallas_call(
        ff_kernel,
        grid=(FF // CHUNK,),
        in_specs=[SM] + [VM] * 4 + [VM, VM, VM, VM]
        + [pl.BlockSpec((D, CHUNK), lambda f: (0, f)), pl.BlockSpec((CHUNK, D), lambda f: (f, 0))],
        out_specs=[pl.BlockSpec((R, CHUNK), lambda f: (0, f)), pl.BlockSpec((R, CHUNK), lambda f: (0, f))] + [whole] * 10,
        out_shape=[shape((R, FF)), shape((R, FF)), full, shape((R, D), F32), shape((D, R)), full, shape((R, D), F32), shape((1, D), F32)]
        + [piece] * 4,
        scratch_shapes=[pltpu.VMEM((R, D), BF), pltpu.VMEM((R, D), F32), pltpu.VMEM((HEADS, HD, R), BF)],
        compiler_params=PARAMS,
        name="ff",
    )(blk, *back_o, hidden, cotangent, gains, w_out, w_up, w_down)
    d_o = spread_pieces(sent, "z")

    def ff_grads(select):
        return pl.pallas_call(
            ff_grad_kernel,
            grid_spec=pltpu.PrefetchScalarGridSpec(
                num_scalar_prefetch=1,
                grid=(4,),
                in_specs=[
                    pl.BlockSpec((R, 384), lambda i, s: (0, 2 * i + s[0])),
                    pl.BlockSpec((R, 384), lambda i, s: (0, 2 * i + s[0])),
                    pl.BlockSpec((R, D), lambda i, s: (0, 0)),
                    pl.BlockSpec((1, ROWS, D), lambda i, s: (0, 0, 0)),
                    pl.BlockSpec((D, R), lambda i, s: (0, 0)),
                    pl.BlockSpec((R, 384), lambda i, s: (0, s[0])),
                ],
                out_specs=[
                    pl.BlockSpec((4, 1, 4, 48, 384), lambda i, s: (0, i, 0, 0, 0)),
                    pl.BlockSpec((4, 4, 1, 48, 384), lambda i, s: (0, 0, i, 0, 0)),
                    pl.BlockSpec((4, 4, 4, 16, 384), lambda i, s: (0, 0, 0, 0, 0)),
                ],
                scratch_shapes=[pltpu.VMEM((R, D), BF), pltpu.VMEM((D, R), BF), pltpu.VMEM((R, D), F32)],
            ),
            out_shape=[shape((4, 4, 4, 48, 384)), shape((4, 4, 4, 48, 384)), shape((4, 4, 4, 16, 384))],
            compiler_params=PARAMS,
            name="ff_grad",
        )(select, active, d_up, second, cotangent, o_turned, d_branch)

    core_index = core.astype(jnp.int32).reshape(1)
    other = ff_grads(1 - core_index)
    swapped = [shift(t, "core", 1) for t in other]
    mine = ff_grads(core_index)
    layer_out = pl.pallas_call(
        layer_out_kernel,
        grid=(FF // CHUNK,),
        in_specs=[VM, pl.BlockSpec((R, CHUNK), lambda f: (0, f)), pl.BlockSpec((CHUNK, D), lambda f: (f, 0))],
        out_specs=VM,
        out_shape=shape((1, ROWS, D)),
        scratch_shapes=[pltpu.VMEM((R, D), F32)],
        compiler_params=PARAMS,
        name="layer_out",
    )(middle, active, w_down)

    a_terms = scatter_sum((mine[0], swapped[0]), x, "x", 1)
    b_terms = scatter_sum((mine[1], swapped[1]), y, "y", 0)
    c_terms = scatter_sum((mine[2], swapped[2]), y, "y", 0)
    a_terms = scatter_sum(a_terms, y, "y", 0)
    b_terms = scatter_sum(b_terms, x, "x", 0)
    c_terms = scatter_sum(c_terms, x, "x", 0)
    bulk = [jnp.concatenate([a, b, c], axis=1) for a, b, c in zip(a_terms, b_terms, c_terms)]
    bulk = add(scatter_sum(bulk, z, "z", 0)).astype(BF)
    bulk = gather(gather(bulk, y, "y"), x, "x")
    bulk = gather_core(bulk, core).astype(F32)
    up, down, out = bulk[..., 0:48, :], bulk[..., 48:96, :], bulk[..., 96:112, :]
    grad_up = up.transpose(2, 3, 1, 0, 4).reshape(192, FF)
    down = down.reshape(2, 2, 2, 4, 48, 384)
    grad_down = down.transpose(0, 3, 1, 4, 2, 5).reshape(D, D)
    grad_out = out[:, :, 0:3].transpose(2, 1, 3, 0, 4).reshape(192, D)

    pieces, grads = [], []
    for g in range(3):
        last = g == 2
        *sent, grad = pl.pallas_call(
            lambda *refs, last=last: attend_back_kernel(last, *refs),
            grid=(1,),
            in_specs=[SM] + [VM] * 4 + [pl.BlockSpec((HD, R), lambda _, g=g: (g, 0))] * 4 + [VM] * 6 + [VM] * (2 if last else 0),
            out_specs=[VM] * 5,
            out_shape=[piece] * 4 + [shape((D, 576 if last else 192))],
            scratch_shapes=[
                pltpu.VMEM((4, 128, R), BF),
                pltpu.VMEM((4, 128, R), BF),
                pltpu.VMEM((4, HD, R), BF),
                pltpu.VMEM((4, R, 128), BF),
                pltpu.VMEM((4, R, 128), BF),
                pltpu.VMEM((4, R, HD), BF),
                pltpu.VMEM((4, HD, R), BF),
                pltpu.VMEM((4, R, HD), BF),
                pltpu.VMEM((4, 1, R), F32),
                pltpu.VMEM((4, HD, R), F32),
                pltpu.VMEM((4, 256, R), BF),
            ],
            compiler_params=PARAMS,
            name="attend_back",
        )(blk, *heads[g], *d_o, attended[g], spreads[g], *turned_all, *(grads if last else ()))
        grads.append(grad)
        pieces.extend(spread_pieces(sent, "z"))

    grad_stream, small = pl.pallas_call(
        last_kernel,
        in_specs=[SM, SM] + [VM] * 17,
        out_specs=[VM, VM],
        out_shape=[shape((1, ROWS, D), F32), shape((8, D), F32)],
        scratch_shapes=[pltpu.VMEM((36, HD, R), BF)],
        compiler_params=PARAMS,
        name="ln_back",
    )(blk, passes, *pieces, hidden, d_middle, gain_term, gains, w_qkv)

    made = grads[2].reshape(4, 2, 4, 24, 576)
    terms = (pick(made, core, 1), shift(pick(made, 1 - core, 1), "core", 1))
    terms = scatter_sum(terms, x, "x", 1)
    mid = add(terms).astype(BF)
    mid = sum_four(mid, "y").astype(BF)
    got = spread_pieces([pick(mid, lax.rem(z + d, 4), 0) for d in range(4)], "z")
    got = jnp.stack(got)
    got = gather_core(gather(got, x, "x"), core)
    got = jnp.take(got, lax.rem(z + 4 - jnp.arange(4, dtype=jnp.int32), 4), axis=2)
    got = got.reshape(2, 4, 4, 24, 3, 3, HD).transpose(0, 1, 3, 5, 4, 2, 6)
    grad_qkv = got.reshape(192, 3 * D).astype(F32)

    for axis in ("core", "x", "y", "z"):
        if axis == "core":
            small = small + shift(small, axis, 1)
        else:
            small = sum_four(small, axis)
    small = lax.dynamic_slice_in_dim(small.T, 192 * z, 192, 0)
    return (
        layer_out,
        grad_stream,
        grad_qkv,
        grad_out,
        grad_up,
        grad_down,
        small[:, 0:2],
        small[:, 2:7],
    )


def solution(mesh):
    tokens = P("batch", "blk", None)
    in_specs = (tokens, tokens, P("batch"), P(), P(), P(), P(), P(), P())
    out_specs = (tokens, tokens) + (P("blk", None),) * 6
    return jax.shard_map(on_device, mesh=mesh, in_specs=in_specs, out_specs=out_specs, check_vma=False)
```

```python
import jax
import jax.numpy as jnp
from jax import lax
from jax.experimental import pallas as pl
from jax.experimental.pallas import tpu as pltpu
from jax.sharding import PartitionSpec as P

D = 768
HEADS = 12
HD = 64
FF = 3072
PASSES = 5
ROWS = 510
R = 512
EPS = 1e-05
NEG = -1e30
BF = jnp.bfloat16
F32 = jnp.float32
VM = pl.BlockSpec(memory_space=pltpu.VMEM)
SM = pl.BlockSpec(memory_space=pltpu.SMEM)
HB = pl.BlockSpec(memory_space=pl.ANY)
MIB = 1024 * 1024


def room(mib):
    return pltpu.CompilerParams(vmem_limit_bytes=mib * MIB)


def run(kernel, name, mib, outs, operands, scratch=(), scalars=1):
    return pl.pallas_call(
        kernel,
        in_specs=[SM] * scalars + [VM] * (len(operands) - scalars),
        out_specs=[VM] * len(outs),
        out_shape=outs,
        scratch_shapes=list(scratch),
        compiler_params=room(mib),
        name=name,
    )(*operands)


def shape(dims, kind=BF):
    return jax.ShapeDtypeStruct(dims, kind)


def dot(left, right):
    return jnp.dot(left, right, preferred_element_type=F32)


def dot_nt(left, right):
    return lax.dot_general(left, right, (((1,), (1,)), ((), ())), preferred_element_type=F32)


def normalize(values):
    mean = jnp.mean(values, axis=-1, keepdims=True)
    centred = values - mean
    inverse = lax.rsqrt(jnp.mean(centred * centred, axis=-1, keepdims=True) + EPS)
    return centred * inverse, inverse


def norm_back(grad, unit, inverse, gain):
    scaled = grad * gain
    first = jnp.mean(scaled, axis=-1, keepdims=True)
    second = jnp.mean(scaled * unit, axis=-1, keepdims=True)
    return inverse * (scaled - first - unit * second)


def pass_index(blk, count):
    row = lax.broadcasted_iota(jnp.int32, (R, 1), 0) + blk * ROWS
    turns = jnp.floor((row.astype(F32) + 0.5) / count.astype(F32)).astype(jnp.int32)
    return row - turns * count


def pieces_out(stage, outs, blk):
    for d, out in enumerate(outs):
        out[...] = stage[lax.rem(blk + d, 4)]


def project(normed, weights, stage, outs, blk):
    for part, weight in enumerate(weights):
        got = dot(normed, weight[...])
        if part == 0:
            got = got.astype(BF) * jnp.asarray(HD ** (-0.5), BF)
        turned = got.astype(BF).T
        for j in range(4):
            stage[j, 64 * part : 64 * part + 64, :] = turned[64 * j : 64 * j + 64]
    pieces_out(stage, outs, blk)


def first_kernel(
    blk_ref, count_ref, stream, embed, gains, wq, wk, wv, hidden, p0, p1, p2, p3, q0, q1, q2, q3, turned, normed, stage
):
    group = pl.program_id(0)
    blk = blk_ref[0]

    @pl.when(group == 0)
    def _():
        hidden[R - 8 : R, :] = jnp.zeros((8, D), F32)
        hidden[0:ROWS, :] = stream[0].astype(F32)
        which = pass_index(blk, count_ref[0])
        added = embed[0:1, :]
        for r in range(1, PASSES):
            added = jnp.where(which == r, embed[r : r + 1, :], added)
        values = hidden[...] + added
        hidden[...] = values
        unit, _ = normalize(values)
        row = lax.broadcasted_iota(jnp.int32, (R, 1), 0)
        low = jnp.where(row < ROWS, unit * gains[0:1, :], 0.0).astype(BF)
        normed[...] = low
        turned[...] = low.T

    for part, weight in enumerate((wq, wk, wv)):
        got = dot(normed[...], weight[...])
        if part == 0:
            got = got.astype(BF) * jnp.asarray(HD ** (-0.5), BF)
        flipped = got.astype(BF).T
        for j in range(4):
            stage[j, 64 * part : 64 * part + 64, :] = flipped[64 * j : 64 * j + 64]
    for d, (early, late) in enumerate(((p0, q0), (p1, q1), (p2, q2), (p3, q3))):
        piece = stage[lax.rem(blk + d, 4)]

        @pl.when(group == 0)
        def _():
            early[0:192, :] = piece

        @pl.when(group == 1)
        def _():
            early[192:384, :] = piece

        @pl.when(group == 2)
        def _():
            late[...] = piece


def load_heads(blk, at, parts, q_rows, k_rows, v_rows, k_cols):
    for d in range(4):
        s = lax.rem(blk + 4 - d, 4)
        piece = parts[d]
        q_rows[s, 0:64, :] = piece[at : at + 64, :]
        k_rows[s, 0:64, :] = piece[at + 64 : at + 128, :]
        v_rows[s] = piece[at + 128 : at + 192, :]
    row = lax.broadcasted_iota(jnp.int32, (64, R), 0)
    col = lax.broadcasted_iota(jnp.int32, (64, R), 1)
    one = jnp.where(row == 0, 1.0, 0.0).astype(BF)
    off = jnp.where((row == 0) & (col >= ROWS), NEG, 0.0).astype(BF)
    for s in range(4):
        q_rows[s, 64:128, :] = one
        k_rows[s, 64:128, :] = off
    for s in range(4):
        k_cols[s] = k_rows[s].T


def causal():
    key = lax.broadcasted_iota(jnp.int32, (R, R), 0)
    query = lax.broadcasted_iota(jnp.int32, (R, R), 1)
    return key <= query


def attend_kernel(g, blk_ref, r0, r1, r2, r3, *rest):
    last = g == 2
    earlier, rest = (rest[:8], rest[8:]) if last else ((), rest)
    p0, p1, p2, p3, attended, spread, q_rows, k_rows, v_rows, k_cols, scores, stage = rest
    blk = blk_ref[0]
    load_heads(blk, 192 if g == 1 else 0, (r0, r1, r2, r3), q_rows, k_rows, v_rows, k_cols)
    for i in range(4):
        top = None
        for j in range(i + 1):
            got = dot(k_cols[j], q_rows[i])
            if i == j:
                got = jnp.where(causal(), got, NEG)
            scores[j] = got
            best = jnp.max(got, axis=0, keepdims=True)
            top = best if top is None else jnp.maximum(top, best)
        total = jnp.zeros((1, R), F32)
        summed = jnp.zeros((HD, R), F32)
        for j in range(i + 1):
            raised = jnp.exp(scores[j] - top)
            total = total + jnp.sum(raised, axis=0, keepdims=True)
            summed = summed + dot(v_rows[j], raised.astype(BF))
        result = summed / total
        attended[i] = result
        spread[i] = top + jnp.log(total)
        stage[i] = result.astype(BF)
    for d, out in enumerate((p0, p1, p2, p3)):
        piece = stage[lax.rem(blk + d, 4)]
        if last:
            out[0:64, :] = earlier[d][...]
            out[64:128, :] = earlier[4 + d][...]
            out[128:192, :] = piece
        else:
            out[...] = piece


def attend_back_kernel(g, blk_ref, r0, r1, r2, r3, g0, g1, g2, g3, attended, spread, *rest):
    last = g == 2
    if last:
        t0, t1, t2, t3, e0, e1, p0, p1, p2, p3, keep, send, *rest = rest
        outs, made, *rest = rest
    else:
        p0, p1, p2, p3, outs, *rest = rest
    q_rows, k_rows, v_rows, k_cols, q_cols, v_cols, o_rows, o_cols, delta, dq = rest
    blk = blk_ref[0]
    load_heads(blk, 192 if g == 1 else 0, (r0, r1, r2, r3), q_rows, k_rows, v_rows, k_cols)
    for d, piece in enumerate((g0, g1, g2, g3)):
        o_rows[lax.rem(blk + 4 - d, 4)] = piece[...]
    for s in range(4):
        q_cols[s] = q_rows[s].T
        v_cols[s] = v_rows[s].T
        o_cols[s] = o_rows[s].T
        delta[s] = jnp.sum(o_rows[s].astype(F32) * attended[s], axis=0, keepdims=True)
        dq[s] = jnp.zeros((HD, R), F32)
    at = 384 if last else 0
    for j in range(4):
        dk = jnp.zeros((R, 2 * HD), F32)
        dv = jnp.zeros((R, HD), F32)
        for i in range(j, 4):
            got = dot(k_cols[j], q_rows[i])
            if i == j:
                got = jnp.where(causal(), got, NEG)
            probs = jnp.exp(got - spread[i])
            d_probs = dot(v_cols[j], o_rows[i])
            d_scores = (probs * (d_probs - delta[i])).astype(BF)
            dv = dv + dot(probs.astype(BF), o_cols[i])
            dk = dk + dot(d_scores, q_cols[i])
            dq[i] = dq[i] + dot(k_rows[j, 0:64, :], d_scores)
        outs[j, at : at + 64, :] = (dq[j] * HD ** (-0.5)).astype(BF)
        outs[j, at + 64 : at + 128, :] = dk[:, 0:64].astype(BF).T
        outs[j, at + 128 : at + 192, :] = dv.astype(BF).T
    for d, out in enumerate((p0, p1, p2, p3)):
        out[...] = outs[lax.rem(blk + d, 4), at : at + 192, :]
    if last:
        for s in range(4):
            outs[s, 0:192, :] = e0[s]
            outs[s, 192:384, :] = e1[s]
            outs[s, 576:640, :] = jnp.zeros((64, R), BF)
        total = jnp.zeros((D, 640), F32)
        for d, piece in enumerate((t0, t1, t2, t3)):
            total = total + dot_nt(piece[...], outs[lax.rem(blk + 4 - d, 4)])
        made[...] = total
        core = blk_ref[3]
        for i in range(4):
            for xx in range(4):
                for out, c in ((keep, core), (send, 1 - core)):
                    row = pl.multiple_of(192 * i + 24 * xx + 96 * c, 8)
                    part = jnp.concatenate([made[pl.ds(row, 24), :], jnp.zeros((8, 640), F32)], axis=0)
                    out[xx, i] = part.astype(BF)


def gelu_both(value):
    c = (2.0 / jnp.pi) ** 0.5
    square = value * value
    t = jnp.tanh(c * value * (1.0 + 0.044715 * square))
    cdf = 0.5 * (1.0 + t)
    slope = cdf + (0.5 * c) * value * (1.0 - t * t) * (1.0 + 3.0 * 0.044715 * square)
    return value * cdf, slope


CHUNK = 384


def up_cut(values, store):
    for z in range(4):
        for yy in range(4):
            store(yy, z, values[192 * z + 48 * yy : 192 * z + 48 * yy + 48, :])


def down_cut(values, store):
    for yy in range(4):
        for xx in range(4):
            r, col = 48 * (2 * yy + xx // 2), 384 * (xx % 2)
            store(yy, xx, values[r : r + 48, col : col + 384])


def put_block(out, at, rows):
    out[at] = rows.astype(BF)


def ff_kernel(
    blk_ref, r0, r1, r2, r3, hidden, cot, gains, w_out, w_up, w_down,
    active, d_up, second, middle, o_turned, d_branch, d_middle, p0, p1, p2, p3, a_out, b_out, gain_term,
    dy, back, stage, second_turned,
):
    step = pl.program_id(0)
    core = blk_ref[3]

    @pl.when(step == 0)
    def _():
        blk = blk_ref[0]
        for d, piece in enumerate((r0, r1, r2, r3)):
            s = lax.rem(blk + 4 - d, 4)
            for g in range(3):
                stage[4 * g + s] = piece[64 * g : 64 * g + 64, :]
        o_rows = stage[...].reshape(D, R)
        o_turned[...] = o_rows
        values = hidden[...] + dot(o_rows.T, w_out[...])
        middle[...] = values
        unit, _ = normalize(values)
        second[...] = (unit * gains[1:2, :]).astype(BF)
        back[R - 8 : R, :] = jnp.zeros((8, D), F32)
        back[0:ROWS, :] = cot[0].astype(F32)
        dy[...] = back[...].astype(BF)
        back[...] = jnp.zeros((R, D), F32)
        second_turned[...] = second[...].T

    upward = dot(second[...], w_up[...])
    act, slope = gelu_both(upward)
    act = act.astype(BF)
    active[...] = act
    d_active = dot_nt(dy[...], w_down[...])
    d_upward = (d_active * slope).astype(BF)
    d_up[...] = d_upward
    back[...] += dot_nt(d_upward, w_up[...])

    @pl.when(lax.rem(step, 2) != core)
    def _():
        i = step // 2
        up_cut(dot(second_turned[...], d_upward), lambda yy, z, rows: put_block(a_out, (yy, i, z), rows))
        down_cut(dot(act.T, dy[...]), lambda yy, xx, rows: put_block(b_out, (yy, xx, i, slice(0, 48)), rows))

    @pl.when(step == FF // CHUNK - 1)
    def _():
        blk = blk_ref[0]
        unit, inverse = normalize(middle[...])
        grad = back[...]
        gain_term[...] = jnp.sum(grad * unit, axis=0, keepdims=True)
        total = dy[...].astype(F32) + norm_back(grad, unit, inverse, gains[1:2, :])
        d_middle[...] = total
        low = total.astype(BF)
        d_branch[...] = low
        stage[...] = dot_nt(w_out[...], low).astype(BF).reshape(HEADS, HD, R)
        half = dot(o_turned[...], jnp.where(core == 0, low[:, 384:768], low[:, 0:384])).astype(BF)
        for i in range(4):
            for n in range(16):
                rows = half[192 * i + 16 * n : 192 * i + 16 * n + 16, :] if n < 12 else jnp.zeros((16, 384), BF)
                b_out[n // 4, n % 4, i, 48:64] = rows
        for d, out in enumerate((p0, p1, p2, p3)):
            j = lax.rem(blk + d, 4)
            for g in range(3):
                out[64 * g : 64 * g + 64, :] = stage[4 * g + j]


def ff_grad_kernel(
    place_ref, active, d_up, second, cot, o_turned, d_branch, got_a, got_b, a0, a1, a2, a3, b0, b1, b2, b3,
    dy, second_turned, pad, kept, half_out,
):
    step = pl.program_id(0)
    x, y = place_ref[1], place_ref[2]
    chunk = lax.rem(x + step, 4)

    @pl.when(step == 0)
    def _():
        pad[R - 8 : R, :] = jnp.zeros((8, D), F32)
        pad[0:ROWS, :] = cot[0].astype(F32)
        dy[...] = pad[...].astype(BF)
        second_turned[...] = second[...].T
        half_out[...] = dot(o_turned[...], d_branch[...])

    up = dot(second_turned[...], d_up[...])
    down = dot(active[...].T, dy[...])
    for s, out in enumerate((a0, a1, a2, a3)):
        @pl.when(step == s)
        def _():
            up_cut(up, lambda yy, z, rows: put_block(out, (yy, z), rows + got_a[yy, 0, z].astype(F32)))

    def keep_down(yy, xx, rows):
        kept[yy, xx, 0:48] = (rows + got_b[yy, xx, 0, 0:48].astype(F32)).astype(BF)

    down_cut(down, keep_down)
    half = half_out[pl.ds(pl.multiple_of(192 * chunk, 8), 192), :]
    for n in range(16):
        if n < 12:
            rows = half[16 * n : 16 * n + 16, :] + got_b[n // 4, n % 4, 0, 48:64].astype(F32)
            kept[n // 4, n % 4, 48:64] = rows.astype(BF)
        else:
            kept[n // 4, n % 4, 48:64] = jnp.zeros((16, 384), BF)
    for d, out in enumerate((b0, b1, b2, b3)):
        out[:, pl.ds(chunk, 1)] = kept[lax.rem(y + d, 4)][:, None]


def total_of(parts):
    return (parts[0].astype(F32) + parts[2].astype(F32)) + (parts[1].astype(F32) + parts[3].astype(F32))


TINY = 96
GROUP = 160
PART_A = 144
PART_B = 192


def put(buffer, at, block):
    rows, lanes = block.shape
    for t in range(lanes // 128):
        buffer[at + rows * t : at + rows * t + rows, :] = block[:, 128 * t : 128 * t + 128]


def put_small(buffer, at, value):
    high = value.astype(BF)
    low = (value - high.astype(F32)).astype(BF)
    put(buffer, at, jnp.concatenate([high, low], axis=0))


def get_small(buffer, at):
    parts = []
    for t in range(6):
        part = buffer[at + 16 * t : at + 16 * t + 16, :].astype(F32)
        parts.append(part[0:8] + part[8:16])
    return jnp.concatenate(parts, axis=1)


def take(buffer, at, rows):
    return jnp.concatenate([buffer[at + rows * t : at + rows * t + rows, :] for t in range(3)], axis=1)


def cut_kernel(place_ref, a0, a1, a2, a3, b0, b1, b2, b3, keep, got, y0, y1, y2, y3, x0, x1, x2, x3):
    x, y = place_ref[1], place_ref[2]
    for d, (y_out, x_out) in enumerate(((y0, x0), (y1, x1), (y2, x2), (y3, x3))):
        yy, xx = lax.rem(y + d, 4), lax.rem(x + d, 4)
        a_sum = total_of([r[yy] for r in (a0, a1, a2, a3)]).astype(BF)
        heads = (keep[yy].astype(F32) + got[yy].astype(F32)).astype(BF)
        for i in range(4):
            put(y_out, PART_A * i, a_sum[i])
            put(y_out, 4 * PART_A + GROUP * i, heads[i])
        x_out[...] = total_of([r[xx] for r in (b0, b1, b2, b3)]).astype(BF)


def block_kernel(place_ref, y0, y1, y2, y3, x0, x1, x2, x3, small, o0, o1, o2, o3):
    z = place_ref[0]
    for d, out in enumerate((o0, o1, o2, o3)):
        i = lax.rem(z + d, 4)
        start = pl.multiple_of(PART_A * i, 16)
        out[0:PART_A, :] = total_of([r[pl.ds(start, PART_A), :] for r in (y0, y1, y2, y3)]).astype(BF)
        put(out, PART_A, total_of([r[i] for r in (x0, x1, x2, x3)]).astype(BF))
        start = pl.multiple_of(4 * PART_A + GROUP * i, 16)
        at = PART_A + PART_B
        out[at : at + GROUP, :] = total_of([r[pl.ds(start, GROUP), :] for r in (y0, y1, y2, y3)]).astype(BF)
        put_small(out, at + GROUP, small[...])


def own_kernel(place_ref, z0, z1, z2, z3, x_out, y_out):
    parts = (z0, z1, z2, z3)
    at = PART_A + PART_B
    for d, r in enumerate(parts):
        x_out[GROUP * d : GROUP * d + GROUP, :] = r[at : at + GROUP, :]
    put_small(x_out, 4 * GROUP, total_of([get_small(r, at + GROUP) for r in parts]))
    x_out[4 * GROUP + TINY : 4 * GROUP + TINY + PART_A, :] = total_of([r[0:PART_A, :] for r in parts]).astype(BF)
    y_out[...] = total_of([r[PART_A : PART_A + PART_B, :] for r in parts]).astype(BF)


def row_kernel(place_ref, x0, x1, x2, x3, y0, y1, y2, y3, y_out, x_out):
    parts = (x0, x1, x2, x3)
    y_out[0 : 4 * GROUP, :] = total_of([r[0 : 4 * GROUP, :] for r in parts]).astype(BF)
    put_small(y_out, 4 * GROUP, total_of([get_small(r, 4 * GROUP) for r in parts]))
    at = 4 * GROUP + TINY
    for d, (a, b) in enumerate(zip(parts, (y0, y1, y2, y3))):
        y_out[at + PART_A * d : at + PART_A * d + PART_A, :] = a[at : at + PART_A, :]
        x_out[PART_B * d : PART_B * d + PART_B, :] = b[...]


ALL_TINY = 16 * GROUP
ALL_A = ALL_TINY + TINY
ALL_B = ALL_A + 16 * PART_A
ALL = ALL_B + 16 * PART_B


def stack_kernel(place_ref, y0, y1, y2, y3, x0, x1, x2, x3, out):
    parts = (y0, y1, y2, y3)
    put_small(out, ALL_TINY, total_of([get_small(r, 4 * GROUP) for r in parts]))
    at = 4 * GROUP + TINY
    for d, (r, b) in enumerate(zip(parts, (x0, x1, x2, x3))):
        out[4 * GROUP * d : 4 * GROUP * d + 4 * GROUP, :] = r[0 : 4 * GROUP, :]
        out[ALL_A + 4 * PART_A * d : ALL_A + 4 * PART_A * d + 4 * PART_A, :] = r[at : at + 4 * PART_A, :]
        out[ALL_B + 4 * PART_B * d : ALL_B + 4 * PART_B * d + 4 * PART_B, :] = b[...]


def finish_kernel(place_ref, mine, other, grad_qkv, grad_out, grad_up, grad_down, gains, passes, pair, turned):
    z, x, y, core = place_ref[0], place_ref[1], place_ref[2], place_ref[3]
    pair[core] = mine[...]
    pair[1 - core] = other[...]

    def rows(c, at, count):
        return pair[c, pl.ds(pl.multiple_of(at, 16), count), :].astype(F32)

    for c in range(2):
        for xx in range(4):
            dx = lax.rem(x + 4 - xx, 4)
            for yy in range(4):
                dy = lax.rem(y + 4 - yy, 4)
                a = rows(c, ALL_A + 4 * PART_A * dy + PART_A * dx, PART_A)
                b = rows(c, ALL_B + 4 * PART_B * dx + PART_B * dy, PART_B)
                r = 384 * c + 48 * (2 * yy + xx // 2)
                for t in range(3):
                    col = 384 * (2 * xx + c) + 128 * t
                    grad_up[48 * yy : 48 * yy + 48, col : col + 128] = a[48 * t : 48 * t + 48]
                    col = 384 * (xx % 2) + 128 * t
                    grad_down[r : r + 48, col : col + 128] = b[64 * t : 64 * t + 48]
                    if yy < 3:
                        n, col = 16 * (4 * yy + xx), 384 * c + 128 * t
                        grad_out[n : n + 16, col : col + 128] = b[64 * t + 48 : 64 * t + 64]
        for yy in range(4):
            dy = lax.rem(y + 4 - yy, 4)
            for j in range(4):
                dz = lax.rem(z + 4 - j, 4)
                piece = rows(c, 4 * GROUP * dy + GROUP * dz, GROUP)
                r = 96 * c + 24 * yy
                for n in range(9):
                    lane = 64 * n
                    block = piece[32 * (lane // 128) : 32 * (lane // 128) + 24, lane % 128 : lane % 128 + 64]
                    col = D * (n % 3) + 64 * (4 * (n // 3) + j)
                    grad_qkv[r : r + 24, col : col + 64] = block
    small = get_small(mine, ALL_TINY) + get_small(other, ALL_TINY)
    turned[...] = small.T
    part = turned[pl.ds(pl.multiple_of(192 * z, 8), 192), :]
    gains[...] = part[:, 0:2]
    passes[...] = part[:, 2:7]


def layer_out_kernel(place_ref, middle, active, w_down, out, total):
    step = pl.program_id(0)

    @pl.when(step == 0)
    def _():
        total[...] = middle[...]

    total[...] += dot(active[...], w_down[...])

    @pl.when(step == FF // CHUNK - 1)
    def _():
        out[0] = total[0:ROWS, :].astype(BF)


def input_grad_kernel(blk_ref, a0, a1, a2, a3, b0, b1, b2, b3, w_qkv, out, stage):
    blk = blk_ref[0]
    stage[...] = jnp.zeros((36, HD, R), BF)
    for g, group in enumerate(((a0, a1, a2, a3), (b0, b1, b2, b3))):
        for d, piece in enumerate(group):
            s = lax.rem(blk + 4 - d, 4)
            for part in range(3):
                stage[12 * part + 4 * g + s] = piece[64 * part : 64 * part + 64, :]
    out[...] = dot(w_qkv[...], stage[...].reshape(3 * D, R))


def last_kernel(
    blk_ref, count_ref, c0, c1, c2, c3, so_far, hidden, d_middle, gain_term, gains, wq, wk, wv, grad_stream, small, stage
):
    blk = blk_ref[0]
    for d, piece in enumerate((c0, c1, c2, c3)):
        s = lax.rem(blk + 4 - d, 4)
        for part in range(3):
            stage[part, s] = piece[64 * part : 64 * part + 64, :]
    turned = so_far[...]
    for part, weight in enumerate((wq, wk, wv)):
        turned = turned + dot(weight[...], stage[part].reshape(256, R))
    grad = turned.T
    unit, inverse = normalize(hidden[...])
    total = d_middle[...] + norm_back(grad, unit, inverse, gains[0:1, :])
    grad_stream[0] = total[0:ROWS, :]
    row = lax.broadcasted_iota(jnp.int32, (R, 1), 0)
    which = jnp.where(row < ROWS, pass_index(blk, count_ref[0]), -1)
    small[0:1, :] = jnp.sum(grad * unit, axis=0, keepdims=True)
    small[1:2, :] = gain_term[...]
    for r in range(PASSES):
        small[2 + r : 3 + r, :] = jnp.sum(jnp.where(which == r, total, 0.0), axis=0, keepdims=True)
    small[7:8, :] = jnp.zeros((1, D), F32)


def shift(values, axis, d):
    if axis == "z":
        return lax.ppermute(values, "blk", [(i, (i + d) % 4) for i in range(4)])
    pairs = []
    for b in range(32):
        y, x, core = b // 8, (b // 2) % 4, b % 2
        if axis == "y":
            y = (y + d) % 4
        elif axis == "x":
            x = (x + d) % 4
        else:
            core = (core + d) % 2
        pairs.append((b, 8 * y + 2 * x + core))
    return lax.ppermute(values, "batch", pairs)


def spread_pieces(pieces, axis):
    return (pieces[0],) + tuple(shift(pieces[d], axis, d) for d in (1, 2, 3))


def all_of(value, axis):
    return spread_pieces((value,) * 4, axis)


def after(value, *others):
    return lax.optimization_barrier((value,) + others)[0]


def far(value):
    return pltpu.with_memory_space_constraint(value, pltpu.HBM)


def weight_spec(column):
    return pl.BlockSpec((D, 256), lambda *_, column=column: (0, column))


def on_device(stream, cotangent, passes, w_qkv, w_out, w_up, w_down, ln_gains, pass_embed):
    z = lax.axis_index("blk").astype(jnp.int32)
    batch = lax.axis_index("batch").astype(jnp.int32)
    place = jnp.stack([z, batch // 2 % 4, batch // 8, batch % 2])
    gains = ln_gains.T
    embed = pass_embed.T
    piece = shape((192, R))
    full = shape((R, D))

    def arrived(*values):
        nonlocal place
        place = lax.optimization_barrier((place,) + values)[0]

    def ordered(outs):
        nonlocal place
        *outs, first = outs
        place, first = lax.optimization_barrier((place, first))
        return (*outs, first)

    hidden, *sent, turned = ordered(pl.pallas_call(
        first_kernel,
        grid=(3,),
        in_specs=[SM, SM, VM, VM, VM, *(pl.BlockSpec((D, 256), lambda g, part=part: (0, 3 * part + g)) for part in range(3))],
        out_specs=[VM] * 10,
        out_shape=[shape((R, D), F32)] + [shape((384, R))] * 4 + [piece] * 4 + [shape((D, R))],
        scratch_shapes=[pltpu.VMEM((R, D), BF), pltpu.VMEM((4, 192, R), BF)],
        compiler_params=room(24),
        name="ln_qkv",
    )(place, passes, far(stream), embed, gains, *([far(w_qkv)] * 3)))
    early, late = spread_pieces(sent[:4], "z"), spread_pieces(sent[4:], "z")
    heads = (early, early, late)

    attended, spreads, sent = [], [], []
    for g in range(3):
        *parts, result, spread = ordered(run(
            lambda *refs, g=g: attend_kernel(g, *refs),
            "attend",
            24,
            [shape((192 if g == 2 else HD, R))] * 4 + [shape((4, HD, R), F32), shape((4, 1, R), F32)],
            (place, *(far(h) for h in heads[g]), *(sent if g == 2 else ())),
            [
                pltpu.VMEM((4, 128, R), BF),
                pltpu.VMEM((4, 128, R), BF),
                pltpu.VMEM((4, HD, R), BF),
                pltpu.VMEM((4, R, 128), BF),
                pltpu.VMEM((4, R, R), F32),
                pltpu.VMEM((4, HD, R), BF),
            ],
        ))
        attended.append(result)
        spreads.append(spread)
        sent += parts
    back_o = spread_pieces(sent[8:], "z")
    near = after(turned, *back_o)
    near = (shift(near, "z", 1), shift(near, "z", 3))

    active, d_up, second, middle, o_turned, d_branch, d_middle, *sent, a_other, b_other, gain_term = ordered(pl.pallas_call(
        ff_kernel,
        grid=(FF // CHUNK,),
        in_specs=[SM] + [VM] * 4 + [VM, VM, VM, VM]
        + [pl.BlockSpec((D, CHUNK), lambda f: (0, f)), pl.BlockSpec((CHUNK, D), lambda f: (f, 0))],
        out_specs=[pl.BlockSpec((R, CHUNK), lambda f: (0, f)), pl.BlockSpec((R, CHUNK), lambda f: (0, f))] + [VM] * 12,
        out_shape=[shape((R, FF)), shape((R, FF)), full, shape((R, D), F32), shape((D, R)), full, shape((R, D), F32)]
        + [piece] * 4 + [shape((4, 4, 4, 48, 384)), shape((4, 4, 4, 64, 384)), shape((1, D), F32)],
        scratch_shapes=[pltpu.VMEM((R, D), BF), pltpu.VMEM((R, D), F32), pltpu.VMEM((HEADS, HD, R), BF), pltpu.VMEM((D, R), BF)],
        compiler_params=room(36),
        name="ff",
    )(place, *(far(o) for o in back_o), far(hidden), far(cotangent), gains, far(w_out), far(w_up), far(w_down)))
    *sent, a_other, b_other = lax.optimization_barrier((*sent, a_other, b_other, *near))[:6]
    d_o = spread_pieces(sent, "z")

    got = (shift(a_other, "core", 1), shift(b_other, "core", 1))
    layer_out = ordered((pl.pallas_call(
        layer_out_kernel,
        grid=(FF // CHUNK,),
        in_specs=[SM, VM, pl.BlockSpec((R, CHUNK), lambda f: (0, f)), pl.BlockSpec((CHUNK, D), lambda f: (f, 0))],
        out_specs=VM,
        out_shape=shape((1, ROWS, D)),
        scratch_shapes=[pltpu.VMEM((R, D), F32)],
        compiler_params=room(16),
        name="layer_out",
    )(place, middle, active, far(w_down)),))[0]
    arrived(*d_o)
    distant = shift(after(turned, *d_o, place), "z", 2)

    def chunk(i, s):
        return (0, 2 * lax.rem(s[1] + i, 4) + s[3])

    def at_chunk(axis):
        return lambda i, s: tuple(lax.rem(s[1] + i, 4) if n == axis else 0 for n in range(5))

    sent = ordered(pl.pallas_call(
        ff_grad_kernel,
        grid_spec=pltpu.PrefetchScalarGridSpec(
            num_scalar_prefetch=1,
            grid=(4,),
            in_specs=[
                pl.BlockSpec((R, 384), chunk),
                pl.BlockSpec((R, 384), chunk),
                VM,
                VM,
                VM,
                pl.BlockSpec((R, 384), lambda i, s: (0, s[3])),
                pl.BlockSpec((4, 1, 4, 48, 384), at_chunk(1)),
                pl.BlockSpec((4, 4, 1, 64, 384), at_chunk(2)),
            ],
            out_specs=[VM] * 8,
            scratch_shapes=[
                pltpu.VMEM((R, D), BF),
                pltpu.VMEM((D, R), BF),
                pltpu.VMEM((R, D), F32),
                pltpu.VMEM((4, 4, 64, 384), BF),
                pltpu.VMEM((D, 384), F32),
            ],
        ),
        out_shape=[shape((4, 4, 48, 384))] * 4 + [shape((4, 4, 64, 384))] * 4,
        compiler_params=room(32),
        name="ff_grad",
    )(place, active, d_up, second, far(cotangent), o_turned, d_branch, *(far(t) for t in got)))
    a_sent, b_sent = sent[0:4], sent[4:8]
    a_parts = [a_sent[0], shift(a_sent[1], "x", 1), None, shift(a_sent[3], "x", 3)]
    b_parts = [b_sent[0], shift(b_sent[1], "y", 1), None, shift(b_sent[3], "y", 3)]

    def attend_back(g):
        last = g == 2
        scratch = [
            pltpu.VMEM((4, 128, R), BF),
            pltpu.VMEM((4, 128, R), BF),
            pltpu.VMEM((4, HD, R), BF),
            pltpu.VMEM((4, R, 128), BF),
            pltpu.VMEM((4, R, 128), BF),
            pltpu.VMEM((4, R, HD), BF),
            pltpu.VMEM((4, HD, R), BF),
            pltpu.VMEM((4, R, HD), BF),
            pltpu.VMEM((4, 1, R), F32),
            pltpu.VMEM((4, HD, R), F32),
        ]
        if last:
            scratch = [pltpu.VMEM((4, 640, R), BF), pltpu.VMEM((D, 640), F32)] + scratch
            extra = (far(turned), far(near[0]), far(distant), far(near[1]), far(made[0]), far(made[1]))
        else:
            extra = ()
        return ordered(pl.pallas_call(
            lambda *refs, g=g: attend_back_kernel(g, *refs),
            grid=(1,),
            in_specs=[SM] + [VM] * 4 + [pl.BlockSpec((HD, R), lambda _, g=g: (g, 0))] * 4 + [VM] * (2 + len(extra)),
            out_specs=[VM] * (6 if last else 5),
            out_shape=[piece] * 4 + ([shape((4, 4, 32, 640))] * 2 if last else [shape((4, 192, R))]),
            scratch_shapes=scratch,
            compiler_params=room(32 if last else 24),
            name="attend_back",
        )(place, *(far(h) for h in heads[g]), *(far(t) for t in d_o), far(attended[g]), far(spreads[g]), *extra))

    pieces, made = [], []
    *sent, one = attend_back(0)
    made.append(one)
    pieces.append(spread_pieces(sent, "z"))
    a_parts[2] = shift(after(a_sent[2], place), "x", 2)
    b_parts[2] = shift(after(b_sent[2], place), "y", 2)
    arrived(a_parts[1], a_parts[3], b_parts[1], b_parts[3], distant)
    *sent, one = attend_back(1)
    made.append(one)
    pieces.append(spread_pieces(sent, "z"))
    arrived(*pieces[0])
    *sent, keep, send = attend_back(2)
    *sent, send = lax.optimization_barrier((*sent, send, *pieces[1], a_parts[2], b_parts[2]))[:5]
    pieces.append(spread_pieces(sent, "z"))
    got = shift(send, "core", 1)
    arrived(*pieces[1], a_parts[2], b_parts[2])

    so_far = ordered(run(
        input_grad_kernel,
        "input_grad",
        24,
        [shape((D, R), F32)],
        (place, *(far(p) for p in pieces[0] + pieces[1]), far(w_qkv)),
        [pltpu.VMEM((36, HD, R), BF)],
    ))[0]
    sent = ordered(run(
        cut_kernel,
        "sum_first",
        24,
        [shape((4 * PART_A + 4 * GROUP, 128))] * 4 + [shape((4, 64, 384))] * 4,
        (place, *(far(t) for t in a_parts + b_parts), far(keep), far(got)),
    ))
    y_parts, x_parts = spread_pieces(sent[0:4], "y"), spread_pieces(sent[4:8], "x")
    grad_stream, small = ordered(pl.pallas_call(
        last_kernel,
        grid=(1,),
        in_specs=[SM, SM] + [VM] * 9 + [weight_spec(c) for c in (2, 5, 8)],
        out_specs=[VM, VM],
        out_shape=[shape((1, ROWS, D), F32), shape((8, D), F32)],
        scratch_shapes=[pltpu.VMEM((3, 4, HD, R), BF)],
        compiler_params=room(24),
        name="ln_back",
    )(place, passes, *(far(p) for p in pieces[2]), so_far, far(hidden), far(d_middle), gain_term, gains, *([far(w_qkv)] * 3)))
    sent = ordered(run(
        block_kernel,
        "sum_second",
        16,
        [shape((PART_A + PART_B + GROUP + TINY, 128))] * 4,
        (place, *(far(t) for t in y_parts + x_parts), small),
    ))
    buffers = ordered(run(
        own_kernel,
        "sum_blocks",
        16,
        [shape((4 * GROUP + TINY + PART_A, 128)), shape((PART_B, 128))],
        (place, *(far(t) for t in spread_pieces(sent, "z"))),
    ))
    buffers = ordered(run(
        row_kernel,
        "stack_rows",
        16,
        [shape((4 * GROUP + TINY + 4 * PART_A, 128)), shape((4 * PART_B, 128))],
        (place, *(far(t) for t in all_of(buffers[0], "x") + all_of(buffers[1], "y"))),
    ))
    buffer = ordered(run(
        stack_kernel,
        "stack",
        16,
        [shape((ALL, 128))],
        (place, *(far(t) for t in all_of(buffers[0], "y") + all_of(buffers[1], "x"))),
    ))[0]
    results = run(
        finish_kernel,
        "finish",
        32,
        [
            shape((192, 3 * D), F32),
            shape((192, D), F32),
            shape((192, FF), F32),
            shape((D, D), F32),
            shape((192, 2), F32),
            shape((192, PASSES), F32),
        ],
        (place, far(buffer), far(shift(buffer, "core", 1))),
        [pltpu.VMEM((2, ALL, 128), BF), pltpu.VMEM((D, 8), F32)],
    )
    return (layer_out, grad_stream, *results)


def solution(mesh):
    tokens = P("batch", "blk", None)
    in_specs = (tokens, tokens, P("batch"), P(), P(), P(), P(), P(), P())
    out_specs = (tokens, tokens) + (P("blk", None),) * 6
    return jax.shard_map(on_device, mesh=mesh, in_specs=in_specs, out_specs=out_specs, check_vma=False)
```

```python
import jax
import jax.numpy as jnp
from jax import lax
from jax.experimental import pallas as pl
from jax.experimental.pallas import tpu as pltpu
from jax.sharding import PartitionSpec as P

D = 768
HEADS = 12
HD = 64
FF = 3072
PASSES = 5
ROWS = 510
R = 512
EPS = 1e-05
NEG = -1e30
BF = jnp.bfloat16
F32 = jnp.float32
VM = pl.BlockSpec(memory_space=pltpu.VMEM)
SM = pl.BlockSpec(memory_space=pltpu.SMEM)
HB = pl.BlockSpec(memory_space=pl.ANY)
MIB = 1024 * 1024


def room(mib):
    return pltpu.CompilerParams(vmem_limit_bytes=mib * MIB)


def run(kernel, name, mib, outs, operands, scratch=(), scalars=1):
    return pl.pallas_call(
        kernel,
        in_specs=[SM] * scalars + [VM] * (len(operands) - scalars),
        out_specs=[VM] * len(outs),
        out_shape=outs,
        scratch_shapes=list(scratch),
        compiler_params=room(mib),
        name=name,
    )(*operands)


def shape(dims, kind=BF):
    return jax.ShapeDtypeStruct(dims, kind)


def kept(dims, kind=BF):
    return pltpu.HBM(dims, kind)


def dot(left, right):
    return jnp.dot(left, right, preferred_element_type=F32)


def dot_nt(left, right):
    return lax.dot_general(left, right, (((1,), (1,)), ((), ())), preferred_element_type=F32)


def normalize(values):
    mean = jnp.mean(values, axis=-1, keepdims=True)
    centred = values - mean
    inverse = lax.rsqrt(jnp.mean(centred * centred, axis=-1, keepdims=True) + EPS)
    return centred * inverse, inverse


def norm_back(grad, unit, inverse, gain):
    scaled = grad * gain
    first = jnp.mean(scaled, axis=-1, keepdims=True)
    second = jnp.mean(scaled * unit, axis=-1, keepdims=True)
    return inverse * (scaled - first - unit * second)


def pass_index(blk, count):
    row = lax.broadcasted_iota(jnp.int32, (R, 1), 0) + blk * ROWS
    turns = jnp.floor((row.astype(F32) + 0.5) / count.astype(F32)).astype(jnp.int32)
    return row - turns * count


def pieces_out(stage, outs, blk):
    for d, out in enumerate(outs):
        out[...] = stage[lax.rem(blk + d, 4)]


def project(normed, weights, stage, outs, blk):
    for part, weight in enumerate(weights):
        got = dot(normed, weight[...])
        if part == 0:
            got = got.astype(BF) * jnp.asarray(HD ** (-0.5), BF)
        turned = got.astype(BF).T
        for j in range(4):
            stage[j, 64 * part : 64 * part + 64, :] = turned[64 * j : 64 * j + 64]
    pieces_out(stage, outs, blk)


def project(normed, weights, stage):
    for part, weight in enumerate(weights):
        got = dot(normed, weight[...])
        if part == 0:
            got = got.astype(BF) * jnp.asarray(HD ** (-0.5), BF)
        flipped = got.astype(BF).T
        for j in range(4):
            stage[j, 64 * part : 64 * part + 64, :] = flipped[64 * j : 64 * j + 64]


def first_kernel(blk_ref, count_ref, stream, embed, gains, wq, wk, wv, hidden, turned, p0, p1, p2, p3, normed, stage):
    blk = blk_ref[0]
    hidden[R - 8 : R, :] = jnp.zeros((8, D), F32)
    hidden[0:ROWS, :] = stream[0].astype(F32)
    which = pass_index(blk, count_ref[0])
    added = embed[0:1, :]
    for r in range(1, PASSES):
        added = jnp.where(which == r, embed[r : r + 1, :], added)
    values = hidden[...] + added
    hidden[...] = values
    unit, _ = normalize(values)
    row = lax.broadcasted_iota(jnp.int32, (R, 1), 0)
    low = jnp.where(row < ROWS, unit * gains[0:1, :], 0.0).astype(BF)
    normed[...] = low
    project(low, (wq, wk, wv), stage)
    for d, out in enumerate((p0, p1, p2, p3)):
        out[...] = stage[lax.rem(blk + d, 4)]
    turned[...] = low.T


def second_kernel(blk_ref, normed, wq1, wk1, wv1, wq2, wk2, wv2, p0, p1, p2, p3, stage):
    blk = blk_ref[0]
    for n, weights in enumerate(((wq1, wk1, wv1), (wq2, wk2, wv2))):
        project(normed[...], weights, stage.at[n])
        for d, out in enumerate((p0, p1, p2, p3)):
            out[192 * n : 192 * n + 192, :] = stage[n, lax.rem(blk + d, 4)]


def load_heads(blk, at, parts, q_rows, k_rows, v_rows, k_cols):
    for d in range(4):
        s = lax.rem(blk + 4 - d, 4)
        piece = parts[d]
        q_rows[s, 0:64, :] = piece[at : at + 64, :]
        k_rows[s, 0:64, :] = piece[at + 64 : at + 128, :]
        v_rows[s] = piece[at + 128 : at + 192, :]
    row = lax.broadcasted_iota(jnp.int32, (64, R), 0)
    col = lax.broadcasted_iota(jnp.int32, (64, R), 1)
    one = jnp.where(row == 0, 1.0, 0.0).astype(BF)
    off = jnp.where((row == 0) & (col >= ROWS), NEG, 0.0).astype(BF)
    for s in range(4):
        q_rows[s, 64:128, :] = one
        k_rows[s, 64:128, :] = off
    for s in range(4):
        k_cols[s] = k_rows[s].T


def causal():
    key = lax.broadcasted_iota(jnp.int32, (R, R), 0)
    query = lax.broadcasted_iota(jnp.int32, (R, R), 1)
    return key <= query


def attend_head(blk, n, parts, attended, spread, q_rows, k_rows, v_rows, k_cols, scores, stage):
    load_heads(blk, 192 * n, parts, q_rows, k_rows, v_rows, k_cols)
    for i in range(4):
        top = None
        for j in range(i + 1):
            got = dot(k_cols[j], q_rows[i])
            if i == j:
                got = jnp.where(causal(), got, NEG)
            scores[j] = got
            best = jnp.max(got, axis=0, keepdims=True)
            top = best if top is None else jnp.maximum(top, best)
        total = jnp.zeros((1, R), F32)
        summed = jnp.zeros((HD, R), F32)
        for j in range(i + 1):
            raised = jnp.exp(scores[j] - top)
            total = total + jnp.sum(raised, axis=0, keepdims=True)
            summed = summed + dot(v_rows[j], raised.astype(BF))
        result = summed / total
        attended[n, i] = result
        spread[n, i] = top + jnp.log(total)
        stage[i] = result.astype(BF)


def attend_kernel(count, blk_ref, r0, r1, r2, r3, *rest):
    earlier, rest = (rest[:4], rest[4:]) if count == 2 else ((), rest)
    p0, p1, p2, p3, attended, spread, *scratch = rest
    blk = blk_ref[0]
    for n in range(count):
        stage = scratch[-1].at[n]
        attend_head(blk, n, (r0, r1, r2, r3), attended, spread, *(ref.at[n] for ref in scratch))
        for d, out in enumerate((p0, p1, p2, p3)):
            at = 64 * (n + 1) if count == 2 else 0
            out[at : at + 64, :] = stage[lax.rem(blk + d, 4)]
    for d, value in enumerate(earlier):
        (p0, p1, p2, p3)[d][0:64, :] = value[...]


def attend_back_kernel(g, blk_ref, r0, r1, r2, r3, g0, g1, g2, g3, attended, spread, *rest):
    last = g == 2
    n = max(g - 1, 0)
    if g == 1:
        f0, f1, f2, f3, *rest = rest
    if last:
        t0, t1, t2, t3, e0, e1, p0, p1, p2, p3, keep, send, *rest = rest
        outs, made, *rest = rest
    else:
        p0, p1, p2, p3, outs, *rest = rest
    q_rows, k_rows, v_rows, k_cols, q_cols, v_cols, o_rows, o_cols, delta, dq = rest
    blk = blk_ref[0]
    load_heads(blk, 192 * n, (r0, r1, r2, r3), q_rows, k_rows, v_rows, k_cols)
    for d, piece in enumerate((g0, g1, g2, g3)):
        o_rows[lax.rem(blk + 4 - d, 4)] = piece[...]
    for s in range(4):
        q_cols[s] = q_rows[s].T
        v_cols[s] = v_rows[s].T
        o_cols[s] = o_rows[s].T
        delta[s] = jnp.sum(o_rows[s].astype(F32) * attended[n, s], axis=0, keepdims=True)
        dq[s] = jnp.zeros((HD, R), F32)
    at = 384 if last else 0
    for j in range(4):
        dk = jnp.zeros((R, 2 * HD), F32)
        dv = jnp.zeros((R, HD), F32)
        for i in range(j, 4):
            got = dot(k_cols[j], q_rows[i])
            if i == j:
                got = jnp.where(causal(), got, NEG)
            probs = jnp.exp(got - spread[n, i])
            d_probs = dot(v_cols[j], o_rows[i])
            d_scores = (probs * (d_probs - delta[i])).astype(BF)
            dv = dv + dot(probs.astype(BF), o_cols[i])
            dk = dk + dot(d_scores, q_cols[i])
            dq[i] = dq[i] + dot(k_rows[j, 0:64, :], d_scores)
        outs[j, at : at + 64, :] = (dq[j] * HD ** (-0.5)).astype(BF)
        outs[j, at + 64 : at + 128, :] = dk[:, 0:64].astype(BF).T
        outs[j, at + 128 : at + 192, :] = dv.astype(BF).T
    for d, out in enumerate((p0, p1, p2, p3)):
        piece = outs[lax.rem(blk + d, 4), at : at + 192, :]
        if g == 1:
            out[0:192, :] = (f0, f1, f2, f3)[d][...]
            out[192:384, :] = piece
        else:
            out[...] = piece
    if last:
        for s in range(4):
            outs[s, 0:192, :] = e0[s]
            outs[s, 192:384, :] = e1[s]
            outs[s, 576:640, :] = jnp.zeros((64, R), BF)
        total = jnp.zeros((D, 640), F32)
        for d, piece in enumerate((t0, t1, t2, t3)):
            total = total + dot_nt(piece[...], outs[lax.rem(blk + 4 - d, 4)])
        made[...] = total
        core = blk_ref[3]
        for i in range(4):
            for xx in range(4):
                for out, c in ((keep, core), (send, 1 - core)):
                    row = pl.multiple_of(192 * i + 24 * xx + 96 * c, 8)
                    part = jnp.concatenate([made[pl.ds(row, 24), :], jnp.zeros((8, 640), F32)], axis=0)
                    out[xx, i] = part.astype(BF)


def gelu_both(value):
    c = (2.0 / jnp.pi) ** 0.5
    square = value * value
    t = jnp.tanh(c * value * (1.0 + 0.044715 * square))
    cdf = 0.5 * (1.0 + t)
    slope = cdf + (0.5 * c) * value * (1.0 - t * t) * (1.0 + 3.0 * 0.044715 * square)
    return value * cdf, slope


CHUNK = 768


def up_cut(values, store):
    for z in range(4):
        for yy in range(4):
            store(yy, z, values[192 * z + 48 * yy : 192 * z + 48 * yy + 48, :])


def down_cut(values, store):
    for yy in range(4):
        for xx in range(4):
            r, col = 48 * (2 * yy + xx // 2), 384 * (xx % 2)
            store(yy, xx, values[r : r + 48, col : col + 384])


def out_cut(values, out):
    for i in range(4):
        for n in range(16):
            rows = values[192 * i + 16 * n : 192 * i + 16 * n + 16, :] if n < 12 else jnp.zeros((16, 384), BF)
            out[n // 4, n % 4, i, 48:64] = rows


def put_block(out, at, rows):
    out[at] = rows.astype(BF)


def ff_kernel(
    blk_ref, r0, r1, r2, r3, hidden, cot, gains, w_out, w_up, w_down,
    active, d_up, second, middle, o_turned, d_branch, d_middle, p0, p1, p2, p3, a_out, b_out, gain_term,
    dy, back, stage, second_turned,
):
    step = pl.program_id(0)
    core = blk_ref[3]

    @pl.when(step == 0)
    def _():
        blk = blk_ref[0]
        for d, piece in enumerate((r0, r1, r2, r3)):
            s = lax.rem(blk + 4 - d, 4)
            for g in range(3):
                stage[4 * g + s] = piece[64 * g : 64 * g + 64, :]
        o_rows = stage[...].reshape(D, R)
        o_turned[...] = o_rows
        values = hidden[...] + dot(o_rows.T, w_out[...])
        middle[...] = values
        unit, _ = normalize(values)
        second[...] = (unit * gains[1:2, :]).astype(BF)
        back[R - 8 : R, :] = jnp.zeros((8, D), F32)
        back[0:ROWS, :] = cot[0].astype(F32)
        dy[...] = back[...].astype(BF)
        back[...] = jnp.zeros((R, D), F32)
        second_turned[...] = second[...].T

    upward = dot(second[...], w_up[...])
    act, slope = gelu_both(upward)
    act = act.astype(BF)
    active[...] = act
    d_active = dot_nt(dy[...], w_down[...])
    d_upward = (d_active * slope).astype(BF)
    d_up[...] = d_upward
    back[...] += dot_nt(d_upward, w_up[...])

    first = core == 0
    other_up = jnp.where(first, d_upward[:, 384:768], d_upward[:, 0:384])
    other_act = jnp.where(first, act[:, 384:768], act[:, 0:384])
    up_cut(dot(second_turned[...], other_up), lambda yy, z, rows: put_block(a_out, (yy, step, z), rows))
    down_cut(dot(other_act.T, dy[...]), lambda yy, xx, rows: put_block(b_out, (yy, xx, step, slice(0, 48)), rows))

    @pl.when(step == FF // CHUNK - 1)
    def _():
        blk = blk_ref[0]
        unit, inverse = normalize(middle[...])
        grad = back[...]
        gain_term[...] = jnp.sum(grad * unit, axis=0, keepdims=True)
        total = dy[...].astype(F32) + norm_back(grad, unit, inverse, gains[1:2, :])
        d_middle[...] = total
        low = total.astype(BF)
        d_branch[...] = low
        stage[...] = dot_nt(w_out[...], low).astype(BF).reshape(HEADS, HD, R)
        out_cut(dot(o_turned[...], jnp.where(core == 0, low[:, 384:768], low[:, 0:384])).astype(BF), b_out)
        for d, out in enumerate((p0, p1, p2, p3)):
            j = lax.rem(blk + d, 4)
            for g in range(3):
                out[64 * g : 64 * g + 64, :] = stage[4 * g + j]


def ff_grad_kernel(place_ref, active, d_up, second, cot, o_turned, d_branch, a_out, b_out, dy, second_turned, pad):
    step = pl.program_id(0)

    @pl.when(step == 0)
    def _():
        pad[R - 8 : R, :] = jnp.zeros((8, D), F32)
        pad[0:ROWS, :] = cot[0].astype(F32)
        dy[...] = pad[...].astype(BF)
        second_turned[...] = second[...].T
        out_cut(dot(o_turned[...], d_branch[...]).astype(BF), b_out)

    up_cut(dot(second_turned[...], d_up[...]), lambda yy, z, rows: put_block(a_out, (yy, step, z), rows))
    down_cut(dot(active[...].T, dy[...]), lambda yy, xx, rows: put_block(b_out, (yy, xx, step, slice(0, 48)), rows))


def core_sum_kernel(place_ref, a_mine, b_mine, a_got, b_got, a0, a1, a2, a3, b0, b1, b2, b3):
    x, y = place_ref[1], place_ref[2]
    for d, (a_out, b_out) in enumerate(((a0, b0), (a1, b1), (a2, b2), (a3, b3))):
        xx, yy = lax.rem(x + d, 4), lax.rem(y + d, 4)
        for n in range(4):
            a_out[n] = (a_mine[n, xx].astype(F32) + a_got[n, xx].astype(F32)).astype(BF)
            b_out[n] = (b_mine[yy, n].astype(F32) + b_got[yy, n].astype(F32)).astype(BF)


def total_of(parts):
    return (parts[0].astype(F32) + parts[2].astype(F32)) + (parts[1].astype(F32) + parts[3].astype(F32))


TINY = 96
GROUP = 160
PART_A = 144
PART_B = 192


def put(buffer, at, block):
    rows, lanes = block.shape
    for t in range(lanes // 128):
        buffer[at + rows * t : at + rows * t + rows, :] = block[:, 128 * t : 128 * t + 128]


def put_small(buffer, at, value):
    high = value.astype(BF)
    low = (value - high.astype(F32)).astype(BF)
    put(buffer, at, jnp.concatenate([high, low], axis=0))


def get_small(buffer, at):
    parts = []
    for t in range(6):
        part = buffer[at + 16 * t : at + 16 * t + 16, :].astype(F32)
        parts.append(part[0:8] + part[8:16])
    return jnp.concatenate(parts, axis=1)


def take(buffer, at, rows):
    return jnp.concatenate([buffer[at + rows * t : at + rows * t + rows, :] for t in range(3)], axis=1)


def cut_kernel(place_ref, a0, a1, a2, a3, b0, b1, b2, b3, keep, got, y0, y1, y2, y3, x0, x1, x2, x3):
    x, y = place_ref[1], place_ref[2]
    for d, (y_out, x_out) in enumerate(((y0, x0), (y1, x1), (y2, x2), (y3, x3))):
        yy, xx = lax.rem(y + d, 4), lax.rem(x + d, 4)
        a_sum = total_of([r[yy] for r in (a0, a1, a2, a3)]).astype(BF)
        heads = (keep[yy].astype(F32) + got[yy].astype(F32)).astype(BF)
        for i in range(4):
            put(y_out, PART_A * i, a_sum[i])
            put(y_out, 4 * PART_A + GROUP * i, heads[i])
        x_out[...] = total_of([r[xx] for r in (b0, b1, b2, b3)]).astype(BF)


def block_kernel(place_ref, y0, y1, y2, y3, x0, x1, x2, x3, small, o0, o1, o2, o3):
    z = place_ref[0]
    for d, out in enumerate((o0, o1, o2, o3)):
        i = lax.rem(z + d, 4)
        start = pl.multiple_of(PART_A * i, 16)
        out[0:PART_A, :] = total_of([r[pl.ds(start, PART_A), :] for r in (y0, y1, y2, y3)]).astype(BF)
        put(out, PART_A, total_of([r[i] for r in (x0, x1, x2, x3)]).astype(BF))
        start = pl.multiple_of(4 * PART_A + GROUP * i, 16)
        at = PART_A + PART_B
        out[at : at + GROUP, :] = total_of([r[pl.ds(start, GROUP), :] for r in (y0, y1, y2, y3)]).astype(BF)
        put_small(out, at + GROUP, small[...])


def own_kernel(place_ref, z0, z1, z2, z3, x_out, y_out):
    parts = (z0, z1, z2, z3)
    at = PART_A + PART_B
    for d, r in enumerate(parts):
        x_out[GROUP * d : GROUP * d + GROUP, :] = r[at : at + GROUP, :]
    put_small(x_out, 4 * GROUP, total_of([get_small(r, at + GROUP) for r in parts]))
    x_out[4 * GROUP + TINY : 4 * GROUP + TINY + PART_A, :] = total_of([r[0:PART_A, :] for r in parts]).astype(BF)
    y_out[...] = total_of([r[PART_A : PART_A + PART_B, :] for r in parts]).astype(BF)


def row_kernel(place_ref, x0, x1, x2, x3, y0, y1, y2, y3, y_out, x_out):
    parts = (x0, x1, x2, x3)
    y_out[0 : 4 * GROUP, :] = total_of([r[0 : 4 * GROUP, :] for r in parts]).astype(BF)
    put_small(y_out, 4 * GROUP, total_of([get_small(r, 4 * GROUP) for r in parts]))
    at = 4 * GROUP + TINY
    for d, (a, b) in enumerate(zip(parts, (y0, y1, y2, y3))):
        y_out[at + PART_A * d : at + PART_A * d + PART_A, :] = a[at : at + PART_A, :]
        x_out[PART_B * d : PART_B * d + PART_B, :] = b[...]


ALL_TINY = 16 * GROUP
ALL_A = ALL_TINY + TINY
ALL_B = ALL_A + 16 * PART_A
ALL = ALL_B + 16 * PART_B


def stack_kernel(place_ref, y0, y1, y2, y3, x0, x1, x2, x3, out):
    parts = (y0, y1, y2, y3)
    put_small(out, ALL_TINY, total_of([get_small(r, 4 * GROUP) for r in parts]))
    at = 4 * GROUP + TINY
    for d, (r, b) in enumerate(zip(parts, (x0, x1, x2, x3))):
        out[4 * GROUP * d : 4 * GROUP * d + 4 * GROUP, :] = r[0 : 4 * GROUP, :]
        out[ALL_A + 4 * PART_A * d : ALL_A + 4 * PART_A * d + 4 * PART_A, :] = r[at : at + 4 * PART_A, :]
        out[ALL_B + 4 * PART_B * d : ALL_B + 4 * PART_B * d + 4 * PART_B, :] = b[...]


def finish_kernel(place_ref, mine, other, grad_qkv, grad_out, grad_up, grad_down, gains, passes, pair, turned):
    z, x, y, core = place_ref[0], place_ref[1], place_ref[2], place_ref[3]
    pair[core] = mine[...]
    pair[1 - core] = other[...]

    def rows(c, at, count):
        return pair[c, pl.ds(pl.multiple_of(at, 16), count), :].astype(F32)

    for c in range(2):
        for xx in range(4):
            dx = lax.rem(x + 4 - xx, 4)
            for yy in range(4):
                dy = lax.rem(y + 4 - yy, 4)
                a = rows(c, ALL_A + 4 * PART_A * dy + PART_A * dx, PART_A)
                b = rows(c, ALL_B + 4 * PART_B * dx + PART_B * dy, PART_B)
                r = 384 * c + 48 * (2 * yy + xx // 2)
                for t in range(3):
                    col = 384 * (2 * xx + c) + 128 * t
                    grad_up[48 * yy : 48 * yy + 48, col : col + 128] = a[48 * t : 48 * t + 48]
                    col = 384 * (xx % 2) + 128 * t
                    grad_down[r : r + 48, col : col + 128] = b[64 * t : 64 * t + 48]
                    if yy < 3:
                        n, col = 16 * (4 * yy + xx), 384 * c + 128 * t
                        grad_out[n : n + 16, col : col + 128] = b[64 * t + 48 : 64 * t + 64]
        for yy in range(4):
            dy = lax.rem(y + 4 - yy, 4)
            for j in range(4):
                dz = lax.rem(z + 4 - j, 4)
                piece = rows(c, 4 * GROUP * dy + GROUP * dz, GROUP)
                r = 96 * c + 24 * yy
                for n in range(9):
                    lane = 64 * n
                    block = piece[32 * (lane // 128) : 32 * (lane // 128) + 24, lane % 128 : lane % 128 + 64]
                    col = D * (n % 3) + 64 * (4 * (n // 3) + j)
                    grad_qkv[r : r + 24, col : col + 64] = block
    small = get_small(mine, ALL_TINY) + get_small(other, ALL_TINY)
    turned[...] = small.T
    part = turned[pl.ds(pl.multiple_of(192 * z, 8), 192), :]
    part = part.T
    gains[...] = part[0:2, :]
    passes[...] = part[2:7, :]


def layer_out_kernel(place_ref, middle, active, w_down, out, total):
    step = pl.program_id(0)

    @pl.when(step == 0)
    def _():
        total[...] = middle[...]

    total[...] += dot(active[...], w_down[...])

    @pl.when(step == FF // CHUNK - 1)
    def _():
        out[0] = total[0:ROWS, :].astype(BF)


def input_grad_kernel(blk_ref, a0, a1, a2, a3, w_qkv, out, stage):
    blk = blk_ref[0]
    stage[...] = jnp.zeros((36, HD, R), BF)
    for d, piece in enumerate((a0, a1, a2, a3)):
        s = lax.rem(blk + 4 - d, 4)
        for n in range(6):
            stage[12 * (n % 3) + 4 * (n // 3) + s] = piece[64 * n : 64 * n + 64, :]
    out[...] = dot(w_qkv[...], stage[...].reshape(3 * D, R))


def last_kernel(
    blk_ref, count_ref, c0, c1, c2, c3, so_far, hidden, d_middle, gain_term, gains, wq, wk, wv, grad_stream, small, stage
):
    blk = blk_ref[0]
    for d, piece in enumerate((c0, c1, c2, c3)):
        s = lax.rem(blk + 4 - d, 4)
        for part in range(3):
            stage[part, s] = piece[64 * part : 64 * part + 64, :]
    turned = so_far[...]
    for part, weight in enumerate((wq, wk, wv)):
        turned = turned + dot(weight[...], stage[part].reshape(256, R))
    grad = turned.T
    unit, inverse = normalize(hidden[...])
    total = d_middle[...] + norm_back(grad, unit, inverse, gains[0:1, :])
    grad_stream[0] = total[0:ROWS, :]
    row = lax.broadcasted_iota(jnp.int32, (R, 1), 0)
    which = jnp.where(row < ROWS, pass_index(blk, count_ref[0]), -1)
    small[0:1, :] = jnp.sum(grad * unit, axis=0, keepdims=True)
    small[1:2, :] = gain_term[...]
    for r in range(PASSES):
        small[2 + r : 3 + r, :] = jnp.sum(jnp.where(which == r, total, 0.0), axis=0, keepdims=True)
    small[7:8, :] = jnp.zeros((1, D), F32)


def shift(values, axis, d):
    if axis == "z":
        return lax.ppermute(values, "blk", [(i, (i + d) % 4) for i in range(4)])
    pairs = []
    for b in range(32):
        y, x, core = b // 8, (b // 2) % 4, b % 2
        if axis == "y":
            y = (y + d) % 4
        elif axis == "x":
            x = (x + d) % 4
        else:
            core = (core + d) % 2
        pairs.append((b, 8 * y + 2 * x + core))
    return lax.ppermute(values, "batch", pairs)


def spread_pieces(pieces, axis):
    return (pieces[0],) + tuple(shift(pieces[d], axis, d) for d in (1, 2, 3))


def all_of(value, axis):
    return spread_pieces((value,) * 4, axis)


def after(value, *others):
    return lax.optimization_barrier((value,) + others)[0]


def far(value):
    return pltpu.with_memory_space_constraint(value, pltpu.HBM)


def weight_spec(column):
    return pl.BlockSpec((D, 256), lambda *_, column=column: (0, column))


def on_device(stream, cotangent, passes, w_qkv, w_out, w_up, w_down, ln_gains, pass_embed):
    z = lax.axis_index("blk").astype(jnp.int32)
    batch = lax.axis_index("batch").astype(jnp.int32)
    place = jnp.stack([z, batch // 2 % 4, batch // 8, batch % 2])
    gains = ln_gains.T
    embed = pass_embed.T
    piece = shape((192, R))
    full = shape((R, D))

    def arrived(*values):
        nonlocal place
        place = lax.optimization_barrier((place,) + values)[0]

    def ordered(outs):
        nonlocal place
        *outs, first = outs
        place, first = lax.optimization_barrier((place, first))
        return (*outs, first)

    hidden, turned, *sent, normed = ordered(pl.pallas_call(
        first_kernel,
        grid=(1,),
        in_specs=[SM, SM, VM, VM, VM, weight_spec(0), weight_spec(3), weight_spec(6)],
        out_specs=[VM] * 7,
        out_shape=[kept((R, D), F32), kept((D, R)), kept((192, R)), piece, piece, piece, full],
        scratch_shapes=[pltpu.VMEM((4, 192, R), BF)],
        compiler_params=room(24),
        name="ln_qkv",
    )(place, passes, far(stream), embed, gains, *([far(w_qkv)] * 3)))
    early = spread_pieces(sent, "z")
    sent = ordered(pl.pallas_call(
        second_kernel,
        grid=(1,),
        in_specs=[SM, VM] + [weight_spec(c) for c in (1, 4, 7, 2, 5, 8)],
        out_specs=[VM] * 4,
        out_shape=[kept((384, R))] + [shape((384, R))] * 3,
        scratch_shapes=[pltpu.VMEM((2, 4, 192, R), BF)],
        compiler_params=room(24),
        name="qkv_rest",
    )(place, normed, *([far(w_qkv)] * 6)))
    late = [sent[0], shift(sent[1], "z", 1), sent[2], shift(sent[3], "z", 3)]

    attended, spreads, sent = [], [], []
    for count, parts in ((1, early), (2, late)):
        *sent, result, spread = ordered(run(
            lambda *refs, count=count: attend_kernel(count, *refs),
            "attend",
            24,
            [shape((192 if count == 2 else HD, R))] * 4 + [kept((count, 4, HD, R), F32), kept((count, 4, 1, R), F32)],
            (place, *(far(h) for h in parts), *sent),
            [
                pltpu.VMEM((count, 4, 128, R), BF),
                pltpu.VMEM((count, 4, 128, R), BF),
                pltpu.VMEM((count, 4, HD, R), BF),
                pltpu.VMEM((count, 4, R, 128), BF),
                pltpu.VMEM((count, 4, R, R), F32),
                pltpu.VMEM((count, 4, HD, R), BF),
            ],
        ))
        if count == 1:
            late[2] = shift(after(late[2], place), "z", 2)
        attended += [result] * count
        spreads += [spread] * count
    heads = (early, late, late)
    back_o = spread_pieces(sent, "z")
    near = after(turned, *back_o)
    near = (shift(near, "z", 1), shift(near, "z", 3))

    active, d_up, second, middle, o_turned, d_branch, d_middle, *sent, a_other, b_other, gain_term = ordered(pl.pallas_call(
        ff_kernel,
        grid=(FF // CHUNK,),
        in_specs=[SM] + [VM] * 4 + [VM, VM, VM, VM]
        + [pl.BlockSpec((D, CHUNK), lambda f: (0, f)), pl.BlockSpec((CHUNK, D), lambda f: (f, 0))],
        out_specs=[pl.BlockSpec((R, CHUNK), lambda f: (0, f)), pl.BlockSpec((R, CHUNK), lambda f: (0, f))] + [VM] * 12,
        out_shape=[shape((R, FF)), shape((R, FF)), full, shape((R, D), F32), shape((D, R)), full, kept((R, D), F32)]
        + [kept((192, R))] + [piece] * 3 + [shape((4, 4, 4, 48, 384)), shape((4, 4, 4, 64, 384)), shape((1, D), F32)],
        scratch_shapes=[pltpu.VMEM((R, D), BF), pltpu.VMEM((R, D), F32), pltpu.VMEM((HEADS, HD, R), BF), pltpu.VMEM((D, R), BF)],
        compiler_params=room(36),
        name="ff",
    )(place, *(far(o) for o in back_o), far(hidden), far(cotangent), gains, far(w_out), far(w_up), far(w_down)))
    *sent, a_other, b_other = lax.optimization_barrier((*sent, a_other, b_other, *near))[:6]
    d_o = spread_pieces(sent, "z")

    got = (shift(a_other, "core", 1), shift(b_other, "core", 1))
    own = ordered(pl.pallas_call(
        ff_grad_kernel,
        grid_spec=pltpu.PrefetchScalarGridSpec(
            num_scalar_prefetch=1,
            grid=(4,),
            in_specs=[
                pl.BlockSpec((R, 384), lambda i, s: (0, 2 * i + s[3])),
                pl.BlockSpec((R, 384), lambda i, s: (0, 2 * i + s[3])),
                VM,
                VM,
                VM,
                pl.BlockSpec((R, 384), lambda i, s: (0, s[3])),
            ],
            out_specs=[VM] * 2,
            scratch_shapes=[pltpu.VMEM((R, D), BF), pltpu.VMEM((D, R), BF), pltpu.VMEM((R, D), F32)],
        ),
        out_shape=[shape((4, 4, 4, 48, 384)), shape((4, 4, 4, 64, 384))],
        compiler_params=room(24),
        name="ff_grad",
    )(place, active, d_up, second, far(cotangent), o_turned, d_branch))
    arrived(*d_o)
    distant = shift(after(turned, *d_o, place), "z", 2)
    sent = ordered(run(
        core_sum_kernel,
        "core_sum",
        24,
        [kept((4, 4, 48, 384))] + [shape((4, 4, 48, 384))] * 3 + [kept((4, 4, 64, 384))] + [shape((4, 4, 64, 384))] * 3,
        (place, *own, *got),
    ))
    a_sent, b_sent = sent[0:4], sent[4:8]
    a_parts = [a_sent[0], shift(a_sent[1], "x", 1), None, shift(a_sent[3], "x", 3)]
    b_parts = [b_sent[0], shift(b_sent[1], "y", 1), None, shift(b_sent[3], "y", 3)]

    def attend_back(g, sent=()):
        last = g == 2
        scratch = [
            pltpu.VMEM((4, 128, R), BF),
            pltpu.VMEM((4, 128, R), BF),
            pltpu.VMEM((4, HD, R), BF),
            pltpu.VMEM((4, R, 128), BF),
            pltpu.VMEM((4, R, 128), BF),
            pltpu.VMEM((4, R, HD), BF),
            pltpu.VMEM((4, HD, R), BF),
            pltpu.VMEM((4, R, HD), BF),
            pltpu.VMEM((4, 1, R), F32),
            pltpu.VMEM((4, HD, R), F32),
        ]
        if last:
            scratch = [pltpu.VMEM((4, 640, R), BF), pltpu.VMEM((D, 640), F32)] + scratch
            extra = (far(turned), far(near[0]), far(distant), far(near[1]), far(made[0]), far(made[1]))
        elif g == 1:
            extra = tuple(sent)
        else:
            extra = ()
        return ordered(pl.pallas_call(
            lambda *refs, g=g: attend_back_kernel(g, *refs),
            grid=(1,),
            in_specs=[SM] + [VM] * 4 + [pl.BlockSpec((HD, R), lambda _, g=g: (g, 0))] * 4 + [VM] * (2 + len(extra)),
            out_specs=[VM] * (6 if last else 5),
            out_shape=[[piece] * 4, [kept((384, R))] + [shape((384, R))] * 3, [kept((192, R))] + [piece] * 3][g]
            + ([shape((4, 4, 32, 640))] * 2 if last else [kept((4, 192, R))]),
            scratch_shapes=scratch,
            compiler_params=room(32 if last else 24),
            name="attend_back",
        )(place, *(far(h) for h in heads[g]), *(far(t) for t in d_o), far(attended[g]), far(spreads[g]), *extra))

    made = []
    *sent, one = attend_back(0)
    made.append(one)
    a_parts[2] = shift(after(a_sent[2], place), "x", 2)
    b_parts[2] = shift(after(b_sent[2], place), "y", 2)
    arrived(a_parts[1], a_parts[3], distant)
    *sent, one = attend_back(1, sent)
    made.append(one)
    first_pieces = spread_pieces(sent, "z")
    arrived(b_parts[1], b_parts[3])
    *sent, keep, send = attend_back(2)
    *sent, send = lax.optimization_barrier((*sent, send, *first_pieces, a_parts[2], b_parts[2]))[:5]
    last_pieces = spread_pieces(sent, "z")
    got = shift(send, "core", 1)

    sent = ordered(run(
        cut_kernel,
        "sum_first",
        24,
        [shape((4 * PART_A + 4 * GROUP, 128))] * 4 + [shape((4, 64, 384))] * 4,
        (place, *a_parts, *b_parts, keep, got),
    ))
    y_parts = [sent[0], shift(sent[1], "y", 1), sent[2], shift(sent[3], "y", 3)]
    x_parts = sent[4:8]
    so_far = ordered(run(
        input_grad_kernel,
        "input_grad",
        24,
        [shape((D, R), F32)],
        (place, *first_pieces, far(w_qkv)),
        [pltpu.VMEM((36, HD, R), BF)],
    ))[0]
    y_parts[2] = shift(after(y_parts[2], place), "y", 2)
    x_parts = [x_parts[0]] + [shift(after(x_parts[d], place), "x", d) for d in (1, 2, 3)]
    grad_stream, small = ordered(pl.pallas_call(
        last_kernel,
        grid=(1,),
        in_specs=[SM, SM] + [VM] * 9 + [weight_spec(c) for c in (2, 5, 8)],
        out_specs=[VM, VM],
        out_shape=[kept((1, ROWS, D), F32), shape((8, D), F32)],
        scratch_shapes=[pltpu.VMEM((3, 4, HD, R), BF)],
        compiler_params=room(24),
        name="ln_back",
    )(place, passes, *last_pieces, so_far, far(hidden), far(d_middle), gain_term, gains, *([far(w_qkv)] * 3)))
    sent = ordered(run(
        block_kernel,
        "sum_second",
        16,
        [shape((PART_A + PART_B + GROUP + TINY, 128))] * 4,
        (place, *y_parts, *x_parts, small),
    ))
    z_parts = spread_pieces(sent, "z")
    layer_out = ordered((pl.pallas_call(
        layer_out_kernel,
        grid=(FF // CHUNK,),
        in_specs=[SM, VM, pl.BlockSpec((R, CHUNK), lambda f: (0, f)), pl.BlockSpec((CHUNK, D), lambda f: (f, 0))],
        out_specs=VM,
        out_shape=kept((1, ROWS, D)),
        scratch_shapes=[pltpu.VMEM((R, D), F32)],
        compiler_params=room(16),
        name="layer_out",
    )(place, far(middle), far(active), far(w_down)),))[0]
    buffers = ordered(run(
        own_kernel,
        "sum_blocks",
        16,
        [shape((4 * GROUP + TINY + PART_A, 128)), shape((PART_B, 128))],
        (place, *z_parts),
    ))
    buffers = ordered(run(
        row_kernel,
        "stack_rows",
        16,
        [shape((4 * GROUP + TINY + 4 * PART_A, 128)), shape((4 * PART_B, 128))],
        (place, *all_of(buffers[0], "x"), *all_of(buffers[1], "y")),
    ))
    buffer = ordered(run(
        stack_kernel,
        "stack",
        16,
        [shape((ALL, 128))],
        (place, *all_of(buffers[0], "y"), *all_of(buffers[1], "x")),
    ))[0]
    *results, grad_gains, grad_pass = run(
        finish_kernel,
        "finish",
        32,
        [
            kept((192, 3 * D), F32),
            kept((192, D), F32),
            kept((192, FF), F32),
            kept((D, D), F32),
            shape((2, 192), F32),
            shape((PASSES, 192), F32),
        ],
        (place, buffer, shift(buffer, "core", 1)),
        [pltpu.VMEM((2, ALL, 128), BF), pltpu.VMEM((D, 8), F32)],
    )
    return (layer_out, grad_stream, *results, grad_gains.T, grad_pass.T)


def solution(mesh):
    tokens = P("batch", "blk", None)
    in_specs = (tokens, tokens, P("batch"), P(), P(), P(), P(), P(), P())
    out_specs = (tokens, tokens) + (P("blk", None),) * 6
    return jax.shard_map(on_device, mesh=mesh, in_specs=in_specs, out_specs=out_specs, check_vma=False)
```

```python
import jax
import jax.numpy as jnp
from jax import lax
from jax.experimental import pallas as pl
from jax.experimental.pallas import tpu as pltpu
from jax.sharding import PartitionSpec as P

D = 768
HEADS = 12
HD = 64
FF = 3072
PASSES = 5
ROWS = 510
R = 512
EPS = 1e-05
NEG = -1e30
BF = jnp.bfloat16
F32 = jnp.float32
VM = pl.BlockSpec(memory_space=pltpu.VMEM)
SM = pl.BlockSpec(memory_space=pltpu.SMEM)
HB = pl.BlockSpec(memory_space=pl.ANY)
MIB = 1024 * 1024


def room(mib):
    return pltpu.CompilerParams(vmem_limit_bytes=mib * MIB)


def run(kernel, name, mib, outs, operands, scratch=(), scalars=1):
    return pl.pallas_call(
        kernel,
        in_specs=[SM] * scalars + [VM] * (len(operands) - scalars),
        out_specs=[VM] * len(outs),
        out_shape=outs,
        scratch_shapes=list(scratch),
        compiler_params=room(mib),
        name=name,
    )(*operands)


def shape(dims, kind=BF):
    return jax.ShapeDtypeStruct(dims, kind)


def kept(dims, kind=BF):
    return pltpu.HBM(dims, kind)


def dot(left, right):
    return jnp.dot(left, right, preferred_element_type=F32)


def dot_nt(left, right):
    return lax.dot_general(left, right, (((1,), (1,)), ((), ())), preferred_element_type=F32)


def normalize(values):
    mean = jnp.mean(values, axis=-1, keepdims=True)
    centred = values - mean
    inverse = lax.rsqrt(jnp.mean(centred * centred, axis=-1, keepdims=True) + EPS)
    return centred * inverse, inverse


def norm_back(grad, unit, inverse, gain):
    scaled = grad * gain
    first = jnp.mean(scaled, axis=-1, keepdims=True)
    second = jnp.mean(scaled * unit, axis=-1, keepdims=True)
    return inverse * (scaled - first - unit * second)


def pass_index(blk, count):
    row = lax.broadcasted_iota(jnp.int32, (R, 1), 0) + blk * ROWS
    turns = jnp.floor((row.astype(F32) + 0.5) / count.astype(F32)).astype(jnp.int32)
    return row - turns * count


def pieces_out(stage, outs, blk):
    for d, out in enumerate(outs):
        out[...] = stage[lax.rem(blk + d, 4)]


def project(normed, weights, stage, outs, blk):
    for part, weight in enumerate(weights):
        got = dot(normed, weight[...])
        if part == 0:
            got = got.astype(BF) * jnp.asarray(HD ** (-0.5), BF)
        turned = got.astype(BF).T
        for j in range(4):
            stage[j, 64 * part : 64 * part + 64, :] = turned[64 * j : 64 * j + 64]
    pieces_out(stage, outs, blk)


def project(normed, weights, stage):
    for part, weight in enumerate(weights):
        got = dot(normed, weight[...])
        if part == 0:
            got = got.astype(BF) * jnp.asarray(HD ** (-0.5), BF)
        flipped = got.astype(BF).T
        for j in range(4):
            stage[j, 64 * part : 64 * part + 64, :] = flipped[64 * j : 64 * j + 64]


def first_kernel(blk_ref, count_ref, stream, embed, gains, wq, wk, wv, hidden, turned, p0, p1, p2, p3, normed, stage):
    blk = blk_ref[0]
    hidden[R - 8 : R, :] = jnp.zeros((8, D), F32)
    hidden[0:ROWS, :] = stream[0].astype(F32)
    which = pass_index(blk, count_ref[0])
    added = embed[0:1, :]
    for r in range(1, PASSES):
        added = jnp.where(which == r, embed[r : r + 1, :], added)
    values = hidden[...] + added
    hidden[...] = values
    unit, _ = normalize(values)
    row = lax.broadcasted_iota(jnp.int32, (R, 1), 0)
    low = jnp.where(row < ROWS, unit * gains[0:1, :], 0.0).astype(BF)
    normed[...] = low
    project(low, (wq, wk, wv), stage)
    for d, out in enumerate((p0, p1, p2, p3)):
        out[...] = stage[lax.rem(blk + d, 4)]
    turned[...] = low.T


def second_kernel(blk_ref, normed, wq1, wk1, wv1, wq2, wk2, wv2, p0, p1, p2, p3, stage):
    blk = blk_ref[0]
    for n, weights in enumerate(((wq1, wk1, wv1), (wq2, wk2, wv2))):
        project(normed[...], weights, stage.at[n])
        for d, out in enumerate((p0, p1, p2, p3)):
            out[192 * n : 192 * n + 192, :] = stage[n, lax.rem(blk + d, 4)]


def load_heads(blk, at, parts, q_rows, k_rows, v_rows, k_cols):
    for d in range(4):
        s = lax.rem(blk + 4 - d, 4)
        piece = parts[d]
        q_rows[s, 0:64, :] = piece[at : at + 64, :]
        k_rows[s, 0:64, :] = piece[at + 64 : at + 128, :]
        v_rows[s] = piece[at + 128 : at + 192, :]
    row = lax.broadcasted_iota(jnp.int32, (64, R), 0)
    col = lax.broadcasted_iota(jnp.int32, (64, R), 1)
    one = jnp.where(row == 0, 1.0, 0.0).astype(BF)
    off = jnp.where((row == 0) & (col >= ROWS), NEG, 0.0).astype(BF)
    for s in range(4):
        q_rows[s, 64:128, :] = one
        k_rows[s, 64:128, :] = off
    for s in range(4):
        k_cols[s] = k_rows[s].T


def causal():
    key = lax.broadcasted_iota(jnp.int32, (R, R), 0)
    query = lax.broadcasted_iota(jnp.int32, (R, R), 1)
    return key <= query


def attend_head(blk, n, parts, attended, spread, q_rows, k_rows, v_rows, k_cols, scores, stage):
    load_heads(blk, 192 * n, parts, q_rows, k_rows, v_rows, k_cols)
    for i in range(4):
        top = None
        for j in range(i + 1):
            got = dot(k_cols[j], q_rows[i])
            if i == j:
                got = jnp.where(causal(), got, NEG)
            scores[j] = got
            best = jnp.max(got, axis=0, keepdims=True)
            top = best if top is None else jnp.maximum(top, best)
        total = jnp.zeros((1, R), F32)
        summed = jnp.zeros((HD, R), F32)
        for j in range(i + 1):
            raised = jnp.exp(scores[j] - top)
            total = total + jnp.sum(raised, axis=0, keepdims=True)
            summed = summed + dot(v_rows[j], raised.astype(BF))
        result = summed / total
        attended[n, i] = result
        spread[n, i] = top + jnp.log(total)
        stage[i] = result.astype(BF)


def attend_kernel(count, blk_ref, r0, r1, r2, r3, *rest):
    earlier, rest = (rest[:4], rest[4:]) if count == 2 else ((), rest)
    p0, p1, p2, p3, attended, spread, *scratch = rest
    blk = blk_ref[0]
    for n in range(count):
        stage = scratch[-1].at[n]
        attend_head(blk, n, (r0, r1, r2, r3), attended, spread, *(ref.at[n] for ref in scratch))
        for d, out in enumerate((p0, p1, p2, p3)):
            at = 64 * (n + 1) if count == 2 else 0
            out[at : at + 64, :] = stage[lax.rem(blk + d, 4)]
    for d, value in enumerate(earlier):
        (p0, p1, p2, p3)[d][0:64, :] = value[...]


def attend_back_kernel(g, blk_ref, r0, r1, r2, r3, g0, g1, g2, g3, attended, spread, *rest):
    n = max(g - 1, 0)
    if g == 1:
        f0, f1, f2, f3, *rest = rest
    p0, p1, p2, p3, outs, q_rows, k_rows, v_rows, k_cols, q_cols, v_cols, o_rows, o_cols, delta, dq = rest
    blk = blk_ref[0]
    load_heads(blk, 192 * n, (r0, r1, r2, r3), q_rows, k_rows, v_rows, k_cols)
    for d, piece in enumerate((g0, g1, g2, g3)):
        o_rows[lax.rem(blk + 4 - d, 4)] = piece[...]
    for s in range(4):
        q_cols[s] = q_rows[s].T
        v_cols[s] = v_rows[s].T
        o_cols[s] = o_rows[s].T
        delta[s] = jnp.sum(o_rows[s].astype(F32) * attended[n, s], axis=0, keepdims=True)
        dq[s] = jnp.zeros((HD, R), F32)
    for j in range(4):
        dk = jnp.zeros((R, 2 * HD), F32)
        dv = jnp.zeros((R, HD), F32)
        for i in range(j, 4):
            got = dot(k_cols[j], q_rows[i])
            if i == j:
                got = jnp.where(causal(), got, NEG)
            probs = jnp.exp(got - spread[n, i])
            d_probs = dot(v_cols[j], o_rows[i])
            d_scores = (probs * (d_probs - delta[i])).astype(BF)
            dv = dv + dot(probs.astype(BF), o_cols[i])
            dk = dk + dot(d_scores, q_cols[i])
            dq[i] = dq[i] + dot(k_rows[j, 0:64, :], d_scores)
        outs[j, 0:64, :] = (dq[j] * HD ** (-0.5)).astype(BF)
        outs[j, 64:128, :] = dk[:, 0:64].astype(BF).T
        outs[j, 128:192, :] = dv.astype(BF).T
    for d, out in enumerate((p0, p1, p2, p3)):
        piece = outs[lax.rem(blk + d, 4)]
        if g == 1:
            out[0:192, :] = (f0, f1, f2, f3)[d][...]
            out[192:384, :] = piece
        else:
            out[...] = piece


def units(piece):
    for n in range(7):
        u = 7 * piece + n
        if u < 48:
            yield 16 * n, (16 * (u // 4), 2 * (u % 4)), (16 * (u // 4), 2 * (u % 4) + 1)
        elif u < 54:
            yield 16 * n, (32 * (u - 48), 8), (32 * (u - 48) + 16, 8)


def head_grad_kernel(place_ref, t0, t1, t2, t3, e0, e1, e2, keep, send, sides, made, pieces):
    blk, core = place_ref[0], place_ref[3]
    total = jnp.zeros((D, 640), F32)
    for d, piece in enumerate((t0, t1, t2, t3)):
        s = lax.rem(blk + 4 - d, 4)
        for g, side in enumerate((e0, e1, e2)):
            sides[d, 192 * g : 192 * g + 192, :] = side[s]
        sides[d, 576:640, :] = jnp.zeros((64, R), BF)
        total = total + dot_nt(piece[...], sides[d])
    made[...] = total
    pieces[...] = jnp.zeros((8, 4, GROUP, 128), BF)
    for k in range(8):
        for at, (row, left), (row_right, right) in units(k):
            for i in range(4):
                r = 192 * i + row
                if right == left:
                    halves = (made[r : r + 16, 512:576], made[r + 16 : r + 32, 512:576])
                    block = jnp.concatenate(halves, axis=1)
                else:
                    block = made[r : r + 16, 64 * left : 64 * left + 128]
                pieces[k, i, at : at + 16, :] = block.astype(BF)
    for q in range(4):
        keep[q] = pieces[4 * core + q]
        send[q] = pieces[4 * (1 - core) + q]


def gelu_both(value):
    c = (2.0 / jnp.pi) ** 0.5
    square = value * value
    t = jnp.tanh(c * value * (1.0 + 0.044715 * square))
    cdf = 0.5 * (1.0 + t)
    slope = cdf + (0.5 * c) * value * (1.0 - t * t) * (1.0 + 3.0 * 0.044715 * square)
    return value * cdf, slope


CHUNK = 768


def active_grad_kernel(place_ref, cot, w_down, out, dy, pad):
    @pl.when(pl.program_id(0) == 0)
    def _():
        pad[R - 8 : R, :] = jnp.zeros((8, D), F32)
        pad[0:ROWS, :] = cot[0].astype(F32)
        dy[...] = pad[...].astype(BF)

    out[...] = dot_nt(dy[...], w_down[...])


def up_cut(values, store):
    for z in range(4):
        for yy in range(4):
            store(yy, z, values[192 * z + 48 * yy : 192 * z + 48 * yy + 48, :])


def down_cut(values, store):
    for yy in range(4):
        for xx in range(4):
            r, col = 48 * (2 * yy + xx // 2), 384 * (xx % 2)
            store(yy, xx, values[r : r + 48, col : col + 384])


def out_cut(values, out):
    for i in range(4):
        for n in range(16):
            rows = values[192 * i + 16 * n : 192 * i + 16 * n + 16, :] if n < 12 else jnp.zeros((16, 384), BF)
            out[n // 4, n % 4, i, 48:64] = rows


def put_block(out, at, rows):
    out[at] = rows.astype(BF)


def ff_kernel(
    blk_ref, r0, r1, r2, r3, hidden, cot, gains, w_out, w_up, d_active,
    active, d_up, second, middle, o_turned, d_branch, d_middle, p0, p1, p2, p3, a_out, b_out, gain_term,
    dy, back, stage, second_turned,
):
    step = pl.program_id(0)
    core = blk_ref[3]

    @pl.when(step == 0)
    def _():
        blk = blk_ref[0]
        for d, piece in enumerate((r0, r1, r2, r3)):
            s = lax.rem(blk + 4 - d, 4)
            for g in range(3):
                stage[4 * g + s] = piece[64 * g : 64 * g + 64, :]
        o_rows = stage[...].reshape(D, R)
        o_turned[...] = o_rows
        values = hidden[...] + dot(o_rows.T, w_out[...])
        middle[...] = values
        unit, _ = normalize(values)
        second[...] = (unit * gains[1:2, :]).astype(BF)
        back[R - 8 : R, :] = jnp.zeros((8, D), F32)
        back[0:ROWS, :] = cot[0].astype(F32)
        dy[...] = back[...].astype(BF)
        back[...] = jnp.zeros((R, D), F32)
        second_turned[...] = second[...].T

    upward = dot(second[...], w_up[...])
    act, slope = gelu_both(upward)
    act = act.astype(BF)
    active[...] = act
    d_upward = (d_active[...] * slope).astype(BF)
    d_up[...] = d_upward
    back[...] += dot_nt(d_upward, w_up[...])

    first = core == 0
    other_up = jnp.where(first, d_upward[:, 384:768], d_upward[:, 0:384])
    other_act = jnp.where(first, act[:, 384:768], act[:, 0:384])
    up_cut(dot(second_turned[...], other_up), lambda yy, z, rows: put_block(a_out, (yy, step, z), rows))
    down_cut(dot(other_act.T, dy[...]), lambda yy, xx, rows: put_block(b_out, (yy, xx, step, slice(0, 48)), rows))

    @pl.when(step == FF // CHUNK - 1)
    def _():
        blk = blk_ref[0]
        unit, inverse = normalize(middle[...])
        grad = back[...]
        gain_term[...] = jnp.sum(grad * unit, axis=0, keepdims=True)
        total = dy[...].astype(F32) + norm_back(grad, unit, inverse, gains[1:2, :])
        d_middle[...] = total
        low = total.astype(BF)
        d_branch[...] = low
        stage[...] = dot_nt(w_out[...], low).astype(BF).reshape(HEADS, HD, R)
        out_cut(dot(o_turned[...], jnp.where(core == 0, low[:, 384:768], low[:, 0:384])).astype(BF), b_out)
        for d, out in enumerate((p0, p1, p2, p3)):
            j = lax.rem(blk + d, 4)
            for g in range(3):
                out[64 * g : 64 * g + 64, :] = stage[4 * g + j]


def ff_grad_kernel(place_ref, active, d_up, second, cot, o_turned, d_branch, a_out, b_out, dy, second_turned, pad):
    step = pl.program_id(0)

    @pl.when(step == 0)
    def _():
        pad[R - 8 : R, :] = jnp.zeros((8, D), F32)
        pad[0:ROWS, :] = cot[0].astype(F32)
        dy[...] = pad[...].astype(BF)
        second_turned[...] = second[...].T
        out_cut(dot(o_turned[...], d_branch[...]).astype(BF), b_out)

    up_cut(dot(second_turned[...], d_up[...]), lambda yy, z, rows: put_block(a_out, (yy, step, z), rows))
    down_cut(dot(active[...].T, dy[...]), lambda yy, xx, rows: put_block(b_out, (yy, xx, step, slice(0, 48)), rows))


def core_sum_kernel(place_ref, a_mine, b_mine, a_got, b_got, a0, a1, a2, a3, b0, b1, b2, b3):
    x, y = place_ref[1], place_ref[2]
    for d, (a_out, b_out) in enumerate(((a0, b0), (a1, b1), (a2, b2), (a3, b3))):
        xx, yy = lax.rem(x + d, 4), lax.rem(y + d, 4)
        for n in range(4):
            a_out[n] = (a_mine[n, xx].astype(F32) + a_got[n, xx].astype(F32)).astype(BF)
            b_out[n] = (b_mine[yy, n].astype(F32) + b_got[yy, n].astype(F32)).astype(BF)


def total_of(parts):
    return (parts[0].astype(F32) + parts[2].astype(F32)) + (parts[1].astype(F32) + parts[3].astype(F32))


TINY = 96
GROUP = 112
PART_A = 144
PART_B = 192


def put(buffer, at, block):
    rows, lanes = block.shape
    for t in range(lanes // 128):
        buffer[at + rows * t : at + rows * t + rows, :] = block[:, 128 * t : 128 * t + 128]


def put_small(buffer, at, value):
    high = value.astype(BF)
    low = (value - high.astype(F32)).astype(BF)
    put(buffer, at, jnp.concatenate([high, low], axis=0))


def get_small(buffer, at):
    parts = []
    for t in range(6):
        part = buffer[at + 16 * t : at + 16 * t + 16, :].astype(F32)
        parts.append(part[0:8] + part[8:16])
    return jnp.concatenate(parts, axis=1)


def take(buffer, at, rows):
    return jnp.concatenate([buffer[at + rows * t : at + rows * t + rows, :] for t in range(3)], axis=1)


def cut_kernel(place_ref, a0, a1, a2, a3, b0, b1, b2, b3, keep, got, y0, y1, y2, y3, x0, x1, x2, x3):
    x, y = place_ref[1], place_ref[2]
    for d, (y_out, x_out) in enumerate(((y0, x0), (y1, x1), (y2, x2), (y3, x3))):
        yy, xx = lax.rem(y + d, 4), lax.rem(x + d, 4)
        a_sum = total_of([r[yy] for r in (a0, a1, a2, a3)]).astype(BF)
        heads = (keep[yy].astype(F32) + got[yy].astype(F32)).astype(BF)
        for i in range(4):
            put(y_out, PART_A * i, a_sum[i])
            y_out[4 * PART_A + GROUP * i : 4 * PART_A + GROUP * i + GROUP, :] = heads[i]
        x_out[...] = total_of([r[xx] for r in (b0, b1, b2, b3)]).astype(BF)


def block_kernel(place_ref, y0, y1, y2, y3, x0, x1, x2, x3, small, o0, o1, o2, o3):
    z = place_ref[0]
    for d, out in enumerate((o0, o1, o2, o3)):
        i = lax.rem(z + d, 4)
        start = pl.multiple_of(PART_A * i, 16)
        out[0:PART_A, :] = total_of([r[pl.ds(start, PART_A), :] for r in (y0, y1, y2, y3)]).astype(BF)
        put(out, PART_A, total_of([r[i] for r in (x0, x1, x2, x3)]).astype(BF))
        start = pl.multiple_of(4 * PART_A + GROUP * i, 16)
        at = PART_A + PART_B
        out[at : at + GROUP, :] = total_of([r[pl.ds(start, GROUP), :] for r in (y0, y1, y2, y3)]).astype(BF)
        put_small(out, at + GROUP, small[...])


def own_kernel(place_ref, z0, z1, z2, z3, x_out, y_out):
    parts = (z0, z1, z2, z3)
    at = PART_A + PART_B
    for d, r in enumerate(parts):
        x_out[GROUP * d : GROUP * d + GROUP, :] = r[at : at + GROUP, :]
    put_small(x_out, 4 * GROUP, total_of([get_small(r, at + GROUP) for r in parts]))
    x_out[4 * GROUP + TINY : 4 * GROUP + TINY + PART_A, :] = total_of([r[0:PART_A, :] for r in parts]).astype(BF)
    y_out[...] = total_of([r[PART_A : PART_A + PART_B, :] for r in parts]).astype(BF)


def row_kernel(place_ref, x0, x1, x2, x3, y0, y1, y2, y3, y_out, x_out):
    parts = (x0, x1, x2, x3)
    y_out[0 : 4 * GROUP, :] = total_of([r[0 : 4 * GROUP, :] for r in parts]).astype(BF)
    put_small(y_out, 4 * GROUP, total_of([get_small(r, 4 * GROUP) for r in parts]))
    at = 4 * GROUP + TINY
    for d, (a, b) in enumerate(zip(parts, (y0, y1, y2, y3))):
        y_out[at + PART_A * d : at + PART_A * d + PART_A, :] = a[at : at + PART_A, :]
        x_out[PART_B * d : PART_B * d + PART_B, :] = b[...]


ALL_TINY = 16 * GROUP
ALL_A = ALL_TINY + TINY
ALL_B = ALL_A + 16 * PART_A
ALL = ALL_B + 16 * PART_B


def stack_kernel(place_ref, y0, y1, y2, y3, x0, x1, x2, x3, out):
    parts = (y0, y1, y2, y3)
    put_small(out, ALL_TINY, total_of([get_small(r, 4 * GROUP) for r in parts]))
    at = 4 * GROUP + TINY
    for d, (r, b) in enumerate(zip(parts, (x0, x1, x2, x3))):
        out[4 * GROUP * d : 4 * GROUP * d + 4 * GROUP, :] = r[0 : 4 * GROUP, :]
        out[ALL_A + 4 * PART_A * d : ALL_A + 4 * PART_A * d + 4 * PART_A, :] = r[at : at + 4 * PART_A, :]
        out[ALL_B + 4 * PART_B * d : ALL_B + 4 * PART_B * d + 4 * PART_B, :] = b[...]


def finish_kernel(place_ref, mine, other, grad_qkv, grad_out, grad_up, grad_down, gains, passes, pair, turned):
    z, x, y, core = place_ref[0], place_ref[1], place_ref[2], place_ref[3]
    pair[core] = mine[...]
    pair[1 - core] = other[...]

    def rows(c, at, count):
        return pair[c, pl.ds(pl.multiple_of(at, 16), count), :].astype(F32)

    for c in range(2):
        for xx in range(4):
            dx = lax.rem(x + 4 - xx, 4)
            for yy in range(4):
                dy = lax.rem(y + 4 - yy, 4)
                a = rows(c, ALL_A + 4 * PART_A * dy + PART_A * dx, PART_A)
                b = rows(c, ALL_B + 4 * PART_B * dx + PART_B * dy, PART_B)
                r = 384 * c + 48 * (2 * yy + xx // 2)
                for t in range(3):
                    col = 384 * (2 * xx + c) + 128 * t
                    grad_up[48 * yy : 48 * yy + 48, col : col + 128] = a[48 * t : 48 * t + 48]
                    col = 384 * (xx % 2) + 128 * t
                    grad_down[r : r + 48, col : col + 128] = b[64 * t : 64 * t + 48]
                    if yy < 3:
                        n, col = 16 * (4 * yy + xx), 384 * c + 128 * t
                        grad_out[n : n + 16, col : col + 128] = b[64 * t + 48 : 64 * t + 64]
        for yy in range(4):
            dy = lax.rem(y + 4 - yy, 4)
            for j in range(4):
                dz = lax.rem(z + 4 - j, 4)
                piece = rows(c, 4 * GROUP * dy + GROUP * dz, GROUP)
                for at, *halves in units(4 * c + yy):
                    for side, (r, n) in enumerate(halves):
                        col = D * (n % 3) + 64 * (4 * (n // 3) + j)
                        grad_qkv[r : r + 16, col : col + 64] = piece[at : at + 16, 64 * side : 64 * side + 64]
    small = get_small(mine, ALL_TINY) + get_small(other, ALL_TINY)
    turned[...] = small.T
    part = turned[pl.ds(pl.multiple_of(192 * z, 8), 192), :]
    part = part.T
    gains[...] = part[0:2, :]
    passes[...] = part[2:7, :]


def layer_out_kernel(place_ref, middle, active, w_down, out, total):
    step = pl.program_id(0)

    @pl.when(step == 0)
    def _():
        total[...] = middle[...]

    total[...] += dot(active[...], w_down[...])

    @pl.when(step == FF // CHUNK - 1)
    def _():
        out[0] = total[0:ROWS, :].astype(BF)


def input_grad_kernel(blk_ref, a0, a1, a2, a3, w_qkv, out, stage):
    blk = blk_ref[0]
    stage[...] = jnp.zeros((36, HD, R), BF)
    for d, piece in enumerate((a0, a1, a2, a3)):
        s = lax.rem(blk + 4 - d, 4)
        for n in range(6):
            stage[12 * (n % 3) + 4 * (n // 3) + s] = piece[64 * n : 64 * n + 64, :]
    out[...] = dot(w_qkv[...], stage[...].reshape(3 * D, R))


def last_kernel(
    blk_ref, count_ref, c0, c1, c2, c3, so_far, hidden, d_middle, gain_term, gains, wq, wk, wv, grad_stream, small, stage
):
    blk = blk_ref[0]
    for d, piece in enumerate((c0, c1, c2, c3)):
        s = lax.rem(blk + 4 - d, 4)
        for part in range(3):
            stage[part, s] = piece[64 * part : 64 * part + 64, :]
    turned = so_far[...]
    for part, weight in enumerate((wq, wk, wv)):
        turned = turned + dot(weight[...], stage[part].reshape(256, R))
    grad = turned.T
    unit, inverse = normalize(hidden[...])
    total = d_middle[...] + norm_back(grad, unit, inverse, gains[0:1, :])
    grad_stream[0] = total[0:ROWS, :]
    row = lax.broadcasted_iota(jnp.int32, (R, 1), 0)
    which = jnp.where(row < ROWS, pass_index(blk, count_ref[0]), -1)
    small[0:1, :] = jnp.sum(grad * unit, axis=0, keepdims=True)
    small[1:2, :] = gain_term[...]
    for r in range(PASSES):
        small[2 + r : 3 + r, :] = jnp.sum(jnp.where(which == r, total, 0.0), axis=0, keepdims=True)
    small[7:8, :] = jnp.zeros((1, D), F32)


def shift(values, axis, d):
    if axis == "z":
        return lax.ppermute(values, "blk", [(i, (i + d) % 4) for i in range(4)])
    pairs = []
    for b in range(32):
        y, x, core = b // 8, (b // 2) % 4, b % 2
        if axis == "y":
            y = (y + d) % 4
        elif axis == "x":
            x = (x + d) % 4
        else:
            core = (core + d) % 2
        pairs.append((b, 8 * y + 2 * x + core))
    return lax.ppermute(values, "batch", pairs)


def spread_pieces(pieces, axis):
    two, three, one = (shift(pieces[d], axis, d) for d in (2, 3, 1))
    return (pieces[0], one, two, three)


def all_of(value, axis):
    return spread_pieces((value,) * 4, axis)


def after(value, *others):
    return lax.optimization_barrier((value,) + others)[0]


def far(value):
    return pltpu.with_memory_space_constraint(value, pltpu.HBM)


def weight_spec(column):
    return pl.BlockSpec((D, 256), lambda *_, column=column: (0, column))


def on_device(stream, cotangent, passes, w_qkv, w_out, w_up, w_down, ln_gains, pass_embed):
    z = lax.axis_index("blk").astype(jnp.int32)
    batch = lax.axis_index("batch").astype(jnp.int32)
    place = jnp.stack([z, batch // 2 % 4, batch // 8, batch % 2])
    gains = ln_gains.T
    embed = pass_embed.T
    piece = shape((192, R))
    full = shape((R, D))

    def arrived(*values):
        nonlocal place
        place = lax.optimization_barrier((place,) + values)[0]

    def ordered(outs):
        nonlocal place
        *outs, first = outs
        place, first = lax.optimization_barrier((place, first))
        return (*outs, first)

    hidden, turned, *sent, normed = ordered(pl.pallas_call(
        first_kernel,
        grid=(1,),
        in_specs=[SM, SM, VM, VM, VM, weight_spec(0), weight_spec(3), weight_spec(6)],
        out_specs=[VM] * 7,
        out_shape=[kept((R, D), F32), kept((D, R)), kept((192, R)), piece, piece, piece, full],
        scratch_shapes=[pltpu.VMEM((4, 192, R), BF)],
        compiler_params=room(24),
        name="ln_qkv",
    )(place, passes, far(stream), far(embed), far(gains), *([far(w_qkv)] * 3)))
    early = spread_pieces(sent, "z")
    sent = ordered(pl.pallas_call(
        second_kernel,
        grid=(1,),
        in_specs=[SM, VM] + [weight_spec(c) for c in (1, 4, 7, 2, 5, 8)],
        out_specs=[VM] * 4,
        out_shape=[kept((384, R))] + [shape((384, R))] * 3,
        scratch_shapes=[pltpu.VMEM((2, 4, 192, R), BF)],
        compiler_params=room(24),
        name="qkv_rest",
    )(place, normed, *([far(w_qkv)] * 6)))
    late = [sent[0], shift(sent[1], "z", 1), sent[2], shift(sent[3], "z", 3)]

    attended, spreads, sent = [], [], []
    for count, parts in ((1, early), (2, late)):
        *sent, result, spread = ordered(run(
            lambda *refs, count=count: attend_kernel(count, *refs),
            "attend",
            24,
            [shape((192 if count == 2 else HD, R))] * 4 + [kept((count, 4, HD, R), F32), kept((count, 4, 1, R), F32)],
            (place, *parts, *sent),
            [
                pltpu.VMEM((count, 4, 128, R), BF),
                pltpu.VMEM((count, 4, 128, R), BF),
                pltpu.VMEM((count, 4, HD, R), BF),
                pltpu.VMEM((count, 4, R, 128), BF),
                pltpu.VMEM((count, 4, R, R), F32),
                pltpu.VMEM((count, 4, HD, R), BF),
            ],
        ))
        if count == 1:
            late[2] = shift(after(late[2], place), "z", 2)
            d_active = ordered((pl.pallas_call(
                active_grad_kernel,
                grid=(FF // CHUNK,),
                in_specs=[SM, VM, pl.BlockSpec((CHUNK, D), lambda f: (f, 0))],
                out_specs=pl.BlockSpec((R, CHUNK), lambda f: (0, f)),
                out_shape=kept((R, FF), F32),
                scratch_shapes=[pltpu.VMEM((R, D), BF), pltpu.VMEM((R, D), F32)],
                compiler_params=room(16),
                name="active_grad",
            )(place, far(cotangent), far(w_down)),))[0]
        attended += [result] * count
        spreads += [spread] * count
    heads = (early, late, late)
    back_o = spread_pieces(sent, "z")
    near = after(turned, *back_o)
    near = (shift(near, "z", 1), shift(near, "z", 3))

    active, d_up, second, middle, o_turned, d_branch, d_middle, *sent, a_other, b_other, gain_term = ordered(pl.pallas_call(
        ff_kernel,
        grid=(FF // CHUNK,),
        in_specs=[SM] + [VM] * 4 + [VM, VM, VM, VM]
        + [pl.BlockSpec((D, CHUNK), lambda f: (0, f)), pl.BlockSpec((R, CHUNK), lambda f: (0, f))],
        out_specs=[pl.BlockSpec((R, CHUNK), lambda f: (0, f)), pl.BlockSpec((R, CHUNK), lambda f: (0, f))] + [VM] * 12,
        out_shape=[shape((R, FF)), shape((R, FF)), full, shape((R, D), F32), shape((D, R)), full, kept((R, D), F32)]
        + [kept((192, R))] + [piece] * 3 + [shape((4, 4, 4, 48, 384)), shape((4, 4, 4, 64, 384)), shape((1, D), F32)],
        scratch_shapes=[pltpu.VMEM((R, D), BF), pltpu.VMEM((R, D), F32), pltpu.VMEM((HEADS, HD, R), BF), pltpu.VMEM((D, R), BF)],
        compiler_params=room(36),
        name="ff",
    )(place, *back_o, far(hidden), far(cotangent), gains, far(w_out), far(w_up), far(d_active)))
    *sent, a_other, b_other = lax.optimization_barrier((*sent, a_other, b_other, *near))[:6]
    d_o = spread_pieces(sent, "z")

    got = (shift(a_other, "core", 1), shift(b_other, "core", 1))
    own = ordered(pl.pallas_call(
        ff_grad_kernel,
        grid_spec=pltpu.PrefetchScalarGridSpec(
            num_scalar_prefetch=1,
            grid=(4,),
            in_specs=[
                pl.BlockSpec((R, 384), lambda i, s: (0, 2 * i + s[3])),
                pl.BlockSpec((R, 384), lambda i, s: (0, 2 * i + s[3])),
                VM,
                VM,
                VM,
                pl.BlockSpec((R, 384), lambda i, s: (0, s[3])),
            ],
            out_specs=[VM] * 2,
            scratch_shapes=[pltpu.VMEM((R, D), BF), pltpu.VMEM((D, R), BF), pltpu.VMEM((R, D), F32)],
        ),
        out_shape=[shape((4, 4, 4, 48, 384)), shape((4, 4, 4, 64, 384))],
        compiler_params=room(24),
        name="ff_grad",
    )(place, active, d_up, second, far(cotangent), o_turned, d_branch))
    arrived(*d_o)
    distant = shift(after(turned, *d_o, place), "z", 2)
    sent = ordered(run(
        core_sum_kernel,
        "core_sum",
        24,
        [kept((4, 4, 48, 384))] + [shape((4, 4, 48, 384))] * 3 + [kept((4, 4, 64, 384))] + [shape((4, 4, 64, 384))] * 3,
        (place, *own, *got),
    ))
    a_sent, b_sent = sent[0:4], sent[4:8]
    a_parts = [a_sent[0], shift(a_sent[1], "x", 1), None, shift(a_sent[3], "x", 3)]
    b_parts = [b_sent[0], shift(b_sent[1], "y", 1), None, shift(b_sent[3], "y", 3)]

    def attend_back(g, sent=()):
        return ordered(pl.pallas_call(
            lambda *refs: attend_back_kernel(g, *refs),
            grid=(1,),
            in_specs=[SM] + [VM] * 4 + [pl.BlockSpec((HD, R), lambda _: (g, 0))] * 4 + [VM] * (2 + len(sent)),
            out_specs=[VM] * 5,
            out_shape=[[piece] * 4, [kept((384, R))] + [shape((384, R))] * 3, [kept((192, R))] + [piece] * 3][g] + [kept((4, 192, R))],
            scratch_shapes=[
                pltpu.VMEM((4, 128, R), BF),
                pltpu.VMEM((4, 128, R), BF),
                pltpu.VMEM((4, HD, R), BF),
                pltpu.VMEM((4, R, 128), BF),
                pltpu.VMEM((4, R, 128), BF),
                pltpu.VMEM((4, R, HD), BF),
                pltpu.VMEM((4, HD, R), BF),
                pltpu.VMEM((4, R, HD), BF),
                pltpu.VMEM((4, 1, R), F32),
                pltpu.VMEM((4, HD, R), F32),
            ],
            compiler_params=room(24),
            name="attend_back",
        )(place, *(far(h) for h in heads[g]), *(far(t) for t in d_o), far(attended[g]), far(spreads[g]), *sent))

    made = []
    *sent, one = attend_back(0)
    made.append(one)
    a_parts[2] = shift(after(a_sent[2], place), "x", 2)
    b_parts[2] = shift(after(b_sent[2], place), "y", 2)
    arrived(a_parts[1], a_parts[3], distant)
    *sent, one = attend_back(1, sent)
    made.append(one)
    first_pieces = spread_pieces(sent, "z")
    arrived(b_parts[1], b_parts[3])
    *sent, one = attend_back(2)
    made.append(one)
    keep, send = ordered(run(
        head_grad_kernel,
        "head_grad",
        32,
        [shape((4, 4, GROUP, 128))] * 2,
        (place, far(turned), far(near[0]), far(distant), far(near[1]), *(far(m) for m in made)),
        [pltpu.VMEM((4, 640, R), BF), pltpu.VMEM((D, 640), F32), pltpu.VMEM((8, 4, GROUP, 128), BF)],
    ))
    arrived(*first_pieces, a_parts[2], b_parts[2])
    *sent, send = lax.optimization_barrier((*sent, send, *first_pieces, a_parts[2], b_parts[2]))[:5]
    last_pieces = spread_pieces(sent, "z")
    got = shift(send, "core", 1)

    so_far = ordered(run(
        input_grad_kernel,
        "input_grad",
        24,
        [shape((D, R), F32)],
        (place, *first_pieces, far(w_qkv)),
        [pltpu.VMEM((36, HD, R), BF)],
    ))[0]
    sent = ordered(run(
        cut_kernel,
        "sum_first",
        24,
        [shape((4 * PART_A + 4 * GROUP, 128))] * 4 + [shape((4, 64, 384))] * 4,
        (place, *a_parts, *b_parts, keep, got),
    ))
    y_parts, x_parts = spread_pieces(sent[0:4], "y"), spread_pieces(sent[4:8], "x")
    grad_stream, small = ordered(pl.pallas_call(
        last_kernel,
        grid=(1,),
        in_specs=[SM, SM] + [VM] * 9 + [weight_spec(c) for c in (2, 5, 8)],
        out_specs=[VM, VM],
        out_shape=[kept((1, ROWS, D), F32), shape((8, D), F32)],
        scratch_shapes=[pltpu.VMEM((3, 4, HD, R), BF)],
        compiler_params=room(24),
        name="ln_back",
    )(place, passes, *last_pieces, so_far, far(hidden), far(d_middle), gain_term, gains, *([far(w_qkv)] * 3)))
    sent = ordered(run(
        block_kernel,
        "sum_second",
        16,
        [shape((PART_A + PART_B + GROUP + TINY, 128))] * 4,
        (place, *y_parts, *x_parts, small),
    ))
    z_parts = spread_pieces(sent, "z")
    layer_out = ordered((pl.pallas_call(
        layer_out_kernel,
        grid=(FF // CHUNK,),
        in_specs=[SM, VM, pl.BlockSpec((R, CHUNK), lambda f: (0, f)), pl.BlockSpec((CHUNK, D), lambda f: (f, 0))],
        out_specs=VM,
        out_shape=kept((1, ROWS, D)),
        scratch_shapes=[pltpu.VMEM((R, D), F32)],
        compiler_params=room(16),
        name="layer_out",
    )(place, far(middle), far(active), far(w_down)),))[0]
    buffers = ordered(run(
        own_kernel,
        "sum_blocks",
        16,
        [shape((4 * GROUP + TINY + PART_A, 128)), shape((PART_B, 128))],
        (place, *z_parts),
    ))
    buffers = ordered(run(
        row_kernel,
        "stack_rows",
        16,
        [shape((4 * GROUP + TINY + 4 * PART_A, 128)), shape((4 * PART_B, 128))],
        (place, *all_of(buffers[0], "x"), *all_of(buffers[1], "y")),
    ))
    buffer = ordered(run(
        stack_kernel,
        "stack",
        16,
        [shape((ALL, 128))],
        (place, *all_of(buffers[0], "y"), *all_of(buffers[1], "x")),
    ))[0]
    *results, grad_gains, grad_pass = run(
        finish_kernel,
        "finish",
        32,
        [
            kept((192, 3 * D), F32),
            kept((192, D), F32),
            kept((192, FF), F32),
            kept((D, D), F32),
            shape((2, 192), F32),
            shape((PASSES, 192), F32),
        ],
        (place, buffer, shift(buffer, "core", 1)),
        [pltpu.VMEM((2, ALL, 128), BF), pltpu.VMEM((D, 8), F32)],
    )
    return (layer_out, grad_stream, *results, grad_gains.T, grad_pass.T)


def solution(mesh):
    tokens = P("batch", "blk", None)
    in_specs = (tokens, tokens, P("batch"), P(), P(), P(), P(), P(), P())
    out_specs = (tokens, tokens) + (P("blk", None),) * 6
    return jax.shard_map(on_device, mesh=mesh, in_specs=in_specs, out_specs=out_specs, check_vma=False)
```

```python
import jax
import jax.numpy as jnp
from jax import lax
from jax.experimental import pallas as pl
from jax.experimental.pallas import tpu as pltpu
from jax.sharding import PartitionSpec as P

D = 768
HEADS = 12
HD = 64
FF = 3072
PASSES = 5
ROWS = 510
R = 512
EPS = 1e-05
NEG = -1e30
BF = jnp.bfloat16
F32 = jnp.float32
VM = pl.BlockSpec(memory_space=pltpu.VMEM)
SM = pl.BlockSpec(memory_space=pltpu.SMEM)
HB = pl.BlockSpec(memory_space=pl.ANY)
MIB = 1024 * 1024


def room(mib):
    return pltpu.CompilerParams(vmem_limit_bytes=mib * MIB)


def run(kernel, name, mib, outs, operands, scratch=(), scalars=1):
    return pl.pallas_call(
        kernel,
        in_specs=[SM] * scalars + [VM] * (len(operands) - scalars),
        out_specs=[VM] * len(outs),
        out_shape=outs,
        scratch_shapes=list(scratch),
        compiler_params=room(mib),
        name=name,
    )(*operands)


def shape(dims, kind=BF):
    return jax.ShapeDtypeStruct(dims, kind)


def kept(dims, kind=BF):
    return pltpu.HBM(dims, kind)


def dot(left, right):
    return jnp.dot(left, right, preferred_element_type=F32)


def dot_nt(left, right):
    return lax.dot_general(left, right, (((1,), (1,)), ((), ())), preferred_element_type=F32)


def normalize(values):
    mean = jnp.mean(values, axis=-1, keepdims=True)
    centred = values - mean
    inverse = lax.rsqrt(jnp.mean(centred * centred, axis=-1, keepdims=True) + EPS)
    return centred * inverse, inverse


def norm_back(grad, unit, inverse, gain):
    scaled = grad * gain
    first = jnp.mean(scaled, axis=-1, keepdims=True)
    second = jnp.mean(scaled * unit, axis=-1, keepdims=True)
    return inverse * (scaled - first - unit * second)


def pass_index(blk, count):
    row = lax.broadcasted_iota(jnp.int32, (R, 1), 0) + blk * ROWS
    turns = jnp.floor((row.astype(F32) + 0.5) / count.astype(F32)).astype(jnp.int32)
    return row - turns * count


def pieces_out(stage, outs, blk):
    for d, out in enumerate(outs):
        out[...] = stage[lax.rem(blk + d, 4)]


def project(normed, weights, stage, outs, blk):
    for part, weight in enumerate(weights):
        got = dot(normed, weight[...])
        if part == 0:
            got = got.astype(BF) * jnp.asarray(HD ** (-0.5), BF)
        turned = got.astype(BF).T
        for j in range(4):
            stage[j, 64 * part : 64 * part + 64, :] = turned[64 * j : 64 * j + 64]
    pieces_out(stage, outs, blk)


def project(normed, weights, stage):
    for part, weight in enumerate(weights):
        got = dot(normed, weight[...])
        if part == 0:
            got = got.astype(BF) * jnp.asarray(HD ** (-0.5), BF)
        flipped = got.astype(BF).T
        for j in range(4):
            stage[j, 64 * part : 64 * part + 64, :] = flipped[64 * j : 64 * j + 64]


def first_kernel(blk_ref, count_ref, stream, embed, gains, wq, wk, wv, hidden, turned, p0, p1, p2, p3, normed, stage):
    blk = blk_ref[0]
    hidden[R - 8 : R, :] = jnp.zeros((8, D), F32)
    hidden[0:ROWS, :] = stream[0].astype(F32)
    which = pass_index(blk, count_ref[0])
    added = embed[0:1, :]
    for r in range(1, PASSES):
        added = jnp.where(which == r, embed[r : r + 1, :], added)
    values = hidden[...] + added
    hidden[...] = values
    unit, _ = normalize(values)
    row = lax.broadcasted_iota(jnp.int32, (R, 1), 0)
    low = jnp.where(row < ROWS, unit * gains[0:1, :], 0.0).astype(BF)
    normed[...] = low
    project(low, (wq, wk, wv), stage)
    for d, out in enumerate((p0, p1, p2, p3)):
        out[...] = stage[lax.rem(blk + d, 4)]
    turned[...] = low.T


def second_kernel(blk_ref, normed, wq1, wk1, wv1, wq2, wk2, wv2, p0, p1, p2, p3, stage):
    blk = blk_ref[0]
    for n, weights in enumerate(((wq1, wk1, wv1), (wq2, wk2, wv2))):
        project(normed[...], weights, stage.at[n])
        for d, out in enumerate((p0, p1, p2, p3)):
            out[192 * n : 192 * n + 192, :] = stage[n, lax.rem(blk + d, 4)]


def load_heads(blk, at, parts, q_rows, k_rows, v_rows, k_cols):
    for d in range(4):
        s = lax.rem(blk + 4 - d, 4)
        piece = parts[d]
        q_rows[s, 0:64, :] = piece[at : at + 64, :]
        k_rows[s, 0:64, :] = piece[at + 64 : at + 128, :]
        v_rows[s] = piece[at + 128 : at + 192, :]
    row = lax.broadcasted_iota(jnp.int32, (64, R), 0)
    col = lax.broadcasted_iota(jnp.int32, (64, R), 1)
    one = jnp.where(row == 0, 1.0, 0.0).astype(BF)
    off = jnp.where((row == 0) & (col >= ROWS), NEG, 0.0).astype(BF)
    for s in range(4):
        q_rows[s, 64:128, :] = one
        k_rows[s, 64:128, :] = off
    for s in range(4):
        k_cols[s] = k_rows[s].T


def causal():
    key = lax.broadcasted_iota(jnp.int32, (R, R), 0)
    query = lax.broadcasted_iota(jnp.int32, (R, R), 1)
    return key <= query


def attend_head(blk, n, parts, attended, spread, q_rows, k_rows, v_rows, k_cols, scores, stage):
    load_heads(blk, 192 * n, parts, q_rows, k_rows, v_rows, k_cols)
    for i in range(4):
        top = None
        for j in range(i + 1):
            got = dot(k_cols[j], q_rows[i])
            if i == j:
                got = jnp.where(causal(), got, NEG)
            scores[j] = got
            best = jnp.max(got, axis=0, keepdims=True)
            top = best if top is None else jnp.maximum(top, best)
        total = jnp.zeros((1, R), F32)
        summed = jnp.zeros((HD, R), F32)
        for j in range(i + 1):
            raised = jnp.exp(scores[j] - top)
            total = total + jnp.sum(raised, axis=0, keepdims=True)
            summed = summed + dot(v_rows[j], raised.astype(BF))
        result = summed / total
        attended[n, i] = result
        spread[n, i] = top + jnp.log(total)
        stage[i] = result.astype(BF)


def attend_kernel(count, blk_ref, r0, r1, r2, r3, *rest):
    earlier, rest = (rest[:4], rest[4:]) if count == 2 else ((), rest)
    p0, p1, p2, p3, attended, spread, *scratch = rest
    blk = blk_ref[0]
    for n in range(count):
        stage = scratch[-1].at[n]
        attend_head(blk, n, (r0, r1, r2, r3), attended, spread, *(ref.at[n] for ref in scratch))
        for d, out in enumerate((p0, p1, p2, p3)):
            at = 64 * (n + 1) if count == 2 else 0
            out[at : at + 64, :] = stage[lax.rem(blk + d, 4)]
    for d, value in enumerate(earlier):
        (p0, p1, p2, p3)[d][0:64, :] = value[...]


def attend_back_head(blk, n, at, parts, back, attended, spread, outs, scratch):
    q_rows, k_rows, v_rows, k_cols, q_cols, v_cols, o_rows, o_cols, delta, dq = scratch
    load_heads(blk, at, parts, q_rows, k_rows, v_rows, k_cols)
    for d, piece in enumerate(back):
        o_rows[lax.rem(blk + 4 - d, 4)] = piece
    for s in range(4):
        q_cols[s] = q_rows[s].T
        v_cols[s] = v_rows[s].T
        o_cols[s] = o_rows[s].T
        delta[s] = jnp.sum(o_rows[s].astype(F32) * attended[n, s], axis=0, keepdims=True)
        dq[s] = jnp.zeros((HD, R), F32)
    for j in range(4):
        dk = jnp.zeros((R, 2 * HD), F32)
        dv = jnp.zeros((R, HD), F32)
        for i in range(j, 4):
            got = dot(k_cols[j], q_rows[i])
            if i == j:
                got = jnp.where(causal(), got, NEG)
            probs = jnp.exp(got - spread[n, i])
            d_probs = dot(v_cols[j], o_rows[i])
            d_scores = (probs * (d_probs - delta[i])).astype(BF)
            dv = dv + dot(probs.astype(BF), o_cols[i])
            dk = dk + dot(d_scores, q_cols[i])
            dq[i] = dq[i] + dot(k_rows[j, 0:64, :], d_scores)
        outs[j, 0:64, :] = (dq[j] * HD ** (-0.5)).astype(BF)
        outs[j, 64:128, :] = dk[:, 0:64].astype(BF).T
        outs[j, 128:192, :] = dv.astype(BF).T


def attend_back_kernel(first, blk_ref, *refs):
    blk = blk_ref[0]
    if first:
        early, late, back, rest = refs[0:4], refs[4:8], refs[8:12], refs[12:]
        (attended, spread, attended_late, spread_late), rest = rest[0:4], rest[4:]
        sources = ((early, attended, spread, 0, 0), (late, attended_late, spread_late, 0, 0))
    else:
        late, back, rest = refs[0:4], refs[4:8], refs[8:]
        (attended_late, spread_late), rest = rest[0:2], rest[2:]
        sources = ((late, attended_late, spread_late, 1, 192),)
    pieces, outs, scratch = rest[0:4], rest[4], rest[5:]
    for h, (parts, attended, spread, n, at) in enumerate(sources):
        grads = [piece[64 * h : 64 * h + 64, :] for piece in back]
        attend_back_head(blk, n, at, parts, grads, attended, spread, outs.at[h], [ref.at[h] for ref in scratch])
        for d, out in enumerate(pieces):
            out[192 * h : 192 * h + 192, :] = outs[h, lax.rem(blk + d, 4)]


def units(piece):
    for n in range(7):
        u = 7 * piece + n
        if u < 48:
            yield 16 * n, (16 * (u // 4), 2 * (u % 4)), (16 * (u // 4), 2 * (u % 4) + 1)
        elif u < 54:
            yield 16 * n, (32 * (u - 48), 8), (32 * (u - 48) + 16, 8)


def head_grad_kernel(place_ref, t0, t1, t2, t3, e01, e2, keep, send, sides, made, pieces):
    blk, core = place_ref[0], place_ref[3]
    total = jnp.zeros((D, 640), F32)
    for d, piece in enumerate((t0, t1, t2, t3)):
        s = lax.rem(blk + 4 - d, 4)
        for g, side in enumerate((e01.at[0], e01.at[1], e2.at[0])):
            sides[d, 192 * g : 192 * g + 192, :] = side[s]
        sides[d, 576:640, :] = jnp.zeros((64, R), BF)
        total = total + dot_nt(piece[...], sides[d])
    made[...] = total
    pieces[...] = jnp.zeros((8, 4, GROUP, 128), BF)
    for k in range(8):
        for at, (row, left), (row_right, right) in units(k):
            for i in range(4):
                r = 192 * i + row
                if right == left:
                    halves = (made[r : r + 16, 512:576], made[r + 16 : r + 32, 512:576])
                    block = jnp.concatenate(halves, axis=1)
                else:
                    block = made[r : r + 16, 64 * left : 64 * left + 128]
                pieces[k, i, at : at + 16, :] = block.astype(BF)
    for q in range(4):
        keep[q] = pieces[4 * core + q]
        send[q] = pieces[4 * (1 - core) + q]


def gelu_both(value):
    c = (2.0 / jnp.pi) ** 0.5
    square = value * value
    t = jnp.tanh(c * value * (1.0 + 0.044715 * square))
    cdf = 0.5 * (1.0 + t)
    slope = cdf + (0.5 * c) * value * (1.0 - t * t) * (1.0 + 3.0 * 0.044715 * square)
    return value * cdf, slope


CHUNK = 768


def active_grad_kernel(place_ref, cot, w_down, out, dy, pad):
    @pl.when(pl.program_id(0) == 0)
    def _():
        pad[R - 8 : R, :] = jnp.zeros((8, D), F32)
        pad[0:ROWS, :] = cot[0].astype(F32)
        dy[...] = pad[...].astype(BF)

    out[...] = dot_nt(dy[...], w_down[...])


def up_cut(values, store):
    for z in range(4):
        for yy in range(4):
            store(yy, z, values[192 * z + 48 * yy : 192 * z + 48 * yy + 48, :])


def down_cut(values, store):
    for yy in range(4):
        for xx in range(4):
            r, col = 48 * (2 * yy + xx // 2), 384 * (xx % 2)
            store(yy, xx, values[r : r + 48, col : col + 384])


def out_cut(values, out):
    for i in range(4):
        for n in range(16):
            rows = values[192 * i + 16 * n : 192 * i + 16 * n + 16, :] if n < 12 else jnp.zeros((16, 384), BF)
            out[n // 4, n % 4, i, 48:64] = rows


def put_block(out, at, rows):
    out[at] = rows.astype(BF)


def ff_kernel(
    blk_ref, r0, r1, r2, r3, hidden, cot, gains, w_out, w_up, d_active,
    active, d_up, second, middle, o_turned, d_branch, d_middle, p0, p1, p2, p3, a_out, b_out, gain_term,
    dy, back, stage, second_turned,
):
    step = pl.program_id(0)
    core = blk_ref[3]

    @pl.when(step == 0)
    def _():
        blk = blk_ref[0]
        for d, piece in enumerate((r0, r1, r2, r3)):
            s = lax.rem(blk + 4 - d, 4)
            for g in range(3):
                stage[4 * g + s] = piece[64 * g : 64 * g + 64, :]
        o_rows = stage[...].reshape(D, R)
        o_turned[...] = o_rows
        values = hidden[...] + dot(o_rows.T, w_out[...])
        middle[...] = values
        unit, _ = normalize(values)
        second[...] = (unit * gains[1:2, :]).astype(BF)
        back[R - 8 : R, :] = jnp.zeros((8, D), F32)
        back[0:ROWS, :] = cot[0].astype(F32)
        dy[...] = back[...].astype(BF)
        back[...] = jnp.zeros((R, D), F32)
        second_turned[...] = second[...].T

    upward = dot(second[...], w_up[...])
    act, slope = gelu_both(upward)
    act = act.astype(BF)
    active[...] = act
    d_upward = (d_active[...] * slope).astype(BF)
    d_up[...] = d_upward
    back[...] += dot_nt(d_upward, w_up[...])

    first = core == 0
    other_up = jnp.where(first, d_upward[:, 384:768], d_upward[:, 0:384])
    other_act = jnp.where(first, act[:, 384:768], act[:, 0:384])
    up_cut(dot(second_turned[...], other_up), lambda yy, z, rows: put_block(a_out, (yy, step, z), rows))
    down_cut(dot(other_act.T, dy[...]), lambda yy, xx, rows: put_block(b_out, (yy, xx, step, slice(0, 48)), rows))

    @pl.when(step == FF // CHUNK - 1)
    def _():
        blk = blk_ref[0]
        unit, inverse = normalize(middle[...])
        grad = back[...]
        gain_term[...] = jnp.sum(grad * unit, axis=0, keepdims=True)
        total = dy[...].astype(F32) + norm_back(grad, unit, inverse, gains[1:2, :])
        d_middle[...] = total
        low = total.astype(BF)
        d_branch[...] = low
        stage[...] = dot_nt(w_out[...], low).astype(BF).reshape(HEADS, HD, R)
        out_cut(dot(o_turned[...], jnp.where(core == 0, low[:, 384:768], low[:, 0:384])).astype(BF), b_out)
        for d, out in enumerate((p0, p1, p2, p3)):
            j = lax.rem(blk + d, 4)
            for g in range(3):
                out[64 * g : 64 * g + 64, :] = stage[4 * g + j]


def ff_grad_kernel(place_ref, active, d_up, second, cot, o_turned, d_branch, a_out, b_out, dy, second_turned, pad):
    step = pl.program_id(0)

    @pl.when(step == 0)
    def _():
        pad[R - 8 : R, :] = jnp.zeros((8, D), F32)
        pad[0:ROWS, :] = cot[0].astype(F32)
        dy[...] = pad[...].astype(BF)
        second_turned[...] = second[...].T
        out_cut(dot(o_turned[...], d_branch[...]).astype(BF), b_out)

    up_cut(dot(second_turned[...], d_up[...]), lambda yy, z, rows: put_block(a_out, (yy, step, z), rows))
    down_cut(dot(active[...].T, dy[...]), lambda yy, xx, rows: put_block(b_out, (yy, xx, step, slice(0, 48)), rows))


def core_sum_kernel(place_ref, a_mine, b_mine, a_got, b_got, a0, a1, a2, a3, b0, b1, b2, b3):
    x, y = place_ref[1], place_ref[2]
    for d, (a_out, b_out) in enumerate(((a0, b0), (a1, b1), (a2, b2), (a3, b3))):
        xx, yy = lax.rem(x + d, 4), lax.rem(y + d, 4)
        for n in range(4):
            a_out[n] = (a_mine[n, xx].astype(F32) + a_got[n, xx].astype(F32)).astype(BF)
            b_out[n] = (b_mine[yy, n].astype(F32) + b_got[yy, n].astype(F32)).astype(BF)


def total_of(parts):
    return (parts[0].astype(F32) + parts[2].astype(F32)) + (parts[1].astype(F32) + parts[3].astype(F32))


TINY = 96
GROUP = 112
PART_A = 144
PART_B = 192


def put(buffer, at, block):
    rows, lanes = block.shape
    for t in range(lanes // 128):
        buffer[at + rows * t : at + rows * t + rows, :] = block[:, 128 * t : 128 * t + 128]


def put_small(buffer, at, value):
    high = value.astype(BF)
    low = (value - high.astype(F32)).astype(BF)
    put(buffer, at, jnp.concatenate([high, low], axis=0))


def get_small(buffer, at):
    parts = []
    for t in range(6):
        part = buffer[at + 16 * t : at + 16 * t + 16, :].astype(F32)
        parts.append(part[0:8] + part[8:16])
    return jnp.concatenate(parts, axis=1)


def take(buffer, at, rows):
    return jnp.concatenate([buffer[at + rows * t : at + rows * t + rows, :] for t in range(3)], axis=1)


def cut_kernel(place_ref, a0, a1, a2, a3, b0, b1, b2, b3, keep, got, y0, y1, y2, y3, x0, x1, x2, x3):
    x, y = place_ref[1], place_ref[2]
    for d, (y_out, x_out) in enumerate(((y0, x0), (y1, x1), (y2, x2), (y3, x3))):
        yy, xx = lax.rem(y + d, 4), lax.rem(x + d, 4)
        a_sum = total_of([r[yy] for r in (a0, a1, a2, a3)]).astype(BF)
        heads = (keep[yy].astype(F32) + got[yy].astype(F32)).astype(BF)
        for i in range(4):
            put(y_out, PART_A * i, a_sum[i])
            y_out[4 * PART_A + GROUP * i : 4 * PART_A + GROUP * i + GROUP, :] = heads[i]
        x_out[...] = total_of([r[xx] for r in (b0, b1, b2, b3)]).astype(BF)


def block_kernel(place_ref, y0, y1, y2, y3, x0, x1, x2, x3, small, o0, o1, o2, o3):
    z = place_ref[0]
    for d, out in enumerate((o0, o1, o2, o3)):
        i = lax.rem(z + d, 4)
        start = pl.multiple_of(PART_A * i, 16)
        out[0:PART_A, :] = total_of([r[pl.ds(start, PART_A), :] for r in (y0, y1, y2, y3)]).astype(BF)
        put(out, PART_A, total_of([r[i] for r in (x0, x1, x2, x3)]).astype(BF))
        start = pl.multiple_of(4 * PART_A + GROUP * i, 16)
        at = PART_A + PART_B
        out[at : at + GROUP, :] = total_of([r[pl.ds(start, GROUP), :] for r in (y0, y1, y2, y3)]).astype(BF)
        put_small(out, at + GROUP, small[...])


def own_kernel(place_ref, z0, z1, z2, z3, x_out, y_out):
    parts = (z0, z1, z2, z3)
    at = PART_A + PART_B
    for d, r in enumerate(parts):
        x_out[GROUP * d : GROUP * d + GROUP, :] = r[at : at + GROUP, :]
    put_small(x_out, 4 * GROUP, total_of([get_small(r, at + GROUP) for r in parts]))
    x_out[4 * GROUP + TINY : 4 * GROUP + TINY + PART_A, :] = total_of([r[0:PART_A, :] for r in parts]).astype(BF)
    y_out[...] = total_of([r[PART_A : PART_A + PART_B, :] for r in parts]).astype(BF)


def row_kernel(place_ref, x0, x1, x2, x3, y0, y1, y2, y3, y_out, x_out):
    parts = (x0, x1, x2, x3)
    y_out[0 : 4 * GROUP, :] = total_of([r[0 : 4 * GROUP, :] for r in parts]).astype(BF)
    put_small(y_out, 4 * GROUP, total_of([get_small(r, 4 * GROUP) for r in parts]))
    at = 4 * GROUP + TINY
    for d, (a, b) in enumerate(zip(parts, (y0, y1, y2, y3))):
        y_out[at + PART_A * d : at + PART_A * d + PART_A, :] = a[at : at + PART_A, :]
        x_out[PART_B * d : PART_B * d + PART_B, :] = b[...]


ALL_TINY = 16 * GROUP
ALL_A = ALL_TINY + TINY
ALL_B = ALL_A + 16 * PART_A
ALL = ALL_B + 16 * PART_B


def stack_kernel(place_ref, y0, y1, y2, y3, x0, x1, x2, x3, out):
    parts = (y0, y1, y2, y3)
    put_small(out, ALL_TINY, total_of([get_small(r, 4 * GROUP) for r in parts]))
    at = 4 * GROUP + TINY
    for d, (r, b) in enumerate(zip(parts, (x0, x1, x2, x3))):
        out[4 * GROUP * d : 4 * GROUP * d + 4 * GROUP, :] = r[0 : 4 * GROUP, :]
        out[ALL_A + 4 * PART_A * d : ALL_A + 4 * PART_A * d + 4 * PART_A, :] = r[at : at + 4 * PART_A, :]
        out[ALL_B + 4 * PART_B * d : ALL_B + 4 * PART_B * d + 4 * PART_B, :] = b[...]


def finish_kernel(place_ref, mine, other, grad_qkv, grad_out, grad_up, grad_down, gains, passes, pair, turned):
    z, x, y, core = place_ref[0], place_ref[1], place_ref[2], place_ref[3]
    pair[core] = mine[...]
    pair[1 - core] = other[...]

    def rows(c, at, count):
        return pair[c, pl.ds(pl.multiple_of(at, 16), count), :].astype(F32)

    for c in range(2):
        for xx in range(4):
            dx = lax.rem(x + 4 - xx, 4)
            for yy in range(4):
                dy = lax.rem(y + 4 - yy, 4)
                a = rows(c, ALL_A + 4 * PART_A * dy + PART_A * dx, PART_A)
                b = rows(c, ALL_B + 4 * PART_B * dx + PART_B * dy, PART_B)
                r = 384 * c + 48 * (2 * yy + xx // 2)
                for t in range(3):
                    col = 384 * (2 * xx + c) + 128 * t
                    grad_up[48 * yy : 48 * yy + 48, col : col + 128] = a[48 * t : 48 * t + 48]
                    col = 384 * (xx % 2) + 128 * t
                    grad_down[r : r + 48, col : col + 128] = b[64 * t : 64 * t + 48]
                    if yy < 3:
                        n, col = 16 * (4 * yy + xx), 384 * c + 128 * t
                        grad_out[n : n + 16, col : col + 128] = b[64 * t + 48 : 64 * t + 64]
        for yy in range(4):
            dy = lax.rem(y + 4 - yy, 4)
            for j in range(4):
                dz = lax.rem(z + 4 - j, 4)
                piece = rows(c, 4 * GROUP * dy + GROUP * dz, GROUP)
                for at, *halves in units(4 * c + yy):
                    for side, (r, n) in enumerate(halves):
                        col = D * (n % 3) + 64 * (4 * (n // 3) + j)
                        grad_qkv[r : r + 16, col : col + 64] = piece[at : at + 16, 64 * side : 64 * side + 64]
    small = get_small(mine, ALL_TINY) + get_small(other, ALL_TINY)
    turned[...] = small.T
    part = turned[pl.ds(pl.multiple_of(192 * z, 8), 192), :]
    part = part.T
    gains[...] = part[0:2, :]
    passes[...] = part[2:7, :]


def layer_out_kernel(place_ref, middle, active, w_down, out, total):
    step = pl.program_id(0)

    @pl.when(step == 0)
    def _():
        total[...] = middle[...]

    total[...] += dot(active[...], w_down[...])

    @pl.when(step == FF // CHUNK - 1)
    def _():
        out[0] = total[0:ROWS, :].astype(BF)


def last_kernel(
    blk_ref, count_ref, a0, a1, a2, a3, c0, c1, c2, c3, hidden, d_middle, gain_term, gains, w_qkv, grad_stream, small, stage
):
    blk = blk_ref[0]
    for d, (early, late) in enumerate(((a0, c0), (a1, c1), (a2, c2), (a3, c3))):
        s = lax.rem(blk + 4 - d, 4)
        for n in range(9):
            piece = early[64 * n : 64 * n + 64, :] if n < 6 else late[64 * n - 384 : 64 * n - 320, :]
            stage[12 * (n % 3) + 4 * (n // 3) + s] = piece
    grad = dot(w_qkv[...], stage[...].reshape(3 * D, R)).T
    unit, inverse = normalize(hidden[...])
    total = d_middle[...] + norm_back(grad, unit, inverse, gains[0:1, :])
    grad_stream[0] = total[0:ROWS, :]
    row = lax.broadcasted_iota(jnp.int32, (R, 1), 0)
    which = jnp.where(row < ROWS, pass_index(blk, count_ref[0]), -1)
    small[0:1, :] = jnp.sum(grad * unit, axis=0, keepdims=True)
    small[1:2, :] = gain_term[...]
    for r in range(PASSES):
        small[2 + r : 3 + r, :] = jnp.sum(jnp.where(which == r, total, 0.0), axis=0, keepdims=True)
    small[7:8, :] = jnp.zeros((1, D), F32)


def shift(values, axis, d):
    if axis == "z":
        return lax.ppermute(values, "blk", [(i, (i + d) % 4) for i in range(4)])
    pairs = []
    for b in range(32):
        y, x, core = b // 8, (b // 2) % 4, b % 2
        if axis == "y":
            y = (y + d) % 4
        elif axis == "x":
            x = (x + d) % 4
        else:
            core = (core + d) % 2
        pairs.append((b, 8 * y + 2 * x + core))
    return lax.ppermute(values, "batch", pairs)


def spread_pieces(pieces, axis):
    two, three, one = (shift(pieces[d], axis, d) for d in (2, 3, 1))
    return (pieces[0], one, two, three)


def all_of(value, axis):
    return spread_pieces((value,) * 4, axis)


def after(value, *others):
    return lax.optimization_barrier((value,) + others)[0]


def far(value):
    return pltpu.with_memory_space_constraint(value, pltpu.HBM)


def weight_spec(column):
    return pl.BlockSpec((D, 256), lambda *_, column=column: (0, column))


def on_device(stream, cotangent, passes, w_qkv, w_out, w_up, w_down, ln_gains, pass_embed):
    z = lax.axis_index("blk").astype(jnp.int32)
    batch = lax.axis_index("batch").astype(jnp.int32)
    place = jnp.stack([z, batch // 2 % 4, batch // 8, batch % 2])
    gains = ln_gains.T
    embed = pass_embed.T
    piece = shape((192, R))
    full = shape((R, D))

    def arrived(*values):
        nonlocal place
        place = lax.optimization_barrier((place,) + values)[0]

    def ordered(outs):
        nonlocal place
        *outs, first = outs
        place, first = lax.optimization_barrier((place, first))
        return (*outs, first)

    hidden, turned, *sent, normed = ordered(pl.pallas_call(
        first_kernel,
        grid=(1,),
        in_specs=[SM, SM, VM, VM, VM, weight_spec(0), weight_spec(3), weight_spec(6)],
        out_specs=[VM] * 7,
        out_shape=[kept((R, D), F32), kept((D, R)), kept((192, R)), piece, piece, piece, full],
        scratch_shapes=[pltpu.VMEM((4, 192, R), BF)],
        compiler_params=room(24),
        name="ln_qkv",
    )(place, passes, far(stream), far(embed), far(gains), *([far(w_qkv)] * 3)))
    early = spread_pieces(sent, "z")
    sent = ordered(pl.pallas_call(
        second_kernel,
        grid=(1,),
        in_specs=[SM, VM] + [weight_spec(c) for c in (1, 4, 7, 2, 5, 8)],
        out_specs=[VM] * 4,
        out_shape=[kept((384, R))] + [shape((384, R))] * 3,
        scratch_shapes=[pltpu.VMEM((2, 4, 192, R), BF)],
        compiler_params=room(24),
        name="qkv_rest",
    )(place, normed, *([far(w_qkv)] * 6)))
    late = [sent[0], shift(sent[1], "z", 1), sent[2], shift(sent[3], "z", 3)]

    attended, spreads, sent = [], [], []
    for count, parts in ((1, early), (2, late)):
        *sent, result, spread = ordered(run(
            lambda *refs, count=count: attend_kernel(count, *refs),
            "attend",
            24,
            [shape((192 if count == 2 else HD, R))] * 4 + [kept((count, 4, HD, R), F32), kept((count, 4, 1, R), F32)],
            (place, *parts, *sent),
            [
                pltpu.VMEM((count, 4, 128, R), BF),
                pltpu.VMEM((count, 4, 128, R), BF),
                pltpu.VMEM((count, 4, HD, R), BF),
                pltpu.VMEM((count, 4, R, 128), BF),
                pltpu.VMEM((count, 4, R, R), F32),
                pltpu.VMEM((count, 4, HD, R), BF),
            ],
        ))
        if count == 1:
            late[2] = shift(after(late[2], place), "z", 2)
            d_active = ordered((pl.pallas_call(
                active_grad_kernel,
                grid=(FF // CHUNK,),
                in_specs=[SM, VM, pl.BlockSpec((CHUNK, D), lambda f: (f, 0))],
                out_specs=pl.BlockSpec((R, CHUNK), lambda f: (0, f)),
                out_shape=kept((R, FF), F32),
                scratch_shapes=[pltpu.VMEM((R, D), BF), pltpu.VMEM((R, D), F32)],
                compiler_params=room(16),
                name="active_grad",
            )(place, far(cotangent), far(w_down)),))[0]
        attended += [result] * count
        spreads += [spread] * count
    heads = (early, late, late)
    back_o = spread_pieces(sent, "z")
    near = after(turned, *back_o)
    near = (shift(near, "z", 1), shift(near, "z", 3))

    active, d_up, second, middle, o_turned, d_branch, d_middle, *sent, a_other, b_other, gain_term = ordered(pl.pallas_call(
        ff_kernel,
        grid=(FF // CHUNK,),
        in_specs=[SM] + [VM] * 4 + [VM, VM, VM, VM]
        + [pl.BlockSpec((D, CHUNK), lambda f: (0, f)), pl.BlockSpec((R, CHUNK), lambda f: (0, f))],
        out_specs=[pl.BlockSpec((R, CHUNK), lambda f: (0, f)), pl.BlockSpec((R, CHUNK), lambda f: (0, f))] + [VM] * 12,
        out_shape=[shape((R, FF)), shape((R, FF)), full, shape((R, D), F32), shape((D, R)), full, kept((R, D), F32)]
        + [kept((192, R))] + [piece] * 3 + [shape((4, 4, 4, 48, 384)), shape((4, 4, 4, 64, 384)), shape((1, D), F32)],
        scratch_shapes=[pltpu.VMEM((R, D), BF), pltpu.VMEM((R, D), F32), pltpu.VMEM((HEADS, HD, R), BF), pltpu.VMEM((D, R), BF)],
        compiler_params=room(36),
        name="ff",
    )(place, *back_o, hidden, cotangent, gains, w_out, far(w_up), far(d_active)))
    *sent, a_other, b_other = lax.optimization_barrier((*sent, a_other, b_other, *near))[:6]
    d_o = spread_pieces(sent, "z")

    got = (shift(a_other, "core", 1), shift(b_other, "core", 1))
    own = ordered(pl.pallas_call(
        ff_grad_kernel,
        grid_spec=pltpu.PrefetchScalarGridSpec(
            num_scalar_prefetch=1,
            grid=(4,),
            in_specs=[
                pl.BlockSpec((R, 384), lambda i, s: (0, 2 * i + s[3])),
                pl.BlockSpec((R, 384), lambda i, s: (0, 2 * i + s[3])),
                VM,
                VM,
                VM,
                pl.BlockSpec((R, 384), lambda i, s: (0, s[3])),
            ],
            out_specs=[VM] * 2,
            scratch_shapes=[pltpu.VMEM((R, D), BF), pltpu.VMEM((D, R), BF), pltpu.VMEM((R, D), F32)],
        ),
        out_shape=[shape((4, 4, 4, 48, 384)), shape((4, 4, 4, 64, 384))],
        compiler_params=room(24),
        name="ff_grad",
    )(place, active, d_up, second, far(cotangent), o_turned, d_branch))
    arrived(*d_o)
    distant = shift(after(turned, *d_o, place), "z", 2)
    sent = ordered(run(
        core_sum_kernel,
        "core_sum",
        24,
        [kept((4, 4, 48, 384))] + [shape((4, 4, 48, 384))] * 3 + [kept((4, 4, 64, 384))] + [shape((4, 4, 64, 384))] * 3,
        (place, *own, *got),
    ))
    a_sent, b_sent = sent[0:4], sent[4:8]
    a_parts = [a_sent[0], shift(a_sent[1], "x", 1), None, shift(a_sent[3], "x", 3)]
    b_parts = [b_sent[0], shift(b_sent[1], "y", 1), None, shift(b_sent[3], "y", 3)]

    def attend_back(first, operands):
        count = 2 if first else 1
        group = pl.BlockSpec((64 * count, R), lambda _: (0 if first else 2, 0))
        return ordered(pl.pallas_call(
            lambda *refs: attend_back_kernel(first, *refs),
            grid=(1,),
            in_specs=[SM] + [VM] * (4 * count) + [group] * 4 + [VM] * (2 * count),
            out_specs=[VM] * 5,
            out_shape=[kept((192 * count, R))] + [shape((192 * count, R))] * 3 + [kept((count, 4, 192, R))],
            scratch_shapes=[
                pltpu.VMEM((count, 4, 128, R), BF),
                pltpu.VMEM((count, 4, 128, R), BF),
                pltpu.VMEM((count, 4, HD, R), BF),
                pltpu.VMEM((count, 4, R, 128), BF),
                pltpu.VMEM((count, 4, R, 128), BF),
                pltpu.VMEM((count, 4, R, HD), BF),
                pltpu.VMEM((count, 4, HD, R), BF),
                pltpu.VMEM((count, 4, R, HD), BF),
                pltpu.VMEM((count, 4, 1, R), F32),
                pltpu.VMEM((count, 4, HD, R), F32),
            ],
            compiler_params=room(32 if first else 24),
            name="attend_back",
        )(place, *(far(t) for t in operands)))

    *sent, made_first = attend_back(True, (*early, *late, *d_o, attended[0], spreads[0], attended[1], spreads[1]))
    first_pieces = spread_pieces(sent, "z")
    a_parts[2] = shift(after(a_sent[2], place), "x", 2)
    b_parts[2] = shift(after(b_sent[2], place), "y", 2)
    arrived(a_parts[1], a_parts[3], b_parts[1], b_parts[3], distant)
    *sent, made_last = attend_back(False, (*late, *d_o, attended[2], spreads[2]))
    keep, send = ordered(run(
        head_grad_kernel,
        "head_grad",
        32,
        [shape((4, 4, GROUP, 128))] * 2,
        (place, far(turned), far(near[0]), far(distant), far(near[1]), far(made_first), far(made_last)),
        [pltpu.VMEM((4, 640, R), BF), pltpu.VMEM((D, 640), F32), pltpu.VMEM((8, 4, GROUP, 128), BF)],
    ))
    arrived(*first_pieces, a_parts[2], b_parts[2])
    *sent, send = lax.optimization_barrier((*sent, send, *first_pieces, a_parts[2], b_parts[2]))[:5]
    last_pieces = spread_pieces(sent, "z")
    got = shift(send, "core", 1)

    sent = ordered(run(
        cut_kernel,
        "sum_first",
        24,
        [shape((4 * PART_A + 4 * GROUP, 128))] * 4 + [shape((4, 64, 384))] * 4,
        (place, *a_parts, *b_parts, keep, got),
    ))
    y_parts, x_parts = spread_pieces(sent[0:4], "y"), spread_pieces(sent[4:8], "x")
    grad_stream, small = ordered(pl.pallas_call(
        last_kernel,
        grid=(1,),
        in_specs=[SM, SM] + [VM] * 13,
        out_specs=[VM, VM],
        out_shape=[kept((1, ROWS, D), F32), shape((8, D), F32)],
        scratch_shapes=[pltpu.VMEM((36, HD, R), BF)],
        compiler_params=room(24),
        name="ln_back",
    )(place, passes, *first_pieces, *last_pieces, far(hidden), far(d_middle), gain_term, gains, far(w_qkv)))
    sent = ordered(run(
        block_kernel,
        "sum_second",
        16,
        [shape((PART_A + PART_B + GROUP + TINY, 128))] * 4,
        (place, *y_parts, *x_parts, small),
    ))
    z_parts = spread_pieces(sent, "z")
    layer_out = ordered((pl.pallas_call(
        layer_out_kernel,
        grid=(FF // CHUNK,),
        in_specs=[SM, VM, pl.BlockSpec((R, CHUNK), lambda f: (0, f)), pl.BlockSpec((CHUNK, D), lambda f: (f, 0))],
        out_specs=VM,
        out_shape=kept((1, ROWS, D)),
        scratch_shapes=[pltpu.VMEM((R, D), F32)],
        compiler_params=room(16),
        name="layer_out",
    )(place, far(middle), far(active), far(w_down)),))[0]
    buffers = ordered(run(
        own_kernel,
        "sum_blocks",
        16,
        [shape((4 * GROUP + TINY + PART_A, 128)), shape((PART_B, 128))],
        (place, *z_parts),
    ))
    buffers = ordered(run(
        row_kernel,
        "stack_rows",
        16,
        [shape((4 * GROUP + TINY + 4 * PART_A, 128)), shape((4 * PART_B, 128))],
        (place, *all_of(buffers[0], "x"), *all_of(buffers[1], "y")),
    ))
    buffer = ordered(run(
        stack_kernel,
        "stack",
        16,
        [shape((ALL, 128))],
        (place, *all_of(buffers[0], "y"), *all_of(buffers[1], "x")),
    ))[0]
    *results, grad_gains, grad_pass = run(
        finish_kernel,
        "finish",
        32,
        [
            kept((192, 3 * D), F32),
            kept((192, D), F32),
            kept((192, FF), F32),
            kept((D, D), F32),
            shape((2, 192), F32),
            shape((PASSES, 192), F32),
        ],
        (place, buffer, shift(buffer, "core", 1)),
        [pltpu.VMEM((2, ALL, 128), BF), pltpu.VMEM((D, 8), F32)],
    )
    return (layer_out, grad_stream, *results, grad_gains.T, grad_pass.T)


def solution(mesh):
    tokens = P("batch", "blk", None)
    in_specs = (tokens, tokens, P("batch"), P(), P(), P(), P(), P(), P())
    out_specs = (tokens, tokens) + (P("blk", None),) * 6
    return jax.shard_map(on_device, mesh=mesh, in_specs=in_specs, out_specs=out_specs, check_vma=False)
```

```python
import jax
import jax.numpy as jnp
from jax import lax
from jax.experimental import pallas as pl
from jax.experimental.pallas import tpu as pltpu
from jax.sharding import PartitionSpec as P

D = 768
HEADS = 12
HD = 64
FF = 3072
PASSES = 5
ROWS = 510
R = 512
EPS = 1e-05
NEG = -1e30
BF = jnp.bfloat16
F32 = jnp.float32
VM = pl.BlockSpec(memory_space=pltpu.VMEM)
SM = pl.BlockSpec(memory_space=pltpu.SMEM)
HB = pl.BlockSpec(memory_space=pl.ANY)
MIB = 1024 * 1024


def room(mib):
    return pltpu.CompilerParams(vmem_limit_bytes=mib * MIB)


def run(kernel, name, mib, outs, operands, scratch=(), scalars=1):
    return pl.pallas_call(
        kernel,
        in_specs=[SM] * scalars + [VM] * (len(operands) - scalars),
        out_specs=[VM] * len(outs),
        out_shape=outs,
        scratch_shapes=list(scratch),
        compiler_params=room(mib),
        name=name,
    )(*operands)


def shape(dims, kind=BF):
    return jax.ShapeDtypeStruct(dims, kind)


def kept(dims, kind=BF):
    return pltpu.HBM(dims, kind)


def dot(left, right):
    return jnp.dot(left, right, preferred_element_type=F32)


def dot_nt(left, right):
    return lax.dot_general(left, right, (((1,), (1,)), ((), ())), preferred_element_type=F32)


def normalize(values):
    mean = jnp.mean(values, axis=-1, keepdims=True)
    centred = values - mean
    inverse = lax.rsqrt(jnp.mean(centred * centred, axis=-1, keepdims=True) + EPS)
    return centred * inverse, inverse


def norm_back(grad, unit, inverse, gain):
    scaled = grad * gain
    first = jnp.mean(scaled, axis=-1, keepdims=True)
    second = jnp.mean(scaled * unit, axis=-1, keepdims=True)
    return inverse * (scaled - first - unit * second)


def pass_index(blk, count):
    row = lax.broadcasted_iota(jnp.int32, (R, 1), 0) + blk * ROWS
    turns = jnp.floor((row.astype(F32) + 0.5) / count.astype(F32)).astype(jnp.int32)
    return row - turns * count


def pieces_out(stage, outs, blk):
    for d, out in enumerate(outs):
        out[...] = stage[lax.rem(blk + d, 4)]


def project(normed, weights, stage, outs, blk):
    for part, weight in enumerate(weights):
        got = dot(normed, weight[...])
        if part == 0:
            got = got.astype(BF) * jnp.asarray(HD ** (-0.5), BF)
        turned = got.astype(BF).T
        for j in range(4):
            stage[j, 64 * part : 64 * part + 64, :] = turned[64 * j : 64 * j + 64]
    pieces_out(stage, outs, blk)


def project(normed, weights, stage):
    for part, weight in enumerate(weights):
        got = dot(normed, weight[...])
        if part == 0:
            got = got.astype(BF) * jnp.asarray(HD ** (-0.5), BF)
        flipped = got.astype(BF).T
        for j in range(4):
            stage[j, 64 * part : 64 * part + 64, :] = flipped[64 * j : 64 * j + 64]


def first_kernel(blk_ref, count_ref, stream, embed, gains, wq, wk, wv, hidden, turned, p0, p1, p2, p3, normed, stage):
    blk = blk_ref[0]
    hidden[R - 8 : R, :] = jnp.zeros((8, D), F32)
    hidden[0:ROWS, :] = stream[0].astype(F32)
    which = pass_index(blk, count_ref[0])
    added = embed[0:1, :]
    for r in range(1, PASSES):
        added = jnp.where(which == r, embed[r : r + 1, :], added)
    values = hidden[...] + added
    hidden[...] = values
    unit, _ = normalize(values)
    row = lax.broadcasted_iota(jnp.int32, (R, 1), 0)
    low = jnp.where(row < ROWS, unit * gains[0:1, :], 0.0).astype(BF)
    normed[...] = low
    project(low, (wq, wk, wv), stage)
    for d, out in enumerate((p0, p1, p2, p3)):
        out[...] = stage[lax.rem(blk + d, 4)]
    turned[...] = low.T


def second_kernel(blk_ref, normed, wq1, wk1, wv1, wq2, wk2, wv2, p0, p1, p2, p3, q0, q1, q2, q3, stage):
    blk = blk_ref[0]
    for n, (weights, outs) in enumerate((((wq1, wk1, wv1), (p0, p1, p2, p3)), ((wq2, wk2, wv2), (q0, q1, q2, q3)))):
        project(normed[...], weights, stage.at[n])
        for d, out in enumerate(outs):
            out[...] = stage[n, lax.rem(blk + d, 4)]


def load_heads(blk, parts, q_rows, k_rows, v_rows, k_cols):
    for d in range(4):
        s = lax.rem(blk + 4 - d, 4)
        piece = parts[d]
        q_rows[s, 0:64, :] = piece[0:64, :]
        k_rows[s, 0:64, :] = piece[64:128, :]
        v_rows[s] = piece[128:192, :]
    row = lax.broadcasted_iota(jnp.int32, (64, R), 0)
    col = lax.broadcasted_iota(jnp.int32, (64, R), 1)
    one = jnp.where(row == 0, 1.0, 0.0).astype(BF)
    off = jnp.where((row == 0) & (col >= ROWS), NEG, 0.0).astype(BF)
    for s in range(4):
        q_rows[s, 64:128, :] = one
        k_rows[s, 64:128, :] = off
    for s in range(4):
        k_cols[s] = k_rows[s].T


def causal():
    key = lax.broadcasted_iota(jnp.int32, (R, R), 0)
    query = lax.broadcasted_iota(jnp.int32, (R, R), 1)
    return key <= query


def attend_kernel(last, blk_ref, r0, r1, r2, r3, *rest):
    earlier, rest = (rest[:8], rest[8:]) if last else ((), rest)
    p0, p1, p2, p3, attended, spread, q_rows, k_rows, v_rows, k_cols, scores, stage = rest
    blk = blk_ref[0]
    load_heads(blk, (r0, r1, r2, r3), q_rows, k_rows, v_rows, k_cols)
    for i in range(4):
        top = None
        for j in range(i + 1):
            got = dot(k_cols[j], q_rows[i])
            if i == j:
                got = jnp.where(causal(), got, NEG)
            scores[j] = got
            best = jnp.max(got, axis=0, keepdims=True)
            top = best if top is None else jnp.maximum(top, best)
        total = jnp.zeros((1, R), F32)
        summed = jnp.zeros((HD, R), F32)
        for j in range(i + 1):
            raised = jnp.exp(scores[j] - top)
            total = total + jnp.sum(raised, axis=0, keepdims=True)
            summed = summed + dot(v_rows[j], raised.astype(BF))
        result = summed / total
        attended[i] = result
        spread[i] = top + jnp.log(total)
        stage[i] = result.astype(BF)
    at = 128 if last else 0
    for d, out in enumerate((p0, p1, p2, p3)):
        out[at : at + 64, :] = stage[lax.rem(blk + d, 4)]
        if last:
            out[0:64, :] = earlier[d][...]
            out[64:128, :] = earlier[4 + d][...]


def attend_back_head(blk, parts, back, attended, spread, outs, scratch):
    q_rows, k_rows, v_rows, k_cols, q_cols, v_cols, o_rows, o_cols, delta, dq = scratch
    load_heads(blk, parts, q_rows, k_rows, v_rows, k_cols)
    for d, piece in enumerate(back):
        o_rows[lax.rem(blk + 4 - d, 4)] = piece
    for s in range(4):
        q_cols[s] = q_rows[s].T
        v_cols[s] = v_rows[s].T
        o_cols[s] = o_rows[s].T
        delta[s] = jnp.sum(o_rows[s].astype(F32) * attended[s], axis=0, keepdims=True)
        dq[s] = jnp.zeros((HD, R), F32)
    for j in range(4):
        dk = jnp.zeros((R, 2 * HD), F32)
        dv = jnp.zeros((R, HD), F32)
        for i in range(j, 4):
            got = dot(k_cols[j], q_rows[i])
            if i == j:
                got = jnp.where(causal(), got, NEG)
            probs = jnp.exp(got - spread[i])
            d_probs = dot(v_cols[j], o_rows[i])
            d_scores = (probs * (d_probs - delta[i])).astype(BF)
            dv = dv + dot(probs.astype(BF), o_cols[i])
            dk = dk + dot(d_scores, q_cols[i])
            dq[i] = dq[i] + dot(k_rows[j, 0:64, :], d_scores)
        outs[j, 0:64, :] = (dq[j] * HD ** (-0.5)).astype(BF)
        outs[j, 64:128, :] = dk[:, 0:64].astype(BF).T
        outs[j, 128:192, :] = dv.astype(BF).T


def attend_back_kernel(count, blk_ref, *refs):
    blk = blk_ref[0]
    sources = [refs[6 * h : 6 * h + 6] for h in range(count)]
    back, rest = refs[6 * count : 6 * count + 4], refs[6 * count + 4 :]
    pieces, outs, scratch = rest[0:4], rest[4], rest[5:]
    for h, (*parts, attended, spread) in enumerate(sources):
        grads = [piece[64 * h : 64 * h + 64, :] for piece in back]
        attend_back_head(blk, parts, grads, attended, spread, outs.at[h], [ref.at[h] for ref in scratch])
        for d, out in enumerate(pieces):
            out[192 * h : 192 * h + 192, :] = outs[h, lax.rem(blk + d, 4)]


def units(piece):
    for n in range(7):
        u = 7 * piece + n
        if u < 48:
            yield 16 * n, (16 * (u // 4), 2 * (u % 4)), (16 * (u // 4), 2 * (u % 4) + 1)
        elif u < 54:
            yield 16 * n, (32 * (u - 48), 8), (32 * (u - 48) + 16, 8)


def head_grad_kernel(place_ref, t0, t1, t2, t3, e01, e2, keep, send, sides, made, pieces):
    blk, core = place_ref[0], place_ref[3]
    total = jnp.zeros((D, 640), F32)
    for d, piece in enumerate((t0, t1, t2, t3)):
        s = lax.rem(blk + 4 - d, 4)
        for g, side in enumerate((e01.at[0], e01.at[1], e2.at[0])):
            sides[d, 192 * g : 192 * g + 192, :] = side[s]
        sides[d, 576:640, :] = jnp.zeros((64, R), BF)
        total = total + dot_nt(piece[...], sides[d])
    made[...] = total
    pieces[...] = jnp.zeros((8, 4, GROUP, 128), BF)
    for k in range(8):
        for at, (row, left), (row_right, right) in units(k):
            for i in range(4):
                r = 192 * i + row
                if right == left:
                    halves = (made[r : r + 16, 512:576], made[r + 16 : r + 32, 512:576])
                    block = jnp.concatenate(halves, axis=1)
                else:
                    block = made[r : r + 16, 64 * left : 64 * left + 128]
                pieces[k, i, at : at + 16, :] = block.astype(BF)
    for q in range(4):
        keep[q] = pieces[4 * core + q]
        send[q] = pieces[4 * (1 - core) + q]


def gelu_both(value):
    c = (2.0 / jnp.pi) ** 0.5
    square = value * value
    t = jnp.tanh(c * value * (1.0 + 0.044715 * square))
    cdf = 0.5 * (1.0 + t)
    slope = cdf + (0.5 * c) * value * (1.0 - t * t) * (1.0 + 3.0 * 0.044715 * square)
    return value * cdf, slope


CHUNK = 768


def active_grad_kernel(place_ref, cot, w_down, out, dy, pad):
    @pl.when(pl.program_id(0) == 0)
    def _():
        pad[R - 8 : R, :] = jnp.zeros((8, D), F32)
        pad[0:ROWS, :] = cot[0].astype(F32)
        dy[...] = pad[...].astype(BF)

    out[...] = dot_nt(dy[...], w_down[...])


def up_cut(values, store):
    for z in range(4):
        for yy in range(4):
            store(yy, z, values[192 * z + 48 * yy : 192 * z + 48 * yy + 48, :])


def down_cut(values, store):
    for yy in range(4):
        for xx in range(4):
            r, col = 48 * (2 * yy + xx // 2), 384 * (xx % 2)
            store(yy, xx, values[r : r + 48, col : col + 384])


def out_cut(values, out):
    for i in range(4):
        for n in range(16):
            rows = values[192 * i + 16 * n : 192 * i + 16 * n + 16, :] if n < 12 else jnp.zeros((16, 384), BF)
            out[n // 4, n % 4, i, 48:64] = rows


def put_block(out, at, rows):
    out[at] = rows.astype(BF)


def ff_kernel(
    blk_ref, r0, r1, r2, r3, hidden, cot, gains, w_out, w_up, d_active,
    active, d_up, second, middle, o_turned, d_branch, d_middle, p0, p1, p2, p3, a_out, b_out, gain_term,
    dy, back, stage, second_turned,
):
    step = pl.program_id(0)
    core = blk_ref[3]

    @pl.when(step == 0)
    def _():
        blk = blk_ref[0]
        for d, piece in enumerate((r0, r1, r2, r3)):
            s = lax.rem(blk + 4 - d, 4)
            for g in range(3):
                stage[4 * g + s] = piece[64 * g : 64 * g + 64, :]
        o_rows = stage[...].reshape(D, R)
        o_turned[...] = o_rows
        values = hidden[...] + dot(o_rows.T, w_out[...])
        middle[...] = values
        unit, _ = normalize(values)
        second[...] = (unit * gains[1:2, :]).astype(BF)
        back[R - 8 : R, :] = jnp.zeros((8, D), F32)
        back[0:ROWS, :] = cot[0].astype(F32)
        dy[...] = back[...].astype(BF)
        back[...] = jnp.zeros((R, D), F32)
        second_turned[...] = second[...].T

    upward = dot(second[...], w_up[...])
    act, slope = gelu_both(upward)
    act = act.astype(BF)
    active[...] = act
    d_upward = (d_active[...] * slope).astype(BF)
    d_up[...] = d_upward
    back[...] += dot_nt(d_upward, w_up[...])

    first = core == 0
    other_up = jnp.where(first, d_upward[:, 384:768], d_upward[:, 0:384])
    other_act = jnp.where(first, act[:, 384:768], act[:, 0:384])
    up_cut(dot(second_turned[...], other_up), lambda yy, z, rows: put_block(a_out, (yy, step, z), rows))
    down_cut(dot(other_act.T, dy[...]), lambda yy, xx, rows: put_block(b_out, (yy, xx, step, slice(0, 48)), rows))

    @pl.when(step == FF // CHUNK - 1)
    def _():
        blk = blk_ref[0]
        unit, inverse = normalize(middle[...])
        grad = back[...]
        gain_term[...] = jnp.sum(grad * unit, axis=0, keepdims=True)
        total = dy[...].astype(F32) + norm_back(grad, unit, inverse, gains[1:2, :])
        d_middle[...] = total
        low = total.astype(BF)
        d_branch[...] = low
        stage[...] = dot_nt(w_out[...], low).astype(BF).reshape(HEADS, HD, R)
        out_cut(dot(o_turned[...], jnp.where(core == 0, low[:, 384:768], low[:, 0:384])).astype(BF), b_out)
        for d, out in enumerate((p0, p1, p2, p3)):
            j = lax.rem(blk + d, 4)
            for g in range(3):
                out[64 * g : 64 * g + 64, :] = stage[4 * g + j]


def ff_grad_kernel(place_ref, active, d_up, second, cot, o_turned, d_branch, a_out, b_out, pad):
    first = place_ref[3] == 0
    pad[R - 8 : R, :] = jnp.zeros((8, D), F32)
    pad[0:ROWS, :] = cot[0].astype(F32)
    dy = pad[...].astype(BF)
    second_turned = second[...].T

    def half(ref, i):
        return jnp.where(first, ref[:, 768 * i : 768 * i + 384], ref[:, 768 * i + 384 : 768 * i + 768])

    out_cut(dot(o_turned[...], half(d_branch, 0)).astype(BF), b_out)
    for pair in ((0, 1), (2, 3)):
        up = dot(second_turned, jnp.concatenate([half(d_up, i) for i in pair], axis=1))
        down = dot(jnp.concatenate([half(active, i).T for i in pair], axis=0), dy)
        for n, i in enumerate(pair):
            up_cut(up[:, 384 * n : 384 * n + 384], lambda yy, z, rows: put_block(a_out, (yy, i, z), rows))
            down_cut(down[384 * n : 384 * n + 384], lambda yy, xx, rows: put_block(b_out, (yy, xx, i, slice(0, 48)), rows))


def core_sum_kernel(place_ref, a_mine, b_mine, a_got, b_got, a0, a1, a2, a3, b0, b1, b2, b3):
    x, y = place_ref[1], place_ref[2]
    for d, (a_out, b_out) in enumerate(((a0, b0), (a1, b1), (a2, b2), (a3, b3))):
        xx, yy = lax.rem(x + d, 4), lax.rem(y + d, 4)
        for n in range(4):
            a_out[n] = (a_mine[n, xx].astype(F32) + a_got[n, xx].astype(F32)).astype(BF)
            b_out[n] = (b_mine[yy, n].astype(F32) + b_got[yy, n].astype(F32)).astype(BF)


def total_of(parts):
    return (parts[0].astype(F32) + parts[2].astype(F32)) + (parts[1].astype(F32) + parts[3].astype(F32))


TINY = 96
GROUP = 112
PART_A = 144
PART_B = 192
PARTS = PART_A + PART_B


def put(buffer, at, block):
    rows, lanes = block.shape
    for t in range(lanes // 128):
        buffer[at + rows * t : at + rows * t + rows, :] = block[:, 128 * t : 128 * t + 128]


def put_small(buffer, at, value):
    high = value.astype(BF)
    low = (value - high.astype(F32)).astype(BF)
    put(buffer, at, jnp.concatenate([high, low], axis=0))


def get_small(buffer, at):
    parts = []
    for t in range(6):
        part = buffer[at + 16 * t : at + 16 * t + 16, :].astype(F32)
        parts.append(part[0:8] + part[8:16])
    return jnp.concatenate(parts, axis=1)


def take(buffer, at, rows):
    return jnp.concatenate([buffer[at + rows * t : at + rows * t + rows, :] for t in range(3)], axis=1)


def cut_kernel(place_ref, a0, a1, a2, a3, b0, b1, b2, b3, keep, got, y0, y1, y2, y3, x0, x1, x2, x3):
    x, y = place_ref[1], place_ref[2]
    for d, (y_out, x_out) in enumerate(((y0, x0), (y1, x1), (y2, x2), (y3, x3))):
        yy, xx = lax.rem(y + d, 4), lax.rem(x + d, 4)
        a_sum = total_of([r[yy] for r in (a0, a1, a2, a3)]).astype(BF)
        heads = (keep[yy].astype(F32) + got[yy].astype(F32)).astype(BF)
        for i in range(4):
            put(y_out, PART_A * i, a_sum[i])
            y_out[4 * PART_A + GROUP * i : 4 * PART_A + GROUP * i + GROUP, :] = heads[i]
        x_out[...] = total_of([r[xx] for r in (b0, b1, b2, b3)]).astype(BF)


def block_kernel(place_ref, y0, y1, y2, y3, x0, x1, x2, x3, small, o0, o1, o2, o3):
    z = place_ref[0]
    for d, out in enumerate((o0, o1, o2, o3)):
        i = lax.rem(z + d, 4)
        start = pl.multiple_of(PART_A * i, 16)
        out[0:PART_A, :] = total_of([r[pl.ds(start, PART_A), :] for r in (y0, y1, y2, y3)]).astype(BF)
        put(out, PART_A, total_of([r[i] for r in (x0, x1, x2, x3)]).astype(BF))
        start = pl.multiple_of(4 * PART_A + GROUP * i, 16)
        at = PART_A + PART_B
        out[at : at + GROUP, :] = total_of([r[pl.ds(start, GROUP), :] for r in (y0, y1, y2, y3)]).astype(BF)
        put_small(out, at + GROUP, small[...])


def own_kernel(place_ref, z0, z1, z2, z3, heads, bulk):
    parts = (z0, z1, z2, z3)
    for d, r in enumerate(parts):
        heads[GROUP * d : GROUP * d + GROUP, :] = r[PARTS : PARTS + GROUP, :]
    put_small(heads, 4 * GROUP, total_of([get_small(r, PARTS + GROUP) for r in parts]))
    bulk[...] = total_of([r[0:PARTS, :] for r in parts]).astype(BF)


def row_kernel(place_ref, y0, y1, y2, y3, out):
    for d, r in enumerate((y0, y1, y2, y3)):
        out[PARTS * d : PARTS * d + PARTS, :] = r[...]


def head_row_kernel(place_ref, x0, x1, x2, x3, out):
    parts = (x0, x1, x2, x3)
    out[0 : 4 * GROUP, :] = total_of([r[0 : 4 * GROUP, :] for r in parts]).astype(BF)
    put_small(out, 4 * GROUP, total_of([get_small(r, 4 * GROUP) for r in parts]))


ALL_TINY = 16 * GROUP
ALL_BULK = ALL_TINY + TINY
ALL = ALL_BULK + 16 * PARTS


def stack_kernel(place_ref, y0, y1, y2, y3, x0, x1, x2, x3, out):
    parts = (y0, y1, y2, y3)
    put_small(out, ALL_TINY, total_of([get_small(r, 4 * GROUP) for r in parts]))
    for d, (r, b) in enumerate(zip(parts, (x0, x1, x2, x3))):
        out[4 * GROUP * d : 4 * GROUP * d + 4 * GROUP, :] = r[0 : 4 * GROUP, :]
        out[ALL_BULK + 4 * PARTS * d : ALL_BULK + 4 * PARTS * d + 4 * PARTS, :] = b[...]


def finish_kernel(place_ref, mine, other, grad_qkv, grad_out, grad_up, grad_down, gains, passes, pair, turned):
    z, x, y, core = place_ref[0], place_ref[1], place_ref[2], place_ref[3]
    pair[core] = mine[...]
    pair[1 - core] = other[...]

    def rows(c, at, count):
        return pair[c, pl.ds(pl.multiple_of(at, 16), count), :].astype(F32)

    for c in range(2):
        for xx in range(4):
            dx = lax.rem(x + 4 - xx, 4)
            for yy in range(4):
                dy = lax.rem(y + 4 - yy, 4)
                a = rows(c, ALL_BULK + 4 * PARTS * dx + PARTS * dy, PART_A)
                b = rows(c, ALL_BULK + 4 * PARTS * dx + PARTS * dy + PART_A, PART_B)
                r = 384 * c + 48 * (2 * yy + xx // 2)
                for t in range(3):
                    col = 384 * (2 * xx + c) + 128 * t
                    grad_up[48 * yy : 48 * yy + 48, col : col + 128] = a[48 * t : 48 * t + 48]
                    col = 384 * (xx % 2) + 128 * t
                    grad_down[r : r + 48, col : col + 128] = b[64 * t : 64 * t + 48]
                    if yy < 3:
                        n, col = 16 * (4 * yy + xx), 384 * c + 128 * t
                        grad_out[n : n + 16, col : col + 128] = b[64 * t + 48 : 64 * t + 64]
        for yy in range(4):
            dy = lax.rem(y + 4 - yy, 4)
            for j in range(4):
                dz = lax.rem(z + 4 - j, 4)
                piece = rows(c, 4 * GROUP * dy + GROUP * dz, GROUP)
                for at, *halves in units(4 * c + yy):
                    for side, (r, n) in enumerate(halves):
                        col = D * (n % 3) + 64 * (4 * (n // 3) + j)
                        grad_qkv[r : r + 16, col : col + 64] = piece[at : at + 16, 64 * side : 64 * side + 64]
    small = get_small(mine, ALL_TINY) + get_small(other, ALL_TINY)
    turned[...] = small.T
    part = turned[pl.ds(pl.multiple_of(192 * z, 8), 192), :]
    part = part.T
    gains[...] = part[0:2, :]
    passes[...] = part[2:7, :]


def layer_out_kernel(place_ref, middle, active, w_down, out, total):
    step = pl.program_id(0)

    @pl.when(step == 0)
    def _():
        total[...] = middle[...]

    total[...] += dot(active[...], w_down[...])

    @pl.when(step == FF // CHUNK - 1)
    def _():
        out[0] = total[0:ROWS, :].astype(BF)


def input_grad_kernel(blk_ref, a0, a1, a2, a3, w0, w1, w2, w3, w4, w5, out, stage):
    blk = blk_ref[0]
    for d, piece in enumerate((a0, a1, a2, a3)):
        s = lax.rem(blk + 4 - d, 4)
        for n in range(6):
            stage[n, s] = piece[64 * n : 64 * n + 64, :]
    total = jnp.zeros((D, R), F32)
    for n, weight in enumerate((w0, w1, w2, w3, w4, w5)):
        total = total + dot(weight[...], stage[n].reshape(256, R))
    out[...] = total


def last_kernel(
    blk_ref, count_ref, c0, c1, c2, c3, so_far, hidden, d_middle, gain_term, gains, wq, wk, wv, grad_stream, small, stage
):
    blk = blk_ref[0]
    for d, piece in enumerate((c0, c1, c2, c3)):
        s = lax.rem(blk + 4 - d, 4)
        for part in range(3):
            stage[part, s] = piece[64 * part : 64 * part + 64, :]
    turned = so_far[...]
    for part, weight in enumerate((wq, wk, wv)):
        turned = turned + dot(weight[...], stage[part].reshape(256, R))
    grad = turned.T
    unit, inverse = normalize(hidden[...])
    total = d_middle[...] + norm_back(grad, unit, inverse, gains[0:1, :])
    grad_stream[0] = total[0:ROWS, :]
    row = lax.broadcasted_iota(jnp.int32, (R, 1), 0)
    which = jnp.where(row < ROWS, pass_index(blk, count_ref[0]), -1)
    small[0:1, :] = jnp.sum(grad * unit, axis=0, keepdims=True)
    small[1:2, :] = gain_term[...]
    for r in range(PASSES):
        small[2 + r : 3 + r, :] = jnp.sum(jnp.where(which == r, total, 0.0), axis=0, keepdims=True)
    small[7:8, :] = jnp.zeros((1, D), F32)


def shift(values, axis, d):
    if axis == "z":
        return lax.ppermute(values, "blk", [(i, (i + d) % 4) for i in range(4)])
    pairs = []
    for b in range(32):
        y, x, core = b // 8, (b // 2) % 4, b % 2
        if axis == "y":
            y = (y + d) % 4
        elif axis == "x":
            x = (x + d) % 4
        else:
            core = (core + d) % 2
        pairs.append((b, 8 * y + 2 * x + core))
    return lax.ppermute(values, "batch", pairs)


def spread_pieces(pieces, axis):
    two, three, one = (shift(pieces[d], axis, d) for d in (2, 3, 1))
    return (pieces[0], one, two, three)


def all_of(value, axis):
    return spread_pieces((value,) * 4, axis)


def after(value, *others):
    return lax.optimization_barrier((value,) + others)[0]


def far(value):
    return pltpu.with_memory_space_constraint(value, pltpu.HBM)


def weight_spec(column):
    return pl.BlockSpec((D, 256), lambda *_, column=column: (0, column))


def on_device(stream, cotangent, passes, w_qkv, w_out, w_up, w_down, ln_gains, pass_embed):
    z = lax.axis_index("blk").astype(jnp.int32)
    batch = lax.axis_index("batch").astype(jnp.int32)
    place = jnp.stack([z, batch // 2 % 4, batch // 8, batch % 2])
    gains = ln_gains.T
    embed = pass_embed.T
    piece = shape((192, R))
    full = shape((R, D))

    def arrived(*values):
        nonlocal place
        place = lax.optimization_barrier((place,) + values)[0]

    def ordered(outs):
        nonlocal place
        *outs, first = outs
        place, first = lax.optimization_barrier((place, first))
        return (*outs, first)

    hidden, turned, *early, normed = ordered(pl.pallas_call(
        first_kernel,
        grid=(1,),
        in_specs=[SM, SM, VM, VM, VM, weight_spec(0), weight_spec(3), weight_spec(6)],
        out_specs=[VM] * 7,
        out_shape=[kept((R, D), F32), kept((D, R)), kept((192, R)), piece, piece, piece, full],
        scratch_shapes=[pltpu.VMEM((4, 192, R), BF)],
        compiler_params=room(24),
        name="ln_qkv",
    )(place, passes, far(stream), far(embed), far(gains), *([far(w_qkv)] * 3)))
    sent = ordered(pl.pallas_call(
        second_kernel,
        grid=(1,),
        in_specs=[SM, VM] + [weight_spec(c) for c in (1, 4, 7, 2, 5, 8)],
        out_specs=[VM] * 8,
        out_shape=([kept((192, R))] + [piece] * 3) * 2,
        scratch_shapes=[pltpu.VMEM((2, 4, 192, R), BF)],
        compiler_params=room(24),
        name="qkv_rest",
    )(place, normed, *([far(w_qkv)] * 6)))
    heads = [spread_pieces(early, "z"), spread_pieces(sent[0:4], "z")]
    last_group = [sent[4], shift(sent[5], "z", 1), sent[6], shift(sent[7], "z", 3)]

    attended, spreads, sent = [], [], []
    for g in range(3):
        *parts, result, spread = ordered(run(
            lambda *refs, g=g: attend_kernel(g == 2, *refs),
            "attend",
            24,
            [shape((192 if g == 2 else HD, R))] * 4 + [kept((4, HD, R), F32), kept((4, 1, R), F32)],
            (place, *heads[g], *(sent if g == 2 else ())),
            [
                pltpu.VMEM((4, 128, R), BF),
                pltpu.VMEM((4, 128, R), BF),
                pltpu.VMEM((4, HD, R), BF),
                pltpu.VMEM((4, R, 128), BF),
                pltpu.VMEM((4, R, R), F32),
                pltpu.VMEM((4, HD, R), BF),
            ],
        ))
        if g == 0:
            last_group[2] = shift(after(last_group[2], place), "z", 2)
            heads.append(last_group)
        attended.append(result)
        spreads.append(spread)
        sent += parts
    sent = sent[8:]
    back_o = spread_pieces(sent, "z")
    d_active = ordered((pl.pallas_call(
        active_grad_kernel,
        grid=(FF // CHUNK,),
        in_specs=[SM, VM, pl.BlockSpec((CHUNK, D), lambda f: (f, 0))],
        out_specs=pl.BlockSpec((R, CHUNK), lambda f: (0, f)),
        out_shape=kept((R, FF), F32),
        scratch_shapes=[pltpu.VMEM((R, D), BF), pltpu.VMEM((R, D), F32)],
        compiler_params=room(16),
        name="active_grad",
    )(place, far(cotangent), far(w_down)),))[0]
    near = after(turned, place, *back_o)
    near = (shift(near, "z", 1), shift(near, "z", 3))

    active, d_up, second, middle, o_turned, d_branch, d_middle, *sent, a_other, b_other, gain_term = ordered(pl.pallas_call(
        ff_kernel,
        grid=(FF // CHUNK,),
        in_specs=[SM] + [VM] * 4 + [VM, VM, VM, VM]
        + [pl.BlockSpec((D, CHUNK), lambda f: (0, f)), pl.BlockSpec((R, CHUNK), lambda f: (0, f))],
        out_specs=[pl.BlockSpec((R, CHUNK), lambda f: (0, f)), pl.BlockSpec((R, CHUNK), lambda f: (0, f))] + [VM] * 12,
        out_shape=[shape((R, FF)), shape((R, FF)), full, shape((R, D), F32), shape((D, R)), full, kept((R, D), F32)]
        + [kept((192, R))] + [piece] * 3 + [shape((4, 4, 4, 48, 384)), shape((4, 4, 4, 64, 384)), shape((1, D), F32)],
        scratch_shapes=[pltpu.VMEM((R, D), BF), pltpu.VMEM((R, D), F32), pltpu.VMEM((HEADS, HD, R), BF), pltpu.VMEM((D, R), BF)],
        compiler_params=room(36),
        name="ff",
    )(place, *back_o, hidden, cotangent, gains, w_out, far(w_up), far(d_active)))
    *sent, a_other, b_other = lax.optimization_barrier((*sent, a_other, b_other, *near))[:6]
    d_o = spread_pieces(sent, "z")

    got = (shift(a_other, "core", 1), shift(b_other, "core", 1))
    own = ordered(run(
        ff_grad_kernel,
        "ff_grad",
        32,
        [shape((4, 4, 4, 48, 384)), shape((4, 4, 4, 64, 384))],
        (place, active, d_up, second, far(cotangent), o_turned, d_branch),
        [pltpu.VMEM((R, D), F32)],
    ))
    sent = ordered(run(
        core_sum_kernel,
        "core_sum",
        24,
        [kept((4, 4, 48, 384))] + [shape((4, 4, 48, 384))] * 3 + [kept((4, 4, 64, 384))] + [shape((4, 4, 64, 384))] * 3,
        (place, *own, *got),
    ))
    arrived(*d_o)
    distant = shift(after(turned, *d_o, place), "z", 2)
    a_sent, b_sent = sent[0:4], sent[4:8]
    a_parts = [a_sent[0], shift(a_sent[1], "x", 1), None, shift(a_sent[3], "x", 3)]
    b_parts = [b_sent[0], shift(b_sent[1], "y", 1), None, shift(b_sent[3], "y", 3)]

    def attend_back(which):
        count = len(which)
        group = pl.BlockSpec((64 * count, R), lambda _: (which[0] // count, 0))
        operands = [t for g in which for t in (*heads[g], attended[g], spreads[g])]
        return ordered(pl.pallas_call(
            lambda *refs: attend_back_kernel(count, *refs),
            grid=(1,),
            in_specs=[SM] + [VM] * (6 * count) + [group] * 4,
            out_specs=[VM] * 5,
            out_shape=[kept((192 * count, R))] + [shape((192 * count, R))] * 3 + [kept((count, 4, 192, R))],
            scratch_shapes=[
                pltpu.VMEM((count, 4, 128, R), BF),
                pltpu.VMEM((count, 4, 128, R), BF),
                pltpu.VMEM((count, 4, HD, R), BF),
                pltpu.VMEM((count, 4, R, 128), BF),
                pltpu.VMEM((count, 4, R, 128), BF),
                pltpu.VMEM((count, 4, R, HD), BF),
                pltpu.VMEM((count, 4, HD, R), BF),
                pltpu.VMEM((count, 4, R, HD), BF),
                pltpu.VMEM((count, 4, 1, R), F32),
                pltpu.VMEM((count, 4, HD, R), F32),
            ],
            compiler_params=room(32 if count == 2 else 24),
            name="attend_back",
        )(place, *(far(t) for t in operands), *(far(t) for t in d_o)))

    *sent, made_first = attend_back((0, 1))
    first_pieces = spread_pieces(sent, "z")
    a_parts[2] = shift(after(a_sent[2], place), "x", 2)
    b_parts[2] = shift(after(b_sent[2], place), "y", 2)
    arrived(a_parts[1], a_parts[3], b_parts[1], b_parts[3], distant)
    *sent, made_last = attend_back((2,))
    keep, send = ordered(run(
        head_grad_kernel,
        "head_grad",
        32,
        [shape((4, 4, GROUP, 128))] * 2,
        (place, far(turned), far(near[0]), far(distant), far(near[1]), far(made_first), far(made_last)),
        [pltpu.VMEM((4, 640, R), BF), pltpu.VMEM((D, 640), F32), pltpu.VMEM((8, 4, GROUP, 128), BF)],
    ))
    arrived(*first_pieces, a_parts[2], b_parts[2])
    *sent, send = lax.optimization_barrier((*sent, send, *first_pieces, a_parts[2], b_parts[2]))[:5]
    last_pieces = spread_pieces(sent, "z")
    got = shift(send, "core", 1)

    sent = ordered(run(
        cut_kernel,
        "sum_first",
        24,
        [shape((4 * PART_A + 4 * GROUP, 128))] * 4 + [shape((4, 64, 384))] * 4,
        (place, *a_parts, *b_parts, keep, got),
    ))
    so_far = ordered((pl.pallas_call(
        input_grad_kernel,
        grid=(1,),
        in_specs=[SM] + [VM] * 4 + [weight_spec(c) for c in (0, 3, 6, 1, 4, 7)],
        out_specs=VM,
        out_shape=shape((D, R), F32),
        scratch_shapes=[pltpu.VMEM((6, 4, HD, R), BF)],
        compiler_params=room(24),
        name="input_grad",
    )(place, *first_pieces, *([far(w_qkv)] * 6)),))[0]
    own_y, *others = lax.optimization_barrier((*sent, place))[:8]
    y_parts, x_parts = spread_pieces([own_y, *others[0:3]], "y"), spread_pieces(others[3:7], "x")
    grad_stream, small = ordered(pl.pallas_call(
        last_kernel,
        grid=(1,),
        in_specs=[SM, SM] + [VM] * 9 + [weight_spec(c) for c in (2, 5, 8)],
        out_specs=[VM, VM],
        out_shape=[kept((1, ROWS, D), F32), shape((8, D), F32)],
        scratch_shapes=[pltpu.VMEM((3, 4, HD, R), BF)],
        compiler_params=room(24),
        name="ln_back",
    )(place, passes, *last_pieces, so_far, far(hidden), far(d_middle), gain_term, gains, *([far(w_qkv)] * 3)))
    sent = ordered(run(
        block_kernel,
        "sum_second",
        16,
        [shape((PART_A + PART_B + GROUP + TINY, 128))] * 4,
        (place, *y_parts, *x_parts, small),
    ))
    z_parts = spread_pieces(sent, "z")
    layer_out = ordered((pl.pallas_call(
        layer_out_kernel,
        grid=(FF // CHUNK,),
        in_specs=[SM, VM, pl.BlockSpec((R, CHUNK), lambda f: (0, f)), pl.BlockSpec((CHUNK, D), lambda f: (f, 0))],
        out_specs=VM,
        out_shape=kept((1, ROWS, D)),
        scratch_shapes=[pltpu.VMEM((R, D), F32)],
        compiler_params=room(16),
        name="layer_out",
    )(place, middle, active, far(w_down)),))[0]
    head, bulk = ordered(run(
        own_kernel, "sum_blocks", 16, [shape((4 * GROUP + TINY, 128)), shape((PARTS, 128))], (place, *z_parts)
    ))
    bulks, heads_x = all_of(bulk, "y"), all_of(head, "x")
    row = ordered(run(row_kernel, "stack_rows", 16, [shape((4 * PARTS, 128))], (place, *bulks)))[0]
    rows = [row, shift(row, "x", 1), None, shift(row, "x", 3)]
    head = ordered(run(head_row_kernel, "sum_heads", 16, [shape((4 * GROUP + TINY, 128))], (place, *heads_x)))[0]
    rows[2] = shift(after(row, place), "x", 2)
    heads_y = all_of(head, "y")
    buffer = ordered(run(stack_kernel, "stack", 16, [shape((ALL, 128))], (place, *heads_y, *rows)))[0]
    *results, grad_gains, grad_pass = run(
        finish_kernel,
        "finish",
        32,
        [
            kept((192, 3 * D), F32),
            kept((192, D), F32),
            kept((192, FF), F32),
            kept((D, D), F32),
            shape((2, 192), F32),
            shape((PASSES, 192), F32),
        ],
        (place, buffer, shift(buffer, "core", 1)),
        [pltpu.VMEM((2, ALL, 128), BF), pltpu.VMEM((D, 8), F32)],
    )
    return (layer_out, grad_stream, *results, grad_gains.T, grad_pass.T)


def solution(mesh):
    tokens = P("batch", "blk", None)
    in_specs = (tokens, tokens, P("batch"), P(), P(), P(), P(), P(), P())
    out_specs = (tokens, tokens) + (P("blk", None),) * 6
    return jax.shard_map(on_device, mesh=mesh, in_specs=in_specs, out_specs=out_specs, check_vma=False)
```

```python
import jax
import jax.numpy as jnp
from jax import lax
from jax.experimental import pallas as pl
from jax.experimental.pallas import tpu as pltpu
from jax.sharding import PartitionSpec as P

D = 768
HEADS = 12
HD = 64
FF = 3072
PASSES = 5
ROWS = 510
R = 512
EPS = 1e-05
NEG = -1e30
BF = jnp.bfloat16
F32 = jnp.float32
VM = pl.BlockSpec(memory_space=pltpu.VMEM)
SM = pl.BlockSpec(memory_space=pltpu.SMEM)
HB = pl.BlockSpec(memory_space=pl.ANY)
MIB = 1024 * 1024


def room(mib):
    return pltpu.CompilerParams(vmem_limit_bytes=mib * MIB)


def run(kernel, name, mib, outs, operands, scratch=(), scalars=1):
    return pl.pallas_call(
        kernel,
        in_specs=[SM] * scalars + [VM] * (len(operands) - scalars),
        out_specs=[VM] * len(outs),
        out_shape=outs,
        scratch_shapes=list(scratch),
        compiler_params=room(mib),
        name=name,
    )(*operands)


def shape(dims, kind=BF):
    return jax.ShapeDtypeStruct(dims, kind)


def kept(dims, kind=BF):
    return pltpu.HBM(dims, kind)


def dot(left, right):
    return jnp.dot(left, right, preferred_element_type=F32)


def dot_nt(left, right):
    return lax.dot_general(left, right, (((1,), (1,)), ((), ())), preferred_element_type=F32)


def normalize(values):
    mean = jnp.mean(values, axis=-1, keepdims=True)
    centred = values - mean
    inverse = lax.rsqrt(jnp.mean(centred * centred, axis=-1, keepdims=True) + EPS)
    return centred * inverse, inverse


def norm_back(grad, unit, inverse, gain):
    scaled = grad * gain
    first = jnp.mean(scaled, axis=-1, keepdims=True)
    second = jnp.mean(scaled * unit, axis=-1, keepdims=True)
    return inverse * (scaled - first - unit * second)


def pass_index(blk, count):
    row = lax.broadcasted_iota(jnp.int32, (R, 1), 0) + blk * ROWS
    turns = jnp.floor((row.astype(F32) + 0.5) / count.astype(F32)).astype(jnp.int32)
    return row - turns * count


def pieces_out(stage, outs, blk):
    for d, out in enumerate(outs):
        out[...] = stage[lax.rem(blk + d, 4)]


def project(normed, weights, stage, outs, blk):
    for part, weight in enumerate(weights):
        got = dot(normed, weight[...])
        if part == 0:
            got = got.astype(BF) * jnp.asarray(HD ** (-0.5), BF)
        turned = got.astype(BF).T
        for j in range(4):
            stage[j, 64 * part : 64 * part + 64, :] = turned[64 * j : 64 * j + 64]
    pieces_out(stage, outs, blk)


def project(normed, weights, stage):
    for part, weight in enumerate(weights):
        got = dot(normed, weight[...])
        if part == 0:
            got = got.astype(BF) * jnp.asarray(HD ** (-0.5), BF)
        flipped = got.astype(BF).T
        for j in range(4):
            stage[j, 64 * part : 64 * part + 64, :] = flipped[64 * j : 64 * j + 64]


def first_kernel(blk_ref, count_ref, stream, embed, gains, wq, wk, wv, hidden, turned, p0, p1, p2, p3, normed, stage):
    blk = blk_ref[0]
    hidden[R - 8 : R, :] = jnp.zeros((8, D), F32)
    hidden[0:ROWS, :] = stream[0].astype(F32)
    which = pass_index(blk, count_ref[0])
    added = embed[0:1, :]
    for r in range(1, PASSES):
        added = jnp.where(which == r, embed[r : r + 1, :], added)
    values = hidden[...] + added
    hidden[...] = values
    unit, _ = normalize(values)
    row = lax.broadcasted_iota(jnp.int32, (R, 1), 0)
    low = jnp.where(row < ROWS, unit * gains[0:1, :], 0.0).astype(BF)
    normed[...] = low
    project(low, (wq, wk, wv), stage)
    for d, out in enumerate((p0, p1, p2, p3)):
        out[...] = stage[lax.rem(blk + d, 4)]
    turned[...] = low.T


def second_kernel(blk_ref, normed, wq1, wk1, wv1, wq2, wk2, wv2, p0, p1, p2, p3, q0, q1, q2, q3, stage):
    blk = blk_ref[0]
    for n, (weights, outs) in enumerate((((wq1, wk1, wv1), (p0, p1, p2, p3)), ((wq2, wk2, wv2), (q0, q1, q2, q3)))):
        project(normed[...], weights, stage.at[n])
        for d, out in enumerate(outs):
            out[...] = stage[n, lax.rem(blk + d, 4)]


def load_heads(whole, q_rows, k_rows, v_rows, k_cols):
    for s in range(4):
        q_rows[s, 0:64, :] = whole[s, 0:64, :]
        k_rows[s, 0:64, :] = whole[s, 64:128, :]
        v_rows[s] = whole[s, 128:192, :]
    row = lax.broadcasted_iota(jnp.int32, (64, R), 0)
    col = lax.broadcasted_iota(jnp.int32, (64, R), 1)
    one = jnp.where(row == 0, 1.0, 0.0).astype(BF)
    off = jnp.where((row == 0) & (col >= ROWS), NEG, 0.0).astype(BF)
    for s in range(4):
        q_rows[s, 64:128, :] = one
        k_rows[s, 64:128, :] = off
    for s in range(4):
        k_cols[s] = k_rows[s].T


HALF = R // 2


def causal(keys, queries):
    key = lax.broadcasted_iota(jnp.int32, (keys, queries), 0)
    query = lax.broadcasted_iota(jnp.int32, (keys, queries), 1)
    return key <= query


def attend_kernel(last, blk_ref, r0, r1, r2, r3, *rest):
    earlier, rest = (rest[:8], rest[8:]) if last else ((), rest)
    p0, p1, p2, p3, whole, attended, spread, q_rows, k_rows, v_rows, k_cols, scores, stage = rest
    blk = blk_ref[0]
    for d, piece in enumerate((r0, r1, r2, r3)):
        whole[lax.rem(blk + 4 - d, 4)] = piece[...]
    load_heads(whole, q_rows, k_rows, v_rows, k_cols)
    for i in range(4):
        low = jnp.where(causal(HALF, R), dot(k_cols[i, 0:HALF, :], q_rows[i]), NEG)
        high = jnp.where(causal(HALF, HALF), dot(k_cols[i, HALF:R, :], q_rows[i, :, HALF:R]), NEG)
        top = jnp.max(low, axis=0, keepdims=True)
        right = jnp.maximum(top[:, HALF:R], jnp.max(high, axis=0, keepdims=True))
        top = jnp.concatenate([top[:, 0:HALF], right], axis=1)
        for j in range(i):
            got = dot(k_cols[j], q_rows[i])
            scores[j] = got
            top = jnp.maximum(top, jnp.max(got, axis=0, keepdims=True))
        low = jnp.exp(low - top)
        high = jnp.exp(high - top[:, HALF:R])
        total = jnp.sum(low, axis=0, keepdims=True)
        summed = dot(v_rows[i, :, 0:HALF], low.astype(BF))
        right = total[:, HALF:R] + jnp.sum(high, axis=0, keepdims=True)
        total = jnp.concatenate([total[:, 0:HALF], right], axis=1)
        right = summed[:, HALF:R] + dot(v_rows[i, :, HALF:R], high.astype(BF))
        summed = jnp.concatenate([summed[:, 0:HALF], right], axis=1)
        for j in range(i):
            raised = jnp.exp(scores[j] - top)
            total = total + jnp.sum(raised, axis=0, keepdims=True)
            summed = summed + dot(v_rows[j], raised.astype(BF))
        result = summed / total
        attended[i] = result
        spread[i] = top + jnp.log(total)
        stage[i] = result.astype(BF)
    at = 128 if last else 0
    for d, out in enumerate((p0, p1, p2, p3)):
        out[at : at + 64, :] = stage[lax.rem(blk + d, 4)]
        if last:
            out[0:64, :] = earlier[d][...]
            out[64:128, :] = earlier[4 + d][...]


def attend_back_head(blk, whole, back, attended, spread, outs, scratch):
    q_rows, k_rows, v_rows, k_cols, q_cols, v_cols, o_rows, o_cols, delta, dq = scratch
    load_heads(whole, q_rows, k_rows, v_rows, k_cols)
    for d, piece in enumerate(back):
        o_rows[lax.rem(blk + 4 - d, 4)] = piece
    for s in range(4):
        q_cols[s] = q_rows[s].T
        v_cols[s] = v_rows[s].T
        o_cols[s] = o_rows[s].T
        delta[s] = jnp.sum(o_rows[s].astype(F32) * attended[s], axis=0, keepdims=True)
        dq[s] = jnp.zeros((HD, R), F32)
    for j in range(4):
        dk = jnp.zeros((R, 2 * HD), F32)
        dv = jnp.zeros((R, HD), F32)
        for i in range(j, 4):
            got = dot(k_cols[j], q_rows[i])
            if i == j:
                got = jnp.where(causal(R, R), got, NEG)
            probs = jnp.exp(got - spread[i])
            d_probs = dot(v_cols[j], o_rows[i])
            d_scores = (probs * (d_probs - delta[i])).astype(BF)
            dv = dv + dot(probs.astype(BF), o_cols[i])
            dk = dk + dot(d_scores, q_cols[i])
            dq[i] = dq[i] + dot(k_rows[j, 0:64, :], d_scores)
        outs[j, 0:64, :] = (dq[j] * HD ** (-0.5)).astype(BF)
        outs[j, 64:128, :] = dk[:, 0:64].astype(BF).T
        outs[j, 128:192, :] = dv.astype(BF).T


def attend_back_kernel(count, blk_ref, *refs):
    blk = blk_ref[0]
    sources = [refs[3 * h : 3 * h + 3] for h in range(count)]
    back, rest = refs[3 * count : 3 * count + 4], refs[3 * count + 4 :]
    pieces, outs, scratch = rest[0:4], rest[4], rest[5:]
    for h, (whole, attended, spread) in enumerate(sources):
        grads = [piece[64 * h : 64 * h + 64, :] for piece in back]
        attend_back_head(blk, whole, grads, attended, spread, outs.at[h], [ref.at[h] for ref in scratch])
        for d, out in enumerate(pieces):
            out[192 * h : 192 * h + 192, :] = outs[h, lax.rem(blk + d, 4)]


def units(piece):
    for n in range(7):
        u = 7 * piece + n
        if u < 48:
            yield 16 * n, (16 * (u // 4), 2 * (u % 4)), (16 * (u // 4), 2 * (u % 4) + 1)
        elif u < 54:
            yield 16 * n, (32 * (u - 48), 8), (32 * (u - 48) + 16, 8)


def head_grad_kernel(place_ref, t0, t1, t2, t3, e01, e2, keep, send, sides, made, pieces):
    blk, core = place_ref[0], place_ref[3]
    total = jnp.zeros((D, 640), F32)
    for d, piece in enumerate((t0, t1, t2, t3)):
        s = lax.rem(blk + 4 - d, 4)
        for g, side in enumerate((e01.at[0], e01.at[1], e2.at[0])):
            sides[d, 192 * g : 192 * g + 192, :] = side[s]
        sides[d, 576:640, :] = jnp.zeros((64, R), BF)
        total = total + dot_nt(piece[...], sides[d])
    made[...] = total
    pieces[...] = jnp.zeros((8, 4, GROUP, 128), BF)
    for k in range(8):
        for at, (row, left), (row_right, right) in units(k):
            for i in range(4):
                r = 192 * i + row
                if right == left:
                    halves = (made[r : r + 16, 512:576], made[r + 16 : r + 32, 512:576])
                    block = jnp.concatenate(halves, axis=1)
                else:
                    block = made[r : r + 16, 64 * left : 64 * left + 128]
                pieces[k, i, at : at + 16, :] = block.astype(BF)
    for q in range(4):
        keep[q] = pieces[4 * core + q]
        send[q] = pieces[4 * (1 - core) + q]


def gelu_both(value):
    c = (2.0 / jnp.pi) ** 0.5
    square = value * value
    t = jnp.tanh(c * value * (1.0 + 0.044715 * square))
    cdf = 0.5 * (1.0 + t)
    slope = cdf + (0.5 * c) * value * (1.0 - t * t) * (1.0 + 3.0 * 0.044715 * square)
    return value * cdf, slope


CHUNK = 768


def active_grad_kernel(place_ref, cot, w_down, out, dy, pad):
    @pl.when(pl.program_id(0) == 0)
    def _():
        pad[R - 8 : R, :] = jnp.zeros((8, D), F32)
        pad[0:ROWS, :] = cot[0].astype(F32)
        dy[...] = pad[...].astype(BF)

    out[...] = dot_nt(dy[...], w_down[...])


def up_cut(values, store):
    for z in range(4):
        for yy in range(4):
            store(yy, z, values[192 * z + 48 * yy : 192 * z + 48 * yy + 48, :])


def down_cut(values, store):
    for yy in range(4):
        for xx in range(4):
            r, col = 48 * (2 * yy + xx // 2), 384 * (xx % 2)
            store(yy, xx, values[r : r + 48, col : col + 384])


def out_cut(values, out):
    for i in range(4):
        for n in range(16):
            rows = values[192 * i + 16 * n : 192 * i + 16 * n + 16, :] if n < 12 else jnp.zeros((16, 384), BF)
            out[n // 4, n % 4, i, 48:64] = rows


def put_block(out, at, rows):
    out[at] = rows.astype(BF)


def ff_kernel(
    blk_ref, r0, r1, r2, r3, hidden, cot, gains, w_out, w_up, d_active,
    active, d_up, second, middle, o_turned, d_branch, d_middle, p0, p1, p2, p3, a_out, b_out, gain_term,
    dy, back, stage, second_turned,
):
    step = pl.program_id(0)
    core = blk_ref[3]

    @pl.when(step == 0)
    def _():
        blk = blk_ref[0]
        for d, piece in enumerate((r0, r1, r2, r3)):
            s = lax.rem(blk + 4 - d, 4)
            for g in range(3):
                stage[4 * g + s] = piece[64 * g : 64 * g + 64, :]
        o_rows = stage[...].reshape(D, R)
        o_turned[...] = o_rows
        values = hidden[...] + dot(o_rows.T, w_out[...])
        middle[...] = values
        unit, _ = normalize(values)
        second[...] = (unit * gains[1:2, :]).astype(BF)
        back[R - 8 : R, :] = jnp.zeros((8, D), F32)
        back[0:ROWS, :] = cot[0].astype(F32)
        dy[...] = back[...].astype(BF)
        back[...] = jnp.zeros((R, D), F32)
        second_turned[...] = second[...].T

    upward = dot(second[...], w_up[...])
    act, slope = gelu_both(upward)
    act = act.astype(BF)
    at = pl.ds(pl.multiple_of(step * CHUNK, 128), CHUNK)
    active[:, at] = act
    d_upward = (d_active[...] * slope).astype(BF)
    d_up[:, at] = d_upward
    back[...] += dot_nt(d_upward, w_up[...])

    first = core == 0
    other_up = jnp.where(first, d_upward[:, 384:768], d_upward[:, 0:384])
    other_act = jnp.where(first, act[:, 384:768], act[:, 0:384])
    up_cut(dot(second_turned[...], other_up), lambda yy, z, rows: put_block(a_out, (yy, step, z), rows))
    down_cut(dot(other_act.T, dy[...]), lambda yy, xx, rows: put_block(b_out, (yy, xx, step, slice(0, 48)), rows))

    @pl.when(step == FF // CHUNK - 1)
    def _():
        blk = blk_ref[0]
        unit, inverse = normalize(middle[...])
        grad = back[...]
        gain_term[...] = jnp.sum(grad * unit, axis=0, keepdims=True)
        total = dy[...].astype(F32) + norm_back(grad, unit, inverse, gains[1:2, :])
        d_middle[...] = total
        low = total.astype(BF)
        d_branch[...] = low
        stage[...] = dot_nt(w_out[...], low).astype(BF).reshape(HEADS, HD, R)
        out_cut(dot(o_turned[...], jnp.where(core == 0, low[:, 384:768], low[:, 0:384])).astype(BF), b_out)
        for d, out in enumerate((p0, p1, p2, p3)):
            j = lax.rem(blk + d, 4)
            for g in range(3):
                out[64 * g : 64 * g + 64, :] = stage[4 * g + j]


def ff_grad_kernel(place_ref, active, d_up, second, cot, o_turned, d_branch, a_out, b_out, pad):
    first = place_ref[3] == 0
    pad[R - 8 : R, :] = jnp.zeros((8, D), F32)
    pad[0:ROWS, :] = cot[0].astype(F32)
    dy = pad[...].astype(BF)
    second_turned = second[...].T

    def half(ref, i):
        return jnp.where(first, ref[:, 768 * i : 768 * i + 384], ref[:, 768 * i + 384 : 768 * i + 768])

    out_cut(dot(o_turned[...], half(d_branch, 0)).astype(BF), b_out)
    for pair in ((0, 1), (2, 3)):
        up = dot(second_turned, jnp.concatenate([half(d_up, i) for i in pair], axis=1))
        down = dot(jnp.concatenate([half(active, i).T for i in pair], axis=0), dy)
        for n, i in enumerate(pair):
            up_cut(up[:, 384 * n : 384 * n + 384], lambda yy, z, rows: put_block(a_out, (yy, i, z), rows))
            down_cut(down[384 * n : 384 * n + 384], lambda yy, xx, rows: put_block(b_out, (yy, xx, i, slice(0, 48)), rows))


def core_sum_kernel(place_ref, a_mine, b_mine, a_got, b_got, a0, a1, a2, a3, b0, b1, b2, b3):
    x, y = place_ref[1], place_ref[2]
    for d, (a_out, b_out) in enumerate(((a0, b0), (a1, b1), (a2, b2), (a3, b3))):
        xx, yy = lax.rem(x + d, 4), lax.rem(y + d, 4)
        for n in range(4):
            a_out[n] = (a_mine[n, xx].astype(F32) + a_got[n, xx].astype(F32)).astype(BF)
            b_out[n] = (b_mine[yy, n].astype(F32) + b_got[yy, n].astype(F32)).astype(BF)


def total_of(parts):
    return (parts[0].astype(F32) + parts[2].astype(F32)) + (parts[1].astype(F32) + parts[3].astype(F32))


TINY = 96
GROUP = 112
PART_A = 144
PART_B = 192
PARTS = PART_A + PART_B
SPACE = 560


def put(buffer, at, block):
    rows, lanes = block.shape
    for t in range(lanes // 128):
        buffer[at + rows * t : at + rows * t + rows, :] = block[:, 128 * t : 128 * t + 128]


def put_small(buffer, at, value):
    high = value.astype(BF)
    low = (value - high.astype(F32)).astype(BF)
    put(buffer, at, jnp.concatenate([high, low], axis=0))


def get_small(buffer, at):
    parts = []
    for t in range(6):
        part = buffer[at + 16 * t : at + 16 * t + 16, :].astype(F32)
        parts.append(part[0:8] + part[8:16])
    return jnp.concatenate(parts, axis=1)


def take(buffer, at, rows):
    return jnp.concatenate([buffer[at + rows * t : at + rows * t + rows, :] for t in range(3)], axis=1)


def cut_kernel(place_ref, a0, a1, a2, a3, b0, b1, b2, b3, keep, got, y0, y1, y2, y3, x0, x1, x2, x3):
    x, y = place_ref[1], place_ref[2]
    for d, (y_out, x_out) in enumerate(((y0, x0), (y1, x1), (y2, x2), (y3, x3))):
        yy, xx = lax.rem(y + d, 4), lax.rem(x + d, 4)
        a_sum = total_of([r[yy] for r in (a0, a1, a2, a3)]).astype(BF)
        heads = (keep[yy].astype(F32) + got[yy].astype(F32)).astype(BF)
        for i in range(4):
            put(y_out, PART_A * i, a_sum[i])
            y_out[4 * PART_A + GROUP * i : 4 * PART_A + GROUP * i + GROUP, :] = heads[i]
        x_out[...] = total_of([r[xx] for r in (b0, b1, b2, b3)]).astype(BF)


def block_kernel(place_ref, y0, y1, y2, y3, x0, x1, x2, x3, small, o0, o1, o2, o3):
    z = place_ref[0]
    for d, out in enumerate((o0, o1, o2, o3)):
        i = lax.rem(z + d, 4)
        start = pl.multiple_of(PART_A * i, 16)
        out[0:PART_A, :] = total_of([r[pl.ds(start, PART_A), :] for r in (y0, y1, y2, y3)]).astype(BF)
        put(out, PART_A, total_of([r[i] for r in (x0, x1, x2, x3)]).astype(BF))
        start = pl.multiple_of(4 * PART_A + GROUP * i, 16)
        at = PART_A + PART_B
        out[at : at + GROUP, :] = total_of([r[pl.ds(start, GROUP), :] for r in (y0, y1, y2, y3)]).astype(BF)
        put_small(out, at + GROUP, small[...])


def own_kernel(place_ref, z0, z1, z2, z3, heads, bulk):
    parts = (z0, z1, z2, z3)
    for d, r in enumerate(parts):
        heads[GROUP * d : GROUP * d + GROUP, :] = r[PARTS : PARTS + GROUP, :]
    put_small(heads, 4 * GROUP, total_of([get_small(r, PARTS + GROUP) for r in parts]))
    bulk[0:PARTS, :] = total_of([r[0:PARTS, :] for r in parts]).astype(BF)
    bulk[PARTS:SPACE, :] = jnp.zeros((SPACE - PARTS, 128), BF)


def row_kernel(place_ref, y0, y1, y2, y3, out):
    for d, r in enumerate((y0, y1, y2, y3)):
        out[PARTS * d : PARTS * d + PARTS, :] = r[0:PARTS, :]


def head_row_kernel(place_ref, x0, x1, x2, x3, out):
    parts = (x0, x1, x2, x3)
    out[0 : 4 * GROUP, :] = total_of([r[0 : 4 * GROUP, :] for r in parts]).astype(BF)
    put_small(out, 4 * GROUP, total_of([get_small(r, 4 * GROUP) for r in parts]))


ALL_TINY = 16 * GROUP
ALL_BULK = ALL_TINY + TINY
ALL = ALL_BULK + 16 * PARTS


def stack_kernel(place_ref, y0, y1, y2, y3, x0, x1, x2, x3, out):
    parts = (y0, y1, y2, y3)
    put_small(out, ALL_TINY, total_of([get_small(r, 4 * GROUP) for r in parts]))
    for d, (r, b) in enumerate(zip(parts, (x0, x1, x2, x3))):
        out[4 * GROUP * d : 4 * GROUP * d + 4 * GROUP, :] = r[0 : 4 * GROUP, :]
        out[ALL_BULK + 4 * PARTS * d : ALL_BULK + 4 * PARTS * d + 4 * PARTS, :] = b[...]


def finish_kernel(place_ref, mine, other, grad_qkv, grad_out, grad_up, grad_down, gains, passes, pair, turned):
    z, x, y, core = place_ref[0], place_ref[1], place_ref[2], place_ref[3]
    pair[core] = mine[...]
    pair[1 - core] = other[...]

    def rows(c, at, count):
        return pair[c, pl.ds(pl.multiple_of(at, 16), count), :].astype(F32)

    for c in range(2):
        for xx in range(4):
            dx = lax.rem(x + 4 - xx, 4)
            for yy in range(4):
                dy = lax.rem(y + 4 - yy, 4)
                a = rows(c, ALL_BULK + 4 * PARTS * dx + PARTS * dy, PART_A)
                b = rows(c, ALL_BULK + 4 * PARTS * dx + PARTS * dy + PART_A, PART_B)
                r = 384 * c + 48 * (2 * yy + xx // 2)
                for t in range(3):
                    col = 384 * (2 * xx + c) + 128 * t
                    grad_up[48 * yy : 48 * yy + 48, col : col + 128] = a[48 * t : 48 * t + 48]
                    col = 384 * (xx % 2) + 128 * t
                    grad_down[r : r + 48, col : col + 128] = b[64 * t : 64 * t + 48]
                    if yy < 3:
                        n, col = 16 * (4 * yy + xx), 384 * c + 128 * t
                        grad_out[n : n + 16, col : col + 128] = b[64 * t + 48 : 64 * t + 64]
        for yy in range(4):
            dy = lax.rem(y + 4 - yy, 4)
            for j in range(4):
                dz = lax.rem(z + 4 - j, 4)
                piece = rows(c, 4 * GROUP * dy + GROUP * dz, GROUP)
                for at, *halves in units(4 * c + yy):
                    for side, (r, n) in enumerate(halves):
                        col = D * (n % 3) + 64 * (4 * (n // 3) + j)
                        grad_qkv[r : r + 16, col : col + 64] = piece[at : at + 16, 64 * side : 64 * side + 64]
    small = get_small(mine, ALL_TINY) + get_small(other, ALL_TINY)
    turned[...] = small.T
    part = turned[pl.ds(pl.multiple_of(192 * z, 8), 192), :]
    part = part.T
    gains[...] = part[0:2, :]
    passes[...] = part[2:7, :]


def layer_out_kernel(place_ref, middle, active, w_down, out, total):
    step = pl.program_id(0)

    @pl.when(step == 0)
    def _():
        total[...] = middle[...]

    total[...] += dot(active[...], w_down[...])

    @pl.when(step == FF // CHUNK - 1)
    def _():
        out[0] = total[0:ROWS, :].astype(BF)


def input_grad_kernel(blk_ref, a0, a1, a2, a3, w0, w1, w2, w3, w4, w5, out, stage):
    blk = blk_ref[0]
    for d, piece in enumerate((a0, a1, a2, a3)):
        s = lax.rem(blk + 4 - d, 4)
        for n in range(6):
            stage[n, s] = piece[64 * n : 64 * n + 64, :]
    total = jnp.zeros((D, R), F32)
    for n, weight in enumerate((w0, w1, w2, w3, w4, w5)):
        total = total + dot(weight[...], stage[n].reshape(256, R))
    out[...] = total


def last_kernel(
    blk_ref, count_ref, c0, c1, c2, c3, so_far, hidden, d_middle, gain_term, gains, wq, wk, wv, grad_stream, small, stage
):
    blk = blk_ref[0]
    for d, piece in enumerate((c0, c1, c2, c3)):
        s = lax.rem(blk + 4 - d, 4)
        for part in range(3):
            stage[part, s] = piece[64 * part : 64 * part + 64, :]
    turned = so_far[...]
    for part, weight in enumerate((wq, wk, wv)):
        turned = turned + dot(weight[...], stage[part].reshape(256, R))
    grad = turned.T
    unit, inverse = normalize(hidden[...])
    total = d_middle[...] + norm_back(grad, unit, inverse, gains[0:1, :])
    grad_stream[0] = total[0:ROWS, :]
    row = lax.broadcasted_iota(jnp.int32, (R, 1), 0)
    which = jnp.where(row < ROWS, pass_index(blk, count_ref[0]), -1)
    small[0:1, :] = jnp.sum(grad * unit, axis=0, keepdims=True)
    small[1:2, :] = gain_term[...]
    for r in range(PASSES):
        small[2 + r : 3 + r, :] = jnp.sum(jnp.where(which == r, total, 0.0), axis=0, keepdims=True)
    small[7:8, :] = jnp.zeros((1, D), F32)


def shift(values, axis, d):
    if axis == "z":
        return lax.ppermute(values, "blk", [(i, (i + d) % 4) for i in range(4)])
    pairs = []
    for b in range(32):
        y, x, core = b // 8, (b // 2) % 4, b % 2
        if axis == "y":
            y = (y + d) % 4
        elif axis == "x":
            x = (x + d) % 4
        else:
            core = (core + d) % 2
        pairs.append((b, 8 * y + 2 * x + core))
    return lax.ppermute(values, "batch", pairs)


def spread_pieces(pieces, axis):
    two, three, one = (shift(pieces[d], axis, d) for d in (2, 3, 1))
    return (pieces[0], one, two, three)


def all_of(value, axis):
    return spread_pieces((value,) * 4, axis)


def after(value, *others):
    return lax.optimization_barrier((value,) + others)[0]


def far(value):
    return pltpu.with_memory_space_constraint(value, pltpu.HBM)


def weight_spec(column):
    return pl.BlockSpec((D, 256), lambda *_, column=column: (0, column))


def on_device(stream, cotangent, passes, w_qkv, w_out, w_up, w_down, ln_gains, pass_embed):
    z = lax.axis_index("blk").astype(jnp.int32)
    batch = lax.axis_index("batch").astype(jnp.int32)
    place = jnp.stack([z, batch // 2 % 4, batch // 8, batch % 2])
    gains = ln_gains.T
    embed = pass_embed.T
    piece = shape((192, R))
    full = shape((R, D))

    def arrived(*values):
        nonlocal place
        place = lax.optimization_barrier((place,) + values)[0]

    def ordered(outs):
        nonlocal place
        *outs, first = outs
        place, first = lax.optimization_barrier((place, first))
        return (*outs, first)

    hidden, turned, *early, normed = ordered(pl.pallas_call(
        first_kernel,
        grid=(1,),
        in_specs=[SM, SM, VM, VM, VM, weight_spec(0), weight_spec(3), weight_spec(6)],
        out_specs=[VM] * 7,
        out_shape=[kept((R, D), F32), kept((D, R)), piece, piece, piece, piece, full],
        scratch_shapes=[pltpu.VMEM((4, 192, R), BF)],
        compiler_params=room(24),
        name="ln_qkv",
    )(place, passes, far(stream), far(embed), far(gains), *([far(w_qkv)] * 3)))
    sent = ordered(pl.pallas_call(
        second_kernel,
        grid=(1,),
        in_specs=[SM, VM] + [weight_spec(c) for c in (1, 4, 7, 2, 5, 8)],
        out_specs=[VM] * 8,
        out_shape=[piece] * 8,
        scratch_shapes=[pltpu.VMEM((2, 4, 192, R), BF)],
        compiler_params=room(24),
        name="qkv_rest",
    )(place, normed, *([far(w_qkv)] * 6)))
    heads = [spread_pieces(early, "z"), spread_pieces(sent[0:4], "z")]
    last_group = [sent[4], shift(sent[5], "z", 1), sent[6], shift(sent[7], "z", 3)]

    wholes, attended, spreads, sent = [], [], [], []
    for g in range(3):
        *parts, whole, result, spread = ordered(run(
            lambda *refs, g=g: attend_kernel(g == 2, *refs),
            "attend",
            24,
            [shape((192 if g == 2 else HD, R))] * 4
            + [kept((4, 192, R)), kept((4, HD, R), F32), kept((4, 1, R), F32)],
            (place, *heads[g], *(sent if g == 2 else ())),
            [
                pltpu.VMEM((4, 128, R), BF),
                pltpu.VMEM((4, 128, R), BF),
                pltpu.VMEM((4, HD, R), BF),
                pltpu.VMEM((4, R, 128), BF),
                pltpu.VMEM((4, R, R), F32),
                pltpu.VMEM((4, HD, R), BF),
            ],
        ))
        if g == 0:
            last_group[2] = shift(after(last_group[2], place), "z", 2)
            heads.append(last_group)
        wholes.append(whole)
        attended.append(result)
        spreads.append(spread)
        sent += parts
    sent = sent[8:]
    back_o = spread_pieces(sent, "z")
    d_active = ordered((pl.pallas_call(
        active_grad_kernel,
        grid=(FF // CHUNK,),
        in_specs=[SM, VM, pl.BlockSpec((CHUNK, D), lambda f: (f, 0))],
        out_specs=pl.BlockSpec((R, CHUNK), lambda f: (0, f)),
        out_shape=kept((R, FF), F32),
        scratch_shapes=[pltpu.VMEM((R, D), BF), pltpu.VMEM((R, D), F32)],
        compiler_params=room(16),
        name="active_grad",
    )(place, far(cotangent), far(w_down)),))[0]
    near = after(turned, place, *back_o)
    near = (shift(near, "z", 1), shift(near, "z", 3))

    active, d_up, second, middle, o_turned, d_branch, d_middle, *sent, a_other, b_other, gain_term = ordered(pl.pallas_call(
        ff_kernel,
        grid=(FF // CHUNK,),
        in_specs=[SM] + [VM] * 4 + [VM, VM, VM, VM]
        + [pl.BlockSpec((D, CHUNK), lambda f: (0, f)), pl.BlockSpec((R, CHUNK), lambda f: (0, f))],
        out_specs=[VM] * 14,
        out_shape=[shape((R, FF)), shape((R, FF)), full, shape((R, D), F32), shape((D, R)), full, kept((R, D), F32)]
        + [kept((192, R))] + [piece] * 3 + [shape((4, 4, 4, 48, 384)), shape((4, 4, 4, 64, 384)), shape((1, D), F32)],
        scratch_shapes=[pltpu.VMEM((R, D), BF), pltpu.VMEM((R, D), F32), pltpu.VMEM((HEADS, HD, R), BF), pltpu.VMEM((D, R), BF)],
        compiler_params=room(36),
        name="ff",
    )(place, *back_o, hidden, cotangent, gains, w_out, far(w_up), far(d_active)))
    *sent, a_other, b_other = lax.optimization_barrier((*sent, a_other, b_other, *near))[:6]
    d_o = spread_pieces(sent, "z")

    got = (shift(a_other, "core", 1), shift(b_other, "core", 1))
    own = ordered(run(
        ff_grad_kernel,
        "ff_grad",
        32,
        [shape((4, 4, 4, 48, 384)), shape((4, 4, 4, 64, 384))],
        (place, active, d_up, second, far(cotangent), o_turned, d_branch),
        [pltpu.VMEM((R, D), F32)],
    ))
    sent = ordered(run(
        core_sum_kernel,
        "core_sum",
        24,
        [kept((4, 4, 48, 384))] + [shape((4, 4, 48, 384))] * 3 + [kept((4, 4, 64, 384))] + [shape((4, 4, 64, 384))] * 3,
        (place, *own, *got),
    ))
    arrived(*d_o)
    distant = shift(after(turned, *d_o, place), "z", 2)
    a_sent, b_sent = sent[0:4], sent[4:8]
    a_parts = [a_sent[0], shift(a_sent[1], "x", 1), None, shift(a_sent[3], "x", 3)]
    b_parts = [b_sent[0], shift(b_sent[1], "y", 1), None, shift(b_sent[3], "y", 3)]

    def attend_back(which):
        count = len(which)
        group = pl.BlockSpec((64 * count, R), lambda _: (which[0] // count, 0))
        operands = [t for g in which for t in (wholes[g], attended[g], spreads[g])]
        return ordered(pl.pallas_call(
            lambda *refs: attend_back_kernel(count, *refs),
            grid=(1,),
            in_specs=[SM] + [VM] * (3 * count) + [group] * 4,
            out_specs=[VM] * 5,
            out_shape=[kept((192 * count, R))] + [shape((192 * count, R))] * 3 + [kept((count, 4, 192, R))],
            scratch_shapes=[
                pltpu.VMEM((count, 4, 128, R), BF),
                pltpu.VMEM((count, 4, 128, R), BF),
                pltpu.VMEM((count, 4, HD, R), BF),
                pltpu.VMEM((count, 4, R, 128), BF),
                pltpu.VMEM((count, 4, R, 128), BF),
                pltpu.VMEM((count, 4, R, HD), BF),
                pltpu.VMEM((count, 4, HD, R), BF),
                pltpu.VMEM((count, 4, R, HD), BF),
                pltpu.VMEM((count, 4, 1, R), F32),
                pltpu.VMEM((count, 4, HD, R), F32),
            ],
            compiler_params=room(32 if count == 2 else 24),
            name="attend_back",
        )(place, *(far(t) for t in operands), *(far(t) for t in d_o)))

    *sent, made_first = attend_back((0, 1))
    first_pieces = spread_pieces(sent, "z")
    a_parts[2] = shift(after(a_sent[2], place), "x", 2)
    b_parts[2] = shift(after(b_sent[2], place), "y", 2)
    arrived(a_parts[1], a_parts[3], b_parts[1], b_parts[3], distant)
    *sent, made_last = attend_back((2,))
    keep, send = ordered(run(
        head_grad_kernel,
        "head_grad",
        32,
        [shape((4, 4, GROUP, 128))] * 2,
        (place, far(turned), far(near[0]), far(distant), far(near[1]), far(made_first), far(made_last)),
        [pltpu.VMEM((4, 640, R), BF), pltpu.VMEM((D, 640), F32), pltpu.VMEM((8, 4, GROUP, 128), BF)],
    ))
    arrived(*first_pieces, a_parts[2], b_parts[2])
    *sent, send = lax.optimization_barrier((*sent, send, *first_pieces, a_parts[2], b_parts[2]))[:5]
    last_pieces = spread_pieces(sent, "z")
    got = shift(send, "core", 1)

    sent = ordered(run(
        cut_kernel,
        "sum_first",
        24,
        [shape((4 * PART_A + 4 * GROUP, 128))] * 4 + [shape((4, 64, 384))] * 4,
        (place, *a_parts, *b_parts, keep, got),
    ))
    so_far = ordered((pl.pallas_call(
        input_grad_kernel,
        grid=(1,),
        in_specs=[SM] + [VM] * 4 + [weight_spec(c) for c in (0, 3, 6, 1, 4, 7)],
        out_specs=VM,
        out_shape=shape((D, R), F32),
        scratch_shapes=[pltpu.VMEM((6, 4, HD, R), BF)],
        compiler_params=room(24),
        name="input_grad",
    )(place, *first_pieces, *([far(w_qkv)] * 6)),))[0]
    own_y, *others = lax.optimization_barrier((*sent, place))[:8]
    y_parts, x_parts = spread_pieces([own_y, *others[0:3]], "y"), spread_pieces(others[3:7], "x")
    grad_stream, small = ordered(pl.pallas_call(
        last_kernel,
        grid=(1,),
        in_specs=[SM, SM] + [VM] * 9 + [weight_spec(c) for c in (2, 5, 8)],
        out_specs=[VM, VM],
        out_shape=[kept((1, ROWS, D), F32), shape((8, D), F32)],
        scratch_shapes=[pltpu.VMEM((3, 4, HD, R), BF)],
        compiler_params=room(24),
        name="ln_back",
    )(place, passes, *last_pieces, so_far, hidden, d_middle, gain_term, gains, *([far(w_qkv)] * 3)))
    sent = ordered(run(
        block_kernel,
        "sum_second",
        16,
        [shape((PART_A + PART_B + GROUP + TINY, 128))] * 4,
        (place, *y_parts, *x_parts, small),
    ))
    z_parts = spread_pieces(sent, "z")
    layer_out = ordered((pl.pallas_call(
        layer_out_kernel,
        grid=(FF // CHUNK,),
        in_specs=[SM, VM, pl.BlockSpec((R, CHUNK), lambda f: (0, f)), pl.BlockSpec((CHUNK, D), lambda f: (f, 0))],
        out_specs=VM,
        out_shape=kept((1, ROWS, D)),
        scratch_shapes=[pltpu.VMEM((R, D), F32)],
        compiler_params=room(16),
        name="layer_out",
    )(place, middle, active, far(w_down)),))[0]
    head, bulk = ordered(run(
        own_kernel, "sum_blocks", 16, [shape((4 * GROUP + TINY, 128)), shape((SPACE, 128))], (place, *z_parts)
    ))
    bulks = all_of(bulk, "y")
    heads_x = all_of(head, "x")
    row = ordered(run(row_kernel, "stack_rows", 16, [shape((4 * PARTS, 128))], (place, *bulks)))[0]
    rows = [row, shift(row, "x", 1), None, shift(row, "x", 3)]
    head = ordered(run(head_row_kernel, "sum_heads", 16, [shape((4 * GROUP + TINY, 128))], (place, *heads_x)))[0]
    rows[2] = shift(after(row, place), "x", 2)
    heads_y = spread_pieces((head, head, after(head, rows[3]), head), "y")
    buffer = ordered(run(stack_kernel, "stack", 16, [shape((ALL, 128))], (place, *heads_y, *rows)))[0]
    *results, grad_gains, grad_pass = run(
        finish_kernel,
        "finish",
        32,
        [
            kept((192, 3 * D), F32),
            kept((192, D), F32),
            kept((192, FF), F32),
            kept((D, D), F32),
            shape((2, 192), F32),
            shape((PASSES, 192), F32),
        ],
        (place, buffer, shift(buffer, "core", 1)),
        [pltpu.VMEM((2, ALL, 128), BF), pltpu.VMEM((D, 8), F32)],
    )
    return (layer_out, grad_stream, *results, grad_gains.T, grad_pass.T)


def solution(mesh):
    tokens = P("batch", "blk", None)
    in_specs = (tokens, tokens, P("batch"), P(), P(), P(), P(), P(), P())
    out_specs = (tokens, tokens) + (P("blk", None),) * 6
    return jax.shard_map(on_device, mesh=mesh, in_specs=in_specs, out_specs=out_specs, check_vma=False)
```

```python
import jax
import jax.numpy as jnp
from jax import lax
from jax.experimental import pallas as pl
from jax.experimental.pallas import tpu as pltpu
from jax.sharding import PartitionSpec as P

D = 768
HEADS = 12
HD = 64
FF = 3072
PASSES = 5
ROWS = 510
R = 512
EPS = 1e-05
NEG = -1e30
BF = jnp.bfloat16
F32 = jnp.float32
VM = pl.BlockSpec(memory_space=pltpu.VMEM)
SM = pl.BlockSpec(memory_space=pltpu.SMEM)
HB = pl.BlockSpec(memory_space=pl.ANY)
MIB = 1024 * 1024


def room(mib):
    return pltpu.CompilerParams(vmem_limit_bytes=mib * MIB)


def run(kernel, name, mib, outs, operands, scratch=(), scalars=1):
    return pl.pallas_call(
        kernel,
        in_specs=[SM] * scalars + [VM] * (len(operands) - scalars),
        out_specs=[VM] * len(outs),
        out_shape=outs,
        scratch_shapes=list(scratch),
        compiler_params=room(mib),
        name=name,
    )(*operands)


def shape(dims, kind=BF):
    return jax.ShapeDtypeStruct(dims, kind)


def kept(dims, kind=BF):
    return pltpu.HBM(dims, kind)


def dot(left, right):
    return jnp.dot(left, right, preferred_element_type=F32)


def dot_nt(left, right):
    return lax.dot_general(left, right, (((1,), (1,)), ((), ())), preferred_element_type=F32)


def normalize(values):
    mean = jnp.mean(values, axis=-1, keepdims=True)
    centred = values - mean
    inverse = lax.rsqrt(jnp.mean(centred * centred, axis=-1, keepdims=True) + EPS)
    return centred * inverse, inverse


def norm_back(grad, unit, inverse, gain):
    scaled = grad * gain
    first = jnp.mean(scaled, axis=-1, keepdims=True)
    second = jnp.mean(scaled * unit, axis=-1, keepdims=True)
    return inverse * (scaled - first - unit * second)


def pass_index(blk, count):
    row = lax.broadcasted_iota(jnp.int32, (R, 1), 0) + blk * ROWS
    turns = jnp.floor((row.astype(F32) + 0.5) / count.astype(F32)).astype(jnp.int32)
    return row - turns * count


def pieces_out(stage, outs, blk):
    for d, out in enumerate(outs):
        out[...] = stage[lax.rem(blk + d, 4)]


def project(normed, weights, stage, outs, blk):
    for part, weight in enumerate(weights):
        got = dot(normed, weight[...])
        if part == 0:
            got = got.astype(BF) * jnp.asarray(HD ** (-0.5), BF)
        turned = got.astype(BF).T
        for j in range(4):
            stage[j, 64 * part : 64 * part + 64, :] = turned[64 * j : 64 * j + 64]
    pieces_out(stage, outs, blk)


def project(normed, weights, stage):
    for part, weight in enumerate(weights):
        got = dot(normed, weight[...])
        if part == 0:
            got = got.astype(BF) * jnp.asarray(HD ** (-0.5), BF)
        flipped = got.astype(BF).T
        for j in range(4):
            stage[j, 64 * part : 64 * part + 64, :] = flipped[64 * j : 64 * j + 64]


def first_kernel(blk_ref, count_ref, stream, embed, gains, wq, wk, wv, hidden, turned, p0, p1, p2, p3, normed, stage):
    blk = blk_ref[0]
    hidden[R - 8 : R, :] = jnp.zeros((8, D), F32)
    hidden[0:ROWS, :] = stream[0].astype(F32)
    which = pass_index(blk, count_ref[0])
    added = embed[0:1, :]
    for r in range(1, PASSES):
        added = jnp.where(which == r, embed[r : r + 1, :], added)
    values = hidden[...] + added
    hidden[...] = values
    unit, _ = normalize(values)
    row = lax.broadcasted_iota(jnp.int32, (R, 1), 0)
    low = jnp.where(row < ROWS, unit * gains[0:1, :], 0.0).astype(BF)
    normed[...] = low
    project(low, (wq, wk, wv), stage)
    for d, out in enumerate((p0, p1, p2, p3)):
        out[...] = stage[lax.rem(blk + d, 4)]
    turned[...] = low.T


def second_kernel(blk_ref, normed, wq1, wk1, wv1, wq2, wk2, wv2, p0, p1, p2, p3, q0, q1, q2, q3, stage):
    blk = blk_ref[0]
    for n, (weights, outs) in enumerate((((wq1, wk1, wv1), (p0, p1, p2, p3)), ((wq2, wk2, wv2), (q0, q1, q2, q3)))):
        project(normed[...], weights, stage.at[n])
        for d, out in enumerate(outs):
            out[...] = stage[n, lax.rem(blk + d, 4)]


def load_heads(whole, q_rows, k_rows, v_rows, k_cols):
    for s in range(4):
        q_rows[s, 0:64, :] = whole[s, 0:64, :]
        k_rows[s, 0:64, :] = whole[s, 64:128, :]
        v_rows[s] = whole[s, 128:192, :]
    row = lax.broadcasted_iota(jnp.int32, (64, R), 0)
    col = lax.broadcasted_iota(jnp.int32, (64, R), 1)
    one = jnp.where(row == 0, 1.0, 0.0).astype(BF)
    off = jnp.where((row == 0) & (col >= ROWS), NEG, 0.0).astype(BF)
    for s in range(4):
        q_rows[s, 64:128, :] = one
        k_rows[s, 64:128, :] = off
    for s in range(4):
        k_cols[s] = k_rows[s].T


HALF = R // 2


def causal(keys, queries):
    key = lax.broadcasted_iota(jnp.int32, (keys, queries), 0)
    query = lax.broadcasted_iota(jnp.int32, (keys, queries), 1)
    return key <= query


def attend_kernel(last, blk_ref, r0, r1, r2, r3, *rest):
    earlier, rest = (rest[:8], rest[8:]) if last else ((), rest)
    p0, p1, p2, p3, whole, attended, spread, q_rows, k_rows, v_rows, k_cols, scores, stage = rest
    blk = blk_ref[0]
    for d, piece in enumerate((r0, r1, r2, r3)):
        whole[lax.rem(blk + 4 - d, 4)] = piece[...]
    load_heads(whole, q_rows, k_rows, v_rows, k_cols)
    for i in range(4):
        low = jnp.where(causal(HALF, R), dot(k_cols[i, 0:HALF, :], q_rows[i]), NEG)
        high = jnp.where(causal(HALF, HALF), dot(k_cols[i, HALF:R, :], q_rows[i, :, HALF:R]), NEG)
        top = jnp.max(low, axis=0, keepdims=True)
        right = jnp.maximum(top[:, HALF:R], jnp.max(high, axis=0, keepdims=True))
        top = jnp.concatenate([top[:, 0:HALF], right], axis=1)
        for j in range(i):
            got = dot(k_cols[j], q_rows[i])
            scores[j] = got
            top = jnp.maximum(top, jnp.max(got, axis=0, keepdims=True))
        low = jnp.exp(low - top)
        high = jnp.exp(high - top[:, HALF:R])
        total = jnp.sum(low, axis=0, keepdims=True)
        summed = dot(v_rows[i, :, 0:HALF], low.astype(BF))
        right = total[:, HALF:R] + jnp.sum(high, axis=0, keepdims=True)
        total = jnp.concatenate([total[:, 0:HALF], right], axis=1)
        right = summed[:, HALF:R] + dot(v_rows[i, :, HALF:R], high.astype(BF))
        summed = jnp.concatenate([summed[:, 0:HALF], right], axis=1)
        for j in range(i):
            raised = jnp.exp(scores[j] - top)
            total = total + jnp.sum(raised, axis=0, keepdims=True)
            summed = summed + dot(v_rows[j], raised.astype(BF))
        result = summed / total
        attended[i] = result
        spread[i] = top + jnp.log(total)
        stage[i] = result.astype(BF)
    at = 128 if last else 0
    for d, out in enumerate((p0, p1, p2, p3)):
        out[at : at + 64, :] = stage[lax.rem(blk + d, 4)]
        if last:
            out[0:64, :] = earlier[d][...]
            out[64:128, :] = earlier[4 + d][...]


def attend_back_head(blk, whole, back, attended, spread, outs, scratch):
    q_rows, k_rows, v_rows, k_cols, q_cols, v_cols, o_rows, o_cols, delta, dq = scratch
    load_heads(whole, q_rows, k_rows, v_rows, k_cols)
    for d, piece in enumerate(back):
        o_rows[lax.rem(blk + 4 - d, 4)] = piece
    for s in range(4):
        q_cols[s] = q_rows[s].T
        v_cols[s] = v_rows[s].T
        o_cols[s] = o_rows[s].T
        delta[s] = jnp.sum(o_rows[s].astype(F32) * attended[s], axis=0, keepdims=True)
        dq[s] = jnp.zeros((HD, R), F32)
    for j in range(4):
        dk = jnp.zeros((R, 2 * HD), F32)
        dv = jnp.zeros((R, HD), F32)
        for i in range(j, 4):
            got = dot(k_cols[j], q_rows[i])
            if i == j:
                got = jnp.where(causal(R, R), got, NEG)
            probs = jnp.exp(got - spread[i])
            d_probs = dot(v_cols[j], o_rows[i])
            d_scores = (probs * (d_probs - delta[i])).astype(BF)
            dv = dv + dot(probs.astype(BF), o_cols[i])
            dk = dk + dot(d_scores, q_cols[i])
            dq[i] = dq[i] + dot(k_rows[j, 0:64, :], d_scores)
        outs[j, 0:64, :] = (dq[j] * HD ** (-0.5)).astype(BF)
        outs[j, 64:128, :] = dk[:, 0:64].astype(BF).T
        outs[j, 128:192, :] = dv.astype(BF).T


def attend_back_kernel(count, blk_ref, *refs):
    blk = blk_ref[0]
    sources = [refs[3 * h : 3 * h + 3] for h in range(count)]
    back, rest = refs[3 * count : 3 * count + 4], refs[3 * count + 4 :]
    pieces, outs, scratch = rest[0:4], rest[4], rest[5:]
    for h, (whole, attended, spread) in enumerate(sources):
        grads = [piece[64 * h : 64 * h + 64, :] for piece in back]
        attend_back_head(blk, whole, grads, attended, spread, outs.at[h], [ref.at[h] for ref in scratch])
        for d, out in enumerate(pieces):
            out[192 * h : 192 * h + 192, :] = outs[h, lax.rem(blk + d, 4)]


def units(piece):
    for n in range(7):
        u = 7 * piece + n
        if u < 48:
            yield 16 * n, (16 * (u // 4), 2 * (u % 4)), (16 * (u // 4), 2 * (u % 4) + 1)
        elif u < 54:
            yield 16 * n, (32 * (u - 48), 8), (32 * (u - 48) + 16, 8)


def head_grad_kernel(place_ref, t0, t1, t2, t3, e01, e2, keep, send, sides, made, pieces):
    blk, core = place_ref[0], place_ref[3]
    total = jnp.zeros((D, 640), F32)
    for d, piece in enumerate((t0, t1, t2, t3)):
        s = lax.rem(blk + 4 - d, 4)
        for g, side in enumerate((e01.at[0], e01.at[1], e2.at[0])):
            sides[d, 192 * g : 192 * g + 192, :] = side[s]
        sides[d, 576:640, :] = jnp.zeros((64, R), BF)
        total = total + dot_nt(piece[...], sides[d])
    made[...] = total
    pieces[...] = jnp.zeros((8, 4, GROUP, 128), BF)
    for k in range(8):
        for at, (row, left), (row_right, right) in units(k):
            for i in range(4):
                r = 192 * i + row
                if right == left:
                    halves = (made[r : r + 16, 512:576], made[r + 16 : r + 32, 512:576])
                    block = jnp.concatenate(halves, axis=1)
                else:
                    block = made[r : r + 16, 64 * left : 64 * left + 128]
                pieces[k, i, at : at + 16, :] = block.astype(BF)
    for q in range(4):
        keep[q] = pieces[4 * core + q]
        send[q] = pieces[4 * (1 - core) + q]


def gelu_both(value):
    c = (2.0 / jnp.pi) ** 0.5
    square = value * value
    t = jnp.tanh(c * value * (1.0 + 0.044715 * square))
    cdf = 0.5 * (1.0 + t)
    slope = cdf + (0.5 * c) * value * (1.0 - t * t) * (1.0 + 3.0 * 0.044715 * square)
    return value * cdf, slope


CHUNK = 768


def active_grad_kernel(place_ref, cot, w_down, out, dy, pad):
    @pl.when(pl.program_id(0) == 0)
    def _():
        pad[R - 8 : R, :] = jnp.zeros((8, D), F32)
        pad[0:ROWS, :] = cot[0].astype(F32)
        dy[...] = pad[...].astype(BF)

    out[...] = dot_nt(dy[...], w_down[...])


def up_cut(values, store):
    for z in range(4):
        for yy in range(4):
            store(yy, z, values[192 * z + 48 * yy : 192 * z + 48 * yy + 48, :])


def down_cut(values, store):
    for yy in range(4):
        for xx in range(4):
            r, col = 48 * (2 * yy + xx // 2), 384 * (xx % 2)
            store(yy, xx, values[r : r + 48, col : col + 384])


def out_cut(values, out):
    for i in range(4):
        for n in range(16):
            rows = values[192 * i + 16 * n : 192 * i + 16 * n + 16, :] if n < 12 else jnp.zeros((16, 384), BF)
            out[n // 4, n % 4, i, 48:64] = rows


def put_block(out, at, rows):
    out[at] = rows.astype(BF)


def ff_kernel(
    blk_ref, r0, r1, r2, r3, hidden, cot, gains, w_out, w_up, d_active,
    active, d_up, second, middle, o_turned, d_branch, d_middle, p0, p1, p2, p3, a_out, b_out, gain_term,
    dy, back, stage, second_turned,
):
    step = pl.program_id(0)
    core = blk_ref[3]

    @pl.when(step == 0)
    def _():
        blk = blk_ref[0]
        for d, piece in enumerate((r0, r1, r2, r3)):
            s = lax.rem(blk + 4 - d, 4)
            for g in range(3):
                stage[4 * g + s] = piece[64 * g : 64 * g + 64, :]
        o_rows = stage[...].reshape(D, R)
        o_turned[...] = o_rows
        values = hidden[...] + dot(o_rows.T, w_out[...])
        middle[...] = values
        unit, _ = normalize(values)
        second[...] = (unit * gains[1:2, :]).astype(BF)
        back[R - 8 : R, :] = jnp.zeros((8, D), F32)
        back[0:ROWS, :] = cot[0].astype(F32)
        dy[...] = back[...].astype(BF)
        back[...] = jnp.zeros((R, D), F32)
        second_turned[...] = second[...].T

    upward = dot(second[...], w_up[...])
    act, slope = gelu_both(upward)
    act = act.astype(BF)
    at = pl.ds(pl.multiple_of(step * CHUNK, 128), CHUNK)
    active[:, at] = act
    d_upward = (d_active[...] * slope).astype(BF)
    d_up[:, at] = d_upward
    back[...] += dot_nt(d_upward, w_up[...])

    first = core == 0
    other_up = jnp.where(first, d_upward[:, 384:768], d_upward[:, 0:384])
    other_act = jnp.where(first, act[:, 384:768], act[:, 0:384])
    up_cut(dot(second_turned[...], other_up), lambda yy, z, rows: put_block(a_out, (yy, step, z), rows))
    down_cut(dot(other_act.T, dy[...]), lambda yy, xx, rows: put_block(b_out, (yy, xx, step, slice(0, 48)), rows))

    @pl.when(step == FF // CHUNK - 1)
    def _():
        blk = blk_ref[0]
        unit, inverse = normalize(middle[...])
        grad = back[...]
        gain_term[...] = jnp.sum(grad * unit, axis=0, keepdims=True)
        total = dy[...].astype(F32) + norm_back(grad, unit, inverse, gains[1:2, :])
        d_middle[...] = total
        low = total.astype(BF)
        d_branch[...] = low
        stage[...] = dot_nt(w_out[...], low).astype(BF).reshape(HEADS, HD, R)
        out_cut(dot(o_turned[...], jnp.where(core == 0, low[:, 384:768], low[:, 0:384])).astype(BF), b_out)
        for d, out in enumerate((p0, p1, p2, p3)):
            j = lax.rem(blk + d, 4)
            for g in range(3):
                out[64 * g : 64 * g + 64, :] = stage[4 * g + j]


def ff_grad_kernel(place_ref, active, d_up, second, cot, o_turned, d_branch, a_out, b_out, pad):
    first = place_ref[3] == 0
    pad[R - 8 : R, :] = jnp.zeros((8, D), F32)
    pad[0:ROWS, :] = cot[0].astype(F32)
    dy = pad[...].astype(BF)
    second_turned = second[...].T

    def half(ref, i):
        return jnp.where(first, ref[:, 768 * i : 768 * i + 384], ref[:, 768 * i + 384 : 768 * i + 768])

    out_cut(dot(o_turned[...], half(d_branch, 0)).astype(BF), b_out)
    for pair in ((0, 1), (2, 3)):
        up = dot(second_turned, jnp.concatenate([half(d_up, i) for i in pair], axis=1))
        down = dot(jnp.concatenate([half(active, i).T for i in pair], axis=0), dy)
        for n, i in enumerate(pair):
            up_cut(up[:, 384 * n : 384 * n + 384], lambda yy, z, rows: put_block(a_out, (yy, i, z), rows))
            down_cut(down[384 * n : 384 * n + 384], lambda yy, xx, rows: put_block(b_out, (yy, xx, i, slice(0, 48)), rows))


def core_sum_kernel(place_ref, a_mine, b_mine, a_got, b_got, a0, a1, a2, a3, b0, b1, b2, b3):
    x, y = place_ref[1], place_ref[2]
    for d, (a_out, b_out) in enumerate(((a0, b0), (a1, b1), (a2, b2), (a3, b3))):
        xx, yy = lax.rem(x + d, 4), lax.rem(y + d, 4)
        for n in range(4):
            a_out[n] = (a_mine[n, xx].astype(F32) + a_got[n, xx].astype(F32)).astype(BF)
            b_out[n] = (b_mine[yy, n].astype(F32) + b_got[yy, n].astype(F32)).astype(BF)


def total_of(parts):
    return (parts[0].astype(F32) + parts[2].astype(F32)) + (parts[1].astype(F32) + parts[3].astype(F32))


TINY = 96
GROUP = 112
PART_A = 144
PART_B = 192
PARTS = PART_A + PART_B


def put(buffer, at, block):
    rows, lanes = block.shape
    for t in range(lanes // 128):
        buffer[at + rows * t : at + rows * t + rows, :] = block[:, 128 * t : 128 * t + 128]


def put_small(buffer, at, value):
    high = value.astype(BF)
    low = (value - high.astype(F32)).astype(BF)
    put(buffer, at, jnp.concatenate([high, low], axis=0))


def get_small(buffer, at):
    parts = []
    for t in range(6):
        part = buffer[at + 16 * t : at + 16 * t + 16, :].astype(F32)
        parts.append(part[0:8] + part[8:16])
    return jnp.concatenate(parts, axis=1)


def take(buffer, at, rows):
    return jnp.concatenate([buffer[at + rows * t : at + rows * t + rows, :] for t in range(3)], axis=1)


def cut_kernel(place_ref, a0, a1, a2, a3, b0, b1, b2, b3, keep, got, y0, y1, y2, y3, x0, x1, x2, x3):
    x, y = place_ref[1], place_ref[2]
    for d, (y_out, x_out) in enumerate(((y0, x0), (y1, x1), (y2, x2), (y3, x3))):
        yy, xx = lax.rem(y + d, 4), lax.rem(x + d, 4)
        a_sum = total_of([r[yy] for r in (a0, a1, a2, a3)]).astype(BF)
        heads = (keep[yy].astype(F32) + got[yy].astype(F32)).astype(BF)
        for i in range(4):
            put(y_out, PART_A * i, a_sum[i])
            y_out[4 * PART_A + GROUP * i : 4 * PART_A + GROUP * i + GROUP, :] = heads[i]
        x_out[...] = total_of([r[xx] for r in (b0, b1, b2, b3)]).astype(BF)


def block_kernel(place_ref, y0, y1, y2, y3, x0, x1, x2, x3, small, o0, o1, o2, o3):
    z = place_ref[0]
    for d, out in enumerate((o0, o1, o2, o3)):
        i = lax.rem(z + d, 4)
        start = pl.multiple_of(PART_A * i, 16)
        out[0:PART_A, :] = total_of([r[pl.ds(start, PART_A), :] for r in (y0, y1, y2, y3)]).astype(BF)
        put(out, PART_A, total_of([r[i] for r in (x0, x1, x2, x3)]).astype(BF))
        start = pl.multiple_of(4 * PART_A + GROUP * i, 16)
        at = PART_A + PART_B
        out[at : at + GROUP, :] = total_of([r[pl.ds(start, GROUP), :] for r in (y0, y1, y2, y3)]).astype(BF)
        put_small(out, at + GROUP, small[...])


def own_kernel(place_ref, z0, z1, z2, z3, heads, bulk):
    parts = (z0, z1, z2, z3)
    for d, r in enumerate(parts):
        heads[GROUP * d : GROUP * d + GROUP, :] = r[PARTS : PARTS + GROUP, :]
    put_small(heads, 4 * GROUP, total_of([get_small(r, PARTS + GROUP) for r in parts]))
    bulk[...] = total_of([r[0:PARTS, :] for r in parts]).astype(BF)


def row_kernel(place_ref, y0, y1, y2, y3, out):
    for d, r in enumerate((y0, y1, y2, y3)):
        out[PARTS * d : PARTS * d + PARTS, :] = r[...]


def head_row_kernel(place_ref, x0, x1, x2, x3, out):
    parts = (x0, x1, x2, x3)
    out[0 : 4 * GROUP, :] = total_of([r[0 : 4 * GROUP, :] for r in parts]).astype(BF)
    put_small(out, 4 * GROUP, total_of([get_small(r, 4 * GROUP) for r in parts]))


ALL_TINY = 16 * GROUP
ALL_BULK = ALL_TINY + TINY
ALL = ALL_BULK + 16 * PARTS


def stack_kernel(place_ref, y0, y1, y2, y3, x0, x1, x2, x3, out):
    parts = (y0, y1, y2, y3)
    put_small(out, ALL_TINY, total_of([get_small(r, 4 * GROUP) for r in parts]))
    for d, (r, b) in enumerate(zip(parts, (x0, x1, x2, x3))):
        out[4 * GROUP * d : 4 * GROUP * d + 4 * GROUP, :] = r[0 : 4 * GROUP, :]
        out[ALL_BULK + 4 * PARTS * d : ALL_BULK + 4 * PARTS * d + 4 * PARTS, :] = b[...]


def finish_kernel(place_ref, mine, other, grad_qkv, grad_out, grad_up, grad_down, gains, passes, pair, turned):
    z, x, y, core = place_ref[0], place_ref[1], place_ref[2], place_ref[3]

    @pl.when(pl.program_id(0) == 0)
    def _():
        pair[core] = mine[...]
        pair[1 - core] = other[...]
        small = get_small(mine, ALL_TINY) + get_small(other, ALL_TINY)
        turned[...] = small.T
        part = turned[pl.ds(pl.multiple_of(192 * z, 8), 192), :].T
        gains[...] = part[0:2, :]
        passes[...] = part[2:7, :]

    def rows(c, at, count):
        return pair[c, pl.ds(pl.multiple_of(at, 16), count), :].astype(F32)

    for step in range(2):
        @pl.when(pl.program_id(0) == step)
        def _():
            for c in range(2):
                for xx in range(4):
                    dx = lax.rem(x + 4 - xx, 4)
                    for yy in range(4):
                        dy = lax.rem(y + 4 - yy, 4)
                        at = ALL_BULK + 4 * PARTS * dx + PARTS * dy
                        if yy // 2 == step:
                            a, r = rows(c, at, PART_A), 48 * (yy % 2)
                            for t in range(3):
                                col = 384 * (2 * xx + c) + 128 * t
                                grad_up[r : r + 48, col : col + 128] = a[48 * t : 48 * t + 48]
                        n = 4 * yy + xx
                        if c == step or n // 6 == step:
                            b, r = rows(c, at + PART_A, PART_B), 48 * (2 * yy + xx // 2)
                            for t in range(3):
                                if c == step:
                                    col = 384 * (xx % 2) + 128 * t
                                    grad_down[r : r + 48, col : col + 128] = b[64 * t : 64 * t + 48]
                                if n // 6 == step:
                                    col = 384 * c + 128 * t
                                    grad_out[16 * (n % 6) : 16 * (n % 6) + 16, col : col + 128] = b[64 * t + 48 : 64 * t + 64]
                for yy in range(4):
                    dy = lax.rem(y + 4 - yy, 4)
                    for j in range(4):
                        dz = lax.rem(z + 4 - j, 4)
                        piece = rows(c, 4 * GROUP * dy + GROUP * dz, GROUP)
                        for at, *halves in units(4 * c + yy):
                            for side, (r, n) in enumerate(halves):
                                if r // 96 == step:
                                    col = D * (n % 3) + 64 * (4 * (n // 3) + j)
                                    block = piece[at : at + 16, 64 * side : 64 * side + 64]
                                    grad_qkv[r % 96 : r % 96 + 16, col : col + 64] = block


def layer_out_kernel(place_ref, middle, active, w_down, out, total):
    step = pl.program_id(0)

    @pl.when(step == 0)
    def _():
        total[...] = middle[...]

    total[...] += dot(active[...], w_down[...])

    @pl.when(step == FF // CHUNK - 1)
    def _():
        out[0] = total[0:ROWS, :].astype(BF)


def input_grad_kernel(blk_ref, a0, a1, a2, a3, w0, w1, w2, w3, w4, w5, out, stage):
    blk = blk_ref[0]
    for d, piece in enumerate((a0, a1, a2, a3)):
        s = lax.rem(blk + 4 - d, 4)
        for n in range(6):
            stage[n, s] = piece[64 * n : 64 * n + 64, :]
    total = jnp.zeros((D, R), F32)
    for n, weight in enumerate((w0, w1, w2, w3, w4, w5)):
        total = total + dot(weight[...], stage[n].reshape(256, R))
    out[...] = total


def last_kernel(
    blk_ref, count_ref, c0, c1, c2, c3, so_far, hidden, d_middle, gain_term, gains, wq, wk, wv, grad_stream, small, stage
):
    blk = blk_ref[0]
    for d, piece in enumerate((c0, c1, c2, c3)):
        s = lax.rem(blk + 4 - d, 4)
        for part in range(3):
            stage[part, s] = piece[64 * part : 64 * part + 64, :]
    turned = so_far[...]
    for part, weight in enumerate((wq, wk, wv)):
        turned = turned + dot(weight[...], stage[part].reshape(256, R))
    grad = turned.T
    unit, inverse = normalize(hidden[...])
    total = d_middle[...] + norm_back(grad, unit, inverse, gains[0:1, :])
    grad_stream[0] = total[0:ROWS, :]
    row = lax.broadcasted_iota(jnp.int32, (R, 1), 0)
    which = jnp.where(row < ROWS, pass_index(blk, count_ref[0]), -1)
    small[0:1, :] = jnp.sum(grad * unit, axis=0, keepdims=True)
    small[1:2, :] = gain_term[...]
    for r in range(PASSES):
        small[2 + r : 3 + r, :] = jnp.sum(jnp.where(which == r, total, 0.0), axis=0, keepdims=True)
    small[7:8, :] = jnp.zeros((1, D), F32)


def shift(values, axis, d):
    if axis == "z":
        return lax.ppermute(values, "blk", [(i, (i + d) % 4) for i in range(4)])
    pairs = []
    for b in range(32):
        y, x, core = b // 8, (b // 2) % 4, b % 2
        if axis == "y":
            y = (y + d) % 4
        elif axis == "x":
            x = (x + d) % 4
        else:
            core = (core + d) % 2
        pairs.append((b, 8 * y + 2 * x + core))
    return lax.ppermute(values, "batch", pairs)


def spread_pieces(pieces, axis):
    two, three, one = (shift(pieces[d], axis, d) for d in (2, 3, 1))
    return (pieces[0], one, two, three)


def all_of(value, axis):
    return spread_pieces((value,) * 4, axis)


def after(value, *others):
    return lax.optimization_barrier((value,) + others)[0]


def far(value):
    return pltpu.with_memory_space_constraint(value, pltpu.HBM)


def weight_spec(column):
    return pl.BlockSpec((D, 256), lambda *_, column=column: (0, column))


def on_device(stream, cotangent, passes, w_qkv, w_out, w_up, w_down, ln_gains, pass_embed):
    z = lax.axis_index("blk").astype(jnp.int32)
    batch = lax.axis_index("batch").astype(jnp.int32)
    place = jnp.stack([z, batch // 2 % 4, batch // 8, batch % 2])
    gains = ln_gains.T
    embed = pass_embed.T
    piece = shape((192, R))
    full = shape((R, D))

    def arrived(*values):
        nonlocal place
        place = lax.optimization_barrier((place,) + values)[0]

    def ordered(outs):
        nonlocal place
        *outs, first = outs
        place, first = lax.optimization_barrier((place, first))
        return (*outs, first)

    hidden, turned, *early, normed = ordered(pl.pallas_call(
        first_kernel,
        grid=(1,),
        in_specs=[SM, SM, VM, VM, VM, weight_spec(0), weight_spec(3), weight_spec(6)],
        out_specs=[VM] * 7,
        out_shape=[kept((R, D), F32), kept((D, R)), piece, piece, piece, piece, full],
        scratch_shapes=[pltpu.VMEM((4, 192, R), BF)],
        compiler_params=room(24),
        name="ln_qkv",
    )(place, passes, far(stream), far(embed), far(gains), *([far(w_qkv)] * 3)))
    sent = ordered(pl.pallas_call(
        second_kernel,
        grid=(1,),
        in_specs=[SM, VM] + [weight_spec(c) for c in (1, 4, 7, 2, 5, 8)],
        out_specs=[VM] * 8,
        out_shape=[piece] * 8,
        scratch_shapes=[pltpu.VMEM((2, 4, 192, R), BF)],
        compiler_params=room(24),
        name="qkv_rest",
    )(place, normed, *([far(w_qkv)] * 6)))
    heads = [spread_pieces(early, "z"), spread_pieces(sent[0:4], "z")]
    last_group = [sent[4], shift(sent[5], "z", 1), sent[6], shift(sent[7], "z", 3)]

    wholes, attended, spreads, sent = [], [], [], []
    for g in range(3):
        *parts, whole, result, spread = ordered(run(
            lambda *refs, g=g: attend_kernel(g == 2, *refs),
            "attend",
            24,
            [shape((192 if g == 2 else HD, R))] * 4
            + [kept((4, 192, R)), kept((4, HD, R), F32), kept((4, 1, R), F32)],
            (place, *heads[g], *(sent if g == 2 else ())),
            [
                pltpu.VMEM((4, 128, R), BF),
                pltpu.VMEM((4, 128, R), BF),
                pltpu.VMEM((4, HD, R), BF),
                pltpu.VMEM((4, R, 128), BF),
                pltpu.VMEM((4, R, R), F32),
                pltpu.VMEM((4, HD, R), BF),
            ],
        ))
        if g == 0:
            last_group[2] = shift(after(last_group[2], place), "z", 2)
            heads.append(last_group)
        wholes.append(whole)
        attended.append(result)
        spreads.append(spread)
        sent += parts
    sent = sent[8:]
    back_o = spread_pieces(sent, "z")
    d_active = ordered((pl.pallas_call(
        active_grad_kernel,
        grid=(FF // CHUNK,),
        in_specs=[SM, VM, pl.BlockSpec((CHUNK, D), lambda f: (f, 0))],
        out_specs=pl.BlockSpec((R, CHUNK), lambda f: (0, f)),
        out_shape=kept((R, FF), F32),
        scratch_shapes=[pltpu.VMEM((R, D), BF), pltpu.VMEM((R, D), F32)],
        compiler_params=room(16),
        name="active_grad",
    )(place, far(cotangent), far(w_down)),))[0]
    near = after(turned, place, *back_o)
    near = (shift(near, "z", 1), shift(near, "z", 3))

    active, d_up, second, middle, o_turned, d_branch, d_middle, *sent, a_other, b_other, gain_term = ordered(pl.pallas_call(
        ff_kernel,
        grid=(FF // CHUNK,),
        in_specs=[SM] + [VM] * 4 + [VM, VM, VM, VM]
        + [pl.BlockSpec((D, CHUNK), lambda f: (0, f)), pl.BlockSpec((R, CHUNK), lambda f: (0, f))],
        out_specs=[VM] * 14,
        out_shape=[shape((R, FF)), shape((R, FF)), full, shape((R, D), F32), shape((D, R)), full, kept((R, D), F32)]
        + [kept((192, R))] + [piece] * 3 + [shape((4, 4, 4, 48, 384)), shape((4, 4, 4, 64, 384)), shape((1, D), F32)],
        scratch_shapes=[pltpu.VMEM((R, D), BF), pltpu.VMEM((R, D), F32), pltpu.VMEM((HEADS, HD, R), BF), pltpu.VMEM((D, R), BF)],
        compiler_params=room(36),
        name="ff",
    )(place, *back_o, hidden, cotangent, gains, w_out, far(w_up), far(d_active)))
    *sent, a_other, b_other = lax.optimization_barrier((*sent, a_other, b_other, *near))[:6]
    d_o = spread_pieces(sent, "z")

    got = (shift(a_other, "core", 1), shift(b_other, "core", 1))
    own = ordered(run(
        ff_grad_kernel,
        "ff_grad",
        32,
        [shape((4, 4, 4, 48, 384)), shape((4, 4, 4, 64, 384))],
        (place, active, d_up, second, far(cotangent), o_turned, d_branch),
        [pltpu.VMEM((R, D), F32)],
    ))
    sent = ordered(run(
        core_sum_kernel,
        "core_sum",
        24,
        [kept((4, 4, 48, 384))] + [shape((4, 4, 48, 384))] * 3 + [kept((4, 4, 64, 384))] + [shape((4, 4, 64, 384))] * 3,
        (place, *own, *got),
    ))
    arrived(*d_o)
    distant = shift(after(turned, *d_o, place), "z", 2)
    a_sent, b_sent = sent[0:4], sent[4:8]
    a_parts = [a_sent[0], shift(a_sent[1], "x", 1), None, shift(a_sent[3], "x", 3)]
    b_parts = [b_sent[0], shift(b_sent[1], "y", 1), None, shift(b_sent[3], "y", 3)]

    def attend_back(which):
        count = len(which)
        group = pl.BlockSpec((64 * count, R), lambda _: (which[0] // count, 0))
        operands = [t for g in which for t in (wholes[g], attended[g], spreads[g])]
        return ordered(pl.pallas_call(
            lambda *refs: attend_back_kernel(count, *refs),
            grid=(1,),
            in_specs=[SM] + [VM] * (3 * count) + [group] * 4,
            out_specs=[VM] * 5,
            out_shape=[kept((192 * count, R))] + [shape((192 * count, R))] * 3 + [kept((count, 4, 192, R))],
            scratch_shapes=[
                pltpu.VMEM((count, 4, 128, R), BF),
                pltpu.VMEM((count, 4, 128, R), BF),
                pltpu.VMEM((count, 4, HD, R), BF),
                pltpu.VMEM((count, 4, R, 128), BF),
                pltpu.VMEM((count, 4, R, 128), BF),
                pltpu.VMEM((count, 4, R, HD), BF),
                pltpu.VMEM((count, 4, HD, R), BF),
                pltpu.VMEM((count, 4, R, HD), BF),
                pltpu.VMEM((count, 4, 1, R), F32),
                pltpu.VMEM((count, 4, HD, R), F32),
            ],
            compiler_params=room(32 if count == 2 else 24),
            name="attend_back",
        )(place, *(far(t) for t in operands), *(far(t) for t in d_o)))

    *sent, made_first = attend_back((0, 1))
    first_pieces = spread_pieces(sent, "z")
    a_parts[2] = shift(after(a_sent[2], place), "x", 2)
    b_parts[2] = shift(after(b_sent[2], place), "y", 2)
    arrived(a_parts[1], a_parts[3], b_parts[1], b_parts[3], distant)
    *sent, made_last = attend_back((2,))
    keep, send = ordered(run(
        head_grad_kernel,
        "head_grad",
        32,
        [shape((4, 4, GROUP, 128))] * 2,
        (place, far(turned), far(near[0]), far(distant), far(near[1]), far(made_first), far(made_last)),
        [pltpu.VMEM((4, 640, R), BF), pltpu.VMEM((D, 640), F32), pltpu.VMEM((8, 4, GROUP, 128), BF)],
    ))
    arrived(*first_pieces, a_parts[2], b_parts[2])
    *sent, send = lax.optimization_barrier((*sent, send, *first_pieces, a_parts[2], b_parts[2]))[:5]
    last_pieces = spread_pieces(sent, "z")
    got = shift(send, "core", 1)

    sent = ordered(run(
        cut_kernel,
        "sum_first",
        24,
        [shape((4 * PART_A + 4 * GROUP, 128))] * 4 + [shape((4, 64, 384))] * 4,
        (place, *a_parts, *b_parts, keep, got),
    ))
    so_far = ordered((pl.pallas_call(
        input_grad_kernel,
        grid=(1,),
        in_specs=[SM] + [VM] * 4 + [weight_spec(c) for c in (0, 3, 6, 1, 4, 7)],
        out_specs=VM,
        out_shape=shape((D, R), F32),
        scratch_shapes=[pltpu.VMEM((6, 4, HD, R), BF)],
        compiler_params=room(24),
        name="input_grad",
    )(place, *first_pieces, *([far(w_qkv)] * 6)),))[0]
    own_y, *others = lax.optimization_barrier((*sent, place))[:8]
    y_parts, x_parts = spread_pieces([own_y, *others[0:3]], "y"), spread_pieces(others[3:7], "x")
    grad_stream, small = ordered(pl.pallas_call(
        last_kernel,
        grid=(1,),
        in_specs=[SM, SM] + [VM] * 9 + [weight_spec(c) for c in (2, 5, 8)],
        out_specs=[VM, VM],
        out_shape=[kept((1, ROWS, D), F32), shape((8, D), F32)],
        scratch_shapes=[pltpu.VMEM((3, 4, HD, R), BF)],
        compiler_params=room(24),
        name="ln_back",
    )(place, passes, *last_pieces, so_far, hidden, d_middle, gain_term, gains, *([far(w_qkv)] * 3)))
    sent = ordered(run(
        block_kernel,
        "sum_second",
        16,
        [shape((PART_A + PART_B + GROUP + TINY, 128))] * 4,
        (place, *y_parts, *x_parts, small),
    ))
    z_parts = spread_pieces(sent, "z")
    layer_out = ordered((pl.pallas_call(
        layer_out_kernel,
        grid=(FF // CHUNK,),
        in_specs=[SM, VM, pl.BlockSpec((R, CHUNK), lambda f: (0, f)), pl.BlockSpec((CHUNK, D), lambda f: (f, 0))],
        out_specs=VM,
        out_shape=kept((1, ROWS, D)),
        scratch_shapes=[pltpu.VMEM((R, D), F32)],
        compiler_params=room(16),
        name="layer_out",
    )(place, middle, active, far(w_down)),))[0]
    head, bulk = ordered(run(
        own_kernel, "sum_blocks", 16, [shape((4 * GROUP + TINY, 128)), shape((PARTS, 128))], (place, *z_parts)
    ))
    bulks = all_of(bulk, "y")
    heads_x = all_of(head, "x")
    row = ordered(run(row_kernel, "stack_rows", 16, [shape((4 * PARTS, 128))], (place, *bulks)))[0]
    rows = [row, shift(row, "x", 1), None, shift(row, "x", 3)]
    head = ordered(run(head_row_kernel, "sum_heads", 16, [shape((4 * GROUP + TINY, 128))], (place, *heads_x)))[0]
    rows[2] = shift(after(row, place), "x", 2)
    heads_y = all_of(head, "y")
    buffer = ordered(run(stack_kernel, "stack", 16, [shape((ALL, 128))], (place, *heads_y, *rows)))[0]
    def half(count, lanes):
        return pl.BlockSpec((count, lanes), lambda i: (i, 0))

    *results, grad_gains, grad_pass = pl.pallas_call(
        finish_kernel,
        grid=(2,),
        in_specs=[SM, VM, VM],
        out_specs=[half(96, 3 * D), half(96, D), half(96, FF), half(384, D), VM, VM],
        out_shape=[
            kept((192, 3 * D), F32),
            kept((192, D), F32),
            kept((192, FF), F32),
            kept((D, D), F32),
            shape((2, 192), F32),
            shape((PASSES, 192), F32),
        ],
        scratch_shapes=[pltpu.VMEM((2, ALL, 128), BF), pltpu.VMEM((D, 8), F32)],
        compiler_params=room(32),
        name="finish",
    )(place, buffer, shift(buffer, "core", 1))
    return (layer_out, grad_stream, *results, grad_gains.T, grad_pass.T)


def solution(mesh):
    tokens = P("batch", "blk", None)
    in_specs = (tokens, tokens, P("batch"), P(), P(), P(), P(), P(), P())
    out_specs = (tokens, tokens) + (P("blk", None),) * 6
    return jax.shard_map(on_device, mesh=mesh, in_specs=in_specs, out_specs=out_specs, check_vma=False)
```

```python
import jax
import jax.numpy as jnp
from jax import lax
from jax.experimental import pallas as pl
from jax.experimental.pallas import tpu as pltpu
from jax.sharding import PartitionSpec as P

D = 768
HEADS = 12
HD = 64
FF = 3072
PASSES = 5
ROWS = 510
R = 512
EPS = 1e-05
NEG = -1e30
BF = jnp.bfloat16
F32 = jnp.float32
VM = pl.BlockSpec(memory_space=pltpu.VMEM)
SM = pl.BlockSpec(memory_space=pltpu.SMEM)
HB = pl.BlockSpec(memory_space=pl.ANY)
MIB = 1024 * 1024


def room(mib):
    return pltpu.CompilerParams(vmem_limit_bytes=mib * MIB)


def run(kernel, name, mib, outs, operands, scratch=(), scalars=1):
    return pl.pallas_call(
        kernel,
        in_specs=[SM] * scalars + [VM] * (len(operands) - scalars),
        out_specs=[VM] * len(outs),
        out_shape=outs,
        scratch_shapes=list(scratch),
        compiler_params=room(mib),
        name=name,
    )(*operands)


def shape(dims, kind=BF):
    return jax.ShapeDtypeStruct(dims, kind)


def kept(dims, kind=BF):
    return pltpu.HBM(dims, kind)


def dot(left, right):
    return jnp.dot(left, right, preferred_element_type=F32)


def dot_nt(left, right):
    return lax.dot_general(left, right, (((1,), (1,)), ((), ())), preferred_element_type=F32)


def normalize(values):
    mean = jnp.mean(values, axis=-1, keepdims=True)
    centred = values - mean
    inverse = lax.rsqrt(jnp.mean(centred * centred, axis=-1, keepdims=True) + EPS)
    return centred * inverse, inverse


def norm_back(grad, unit, inverse, gain):
    scaled = grad * gain
    first = jnp.mean(scaled, axis=-1, keepdims=True)
    second = jnp.mean(scaled * unit, axis=-1, keepdims=True)
    return inverse * (scaled - first - unit * second)


def pass_index(blk, count):
    row = lax.broadcasted_iota(jnp.int32, (R, 1), 0) + blk * ROWS
    turns = jnp.floor((row.astype(F32) + 0.5) / count.astype(F32)).astype(jnp.int32)
    return row - turns * count


def pieces_out(stage, outs, blk):
    for d, out in enumerate(outs):
        out[...] = stage[lax.rem(blk + d, 4)]


def project(normed, weights, stage, outs, blk):
    for part, weight in enumerate(weights):
        got = dot(normed, weight[...])
        if part == 0:
            got = got.astype(BF) * jnp.asarray(HD ** (-0.5), BF)
        turned = got.astype(BF).T
        for j in range(4):
            stage[j, 64 * part : 64 * part + 64, :] = turned[64 * j : 64 * j + 64]
    pieces_out(stage, outs, blk)


def project(normed, weights, stage):
    for part, weight in enumerate(weights):
        got = dot(normed, weight[...])
        if part == 0:
            got = got.astype(BF) * jnp.asarray(HD ** (-0.5), BF)
        flipped = got.astype(BF).T
        for j in range(4):
            stage[j, 64 * part : 64 * part + 64, :] = flipped[64 * j : 64 * j + 64]


def first_kernel(blk_ref, count_ref, stream, embed, gains, wq, wk, wv, hidden, p0, p1, p2, p3, normed, stage):
    blk = blk_ref[0]
    hidden[R - 8 : R, :] = jnp.zeros((8, D), F32)
    hidden[0:ROWS, :] = stream[0].astype(F32)
    which = pass_index(blk, count_ref[0])
    added = embed[0:1, :]
    for r in range(1, PASSES):
        added = jnp.where(which == r, embed[r : r + 1, :], added)
    values = hidden[...] + added
    hidden[...] = values
    unit, _ = normalize(values)
    row = lax.broadcasted_iota(jnp.int32, (R, 1), 0)
    low = jnp.where(row < ROWS, unit * gains[0:1, :], 0.0).astype(BF)
    normed[...] = low
    project(low, (wq, wk, wv), stage)
    for d, out in enumerate((p0, p1, p2, p3)):
        out[...] = stage[lax.rem(blk + d, 4)]


def second_kernel(blk_ref, normed, wq1, wk1, wv1, wq2, wk2, wv2, p0, p1, p2, p3, q0, q1, q2, q3, turned, stage):
    blk = blk_ref[0]
    turned[...] = normed[...].T
    for n, (weights, outs) in enumerate((((wq1, wk1, wv1), (p0, p1, p2, p3)), ((wq2, wk2, wv2), (q0, q1, q2, q3)))):
        project(normed[...], weights, stage.at[n])
        for d, out in enumerate(outs):
            out[...] = stage[n, lax.rem(blk + d, 4)]


def load_heads(whole, q_rows, k_rows, v_rows, k_cols):
    for s in range(4):
        q_rows[s, 0:64, :] = whole[s, 0:64, :]
        k_rows[s, 0:64, :] = whole[s, 64:128, :]
        v_rows[s] = whole[s, 128:192, :]
    row = lax.broadcasted_iota(jnp.int32, (64, R), 0)
    col = lax.broadcasted_iota(jnp.int32, (64, R), 1)
    one = jnp.where(row == 0, 1.0, 0.0).astype(BF)
    off = jnp.where((row == 0) & (col >= ROWS), NEG, 0.0).astype(BF)
    for s in range(4):
        q_rows[s, 64:128, :] = one
        k_rows[s, 64:128, :] = off
    for s in range(4):
        k_cols[s] = k_rows[s].T


HALF = R // 2


def causal(keys, queries):
    key = lax.broadcasted_iota(jnp.int32, (keys, queries), 0)
    query = lax.broadcasted_iota(jnp.int32, (keys, queries), 1)
    return key <= query


def attend_kernel(last, blk_ref, r0, r1, r2, r3, *rest):
    earlier, rest = (rest[:8], rest[8:]) if last else ((), rest)
    p0, p1, p2, p3, whole, attended, spread, q_rows, k_rows, v_rows, k_cols, scores, stage = rest
    blk = blk_ref[0]
    for d, piece in enumerate((r0, r1, r2, r3)):
        whole[lax.rem(blk + 4 - d, 4)] = piece[...]
    load_heads(whole, q_rows, k_rows, v_rows, k_cols)
    for i in range(4):
        low = jnp.where(causal(HALF, R), dot(k_cols[i, 0:HALF, :], q_rows[i]), NEG)
        high = jnp.where(causal(HALF, HALF), dot(k_cols[i, HALF:R, :], q_rows[i, :, HALF:R]), NEG)
        top = jnp.max(low, axis=0, keepdims=True)
        right = jnp.maximum(top[:, HALF:R], jnp.max(high, axis=0, keepdims=True))
        top = jnp.concatenate([top[:, 0:HALF], right], axis=1)
        for j in range(i):
            got = dot(k_cols[j], q_rows[i])
            scores[j] = got
            top = jnp.maximum(top, jnp.max(got, axis=0, keepdims=True))
        low = jnp.exp(low - top)
        high = jnp.exp(high - top[:, HALF:R])
        total = jnp.sum(low, axis=0, keepdims=True)
        summed = dot(v_rows[i, :, 0:HALF], low.astype(BF))
        right = total[:, HALF:R] + jnp.sum(high, axis=0, keepdims=True)
        total = jnp.concatenate([total[:, 0:HALF], right], axis=1)
        right = summed[:, HALF:R] + dot(v_rows[i, :, HALF:R], high.astype(BF))
        summed = jnp.concatenate([summed[:, 0:HALF], right], axis=1)
        for j in range(i):
            raised = jnp.exp(scores[j] - top)
            total = total + jnp.sum(raised, axis=0, keepdims=True)
            summed = summed + dot(v_rows[j], raised.astype(BF))
        result = summed / total
        attended[i] = result
        spread[i] = top + jnp.log(total)
        stage[i] = result.astype(BF)
    at = 128 if last else 0
    for d, out in enumerate((p0, p1, p2, p3)):
        out[at : at + 64, :] = stage[lax.rem(blk + d, 4)]
        if last:
            out[0:64, :] = earlier[d][...]
            out[64:128, :] = earlier[4 + d][...]


def attend_back_head(blk, whole, back, attended, spread, outs, scratch):
    q_rows, k_rows, v_rows, k_cols, q_cols, v_cols, o_rows, o_cols, delta, dq = scratch
    load_heads(whole, q_rows, k_rows, v_rows, k_cols)
    for d, piece in enumerate(back):
        o_rows[lax.rem(blk + 4 - d, 4)] = piece
    for s in range(4):
        q_cols[s] = q_rows[s].T
        v_cols[s] = v_rows[s].T
        o_cols[s] = o_rows[s].T
        delta[s] = jnp.sum(o_rows[s].astype(F32) * attended[s], axis=0, keepdims=True)
        dq[s] = jnp.zeros((HD, R), F32)
    for j in range(4):
        dk = jnp.zeros((R, 2 * HD), F32)
        dv = jnp.zeros((R, HD), F32)
        for i in range(j, 4):
            got = dot(k_cols[j], q_rows[i])
            if i == j:
                got = jnp.where(causal(R, R), got, NEG)
            probs = jnp.exp(got - spread[i])
            d_probs = dot(v_cols[j], o_rows[i])
            d_scores = (probs * (d_probs - delta[i])).astype(BF)
            dv = dv + dot(probs.astype(BF), o_cols[i])
            dk = dk + dot(d_scores, q_cols[i])
            dq[i] = dq[i] + dot(k_rows[j, 0:64, :], d_scores)
        outs[j, 0:64, :] = (dq[j] * HD ** (-0.5)).astype(BF)
        outs[j, 64:128, :] = dk[:, 0:64].astype(BF).T
        outs[j, 128:192, :] = dv.astype(BF).T


def attend_back_kernel(count, blk_ref, *refs):
    blk = blk_ref[0]
    sources = [refs[3 * h : 3 * h + 3] for h in range(count)]
    back, rest = refs[3 * count : 3 * count + 4], refs[3 * count + 4 :]
    pieces, outs, scratch = rest[0:4], rest[4], rest[5:]
    for h, (whole, attended, spread) in enumerate(sources):
        grads = [piece[64 * h : 64 * h + 64, :] for piece in back]
        attend_back_head(blk, whole, grads, attended, spread, outs.at[h], [ref.at[h] for ref in scratch])
        for d, out in enumerate(pieces):
            out[192 * h : 192 * h + 192, :] = outs[h, lax.rem(blk + d, 4)]


def units(piece):
    for n in range(7):
        u = 7 * piece + n
        if u < 48:
            yield 16 * n, (16 * (u // 4), 2 * (u % 4)), (16 * (u // 4), 2 * (u % 4) + 1)
        elif u < 54:
            yield 16 * n, (32 * (u - 48), 8), (32 * (u - 48) + 16, 8)


def head_grad_kernel(place_ref, t0, t1, t2, t3, e01, e2, keep, send, sides, made, pieces):
    blk, core = place_ref[0], place_ref[3]
    total = jnp.zeros((D, 640), F32)
    for d, piece in enumerate((t0, t1, t2, t3)):
        s = lax.rem(blk + 4 - d, 4)
        for g, side in enumerate((e01.at[0], e01.at[1], e2.at[0])):
            sides[d, 192 * g : 192 * g + 192, :] = side[s]
        sides[d, 576:640, :] = jnp.zeros((64, R), BF)
        total = total + dot_nt(piece[...], sides[d])
    made[...] = total
    pieces[...] = jnp.zeros((8, 4, GROUP, 128), BF)
    for k in range(8):
        for at, (row, left), (row_right, right) in units(k):
            for i in range(4):
                r = 192 * i + row
                if right == left:
                    halves = (made[r : r + 16, 512:576], made[r + 16 : r + 32, 512:576])
                    block = jnp.concatenate(halves, axis=1)
                else:
                    block = made[r : r + 16, 64 * left : 64 * left + 128]
                pieces[k, i, at : at + 16, :] = block.astype(BF)
    for q in range(4):
        keep[q] = pieces[4 * core + q]
        send[q] = pieces[4 * (1 - core) + q]


def gelu_both(value):
    c = (2.0 / jnp.pi) ** 0.5
    square = value * value
    t = jnp.tanh(c * value * (1.0 + 0.044715 * square))
    cdf = 0.5 * (1.0 + t)
    slope = cdf + (0.5 * c) * value * (1.0 - t * t) * (1.0 + 3.0 * 0.044715 * square)
    return value * cdf, slope


CHUNK = 768


def active_grad_kernel(place_ref, cot, w_down, out, dy, pad):
    @pl.when(pl.program_id(0) == 0)
    def _():
        pad[R - 8 : R, :] = jnp.zeros((8, D), F32)
        pad[0:ROWS, :] = cot[0].astype(F32)
        dy[...] = pad[...].astype(BF)

    out[...] = dot_nt(dy[...], w_down[...])


def up_cut(values, store):
    for z in range(4):
        for yy in range(4):
            store(yy, z, values[192 * z + 48 * yy : 192 * z + 48 * yy + 48, :])


def down_cut(values, store):
    for yy in range(4):
        for xx in range(4):
            r, col = 48 * (2 * yy + xx // 2), 384 * (xx % 2)
            store(yy, xx, values[r : r + 48, col : col + 384])


def out_cut(values, out):
    for i in range(4):
        for n in range(16):
            rows = values[192 * i + 16 * n : 192 * i + 16 * n + 16, :] if n < 12 else jnp.zeros((16, 384), BF)
            out[n // 4, n % 4, i, 48:64] = rows


def put_block(out, at, rows):
    out[at] = rows.astype(BF)


def ff_kernel(
    blk_ref, r0, r1, r2, r3, hidden, cot, gains, w_out, w_up, d_active,
    active, d_up, second, middle, o_turned, d_branch, d_middle, p0, p1, p2, p3, a_out, b_out, gain_term,
    dy, back, stage, second_turned,
):
    step = pl.program_id(0)
    core = blk_ref[3]

    @pl.when(step == 0)
    def _():
        blk = blk_ref[0]
        for d, piece in enumerate((r0, r1, r2, r3)):
            s = lax.rem(blk + 4 - d, 4)
            for g in range(3):
                stage[4 * g + s] = piece[64 * g : 64 * g + 64, :]
        o_rows = stage[...].reshape(D, R)
        o_turned[...] = o_rows
        values = hidden[...] + dot(o_rows.T, w_out[...])
        middle[...] = values
        unit, _ = normalize(values)
        second[...] = (unit * gains[1:2, :]).astype(BF)
        back[R - 8 : R, :] = jnp.zeros((8, D), F32)
        back[0:ROWS, :] = cot[0].astype(F32)
        dy[...] = back[...].astype(BF)
        back[...] = jnp.zeros((R, D), F32)
        second_turned[...] = second[...].T

    upward = dot(second[...], w_up[...])
    act, slope = gelu_both(upward)
    act = act.astype(BF)
    at = pl.ds(pl.multiple_of(step * CHUNK, 128), CHUNK)
    active[:, at] = act
    d_upward = (d_active[...] * slope).astype(BF)
    d_up[:, at] = d_upward
    back[...] += dot_nt(d_upward, w_up[...])

    first = core == 0
    other_up = jnp.where(first, d_upward[:, 384:768], d_upward[:, 0:384])
    other_act = jnp.where(first, act[:, 384:768], act[:, 0:384])
    up_cut(dot(second_turned[...], other_up), lambda yy, z, rows: put_block(a_out, (yy, step, z), rows))
    down_cut(dot(other_act.T, dy[...]), lambda yy, xx, rows: put_block(b_out, (yy, xx, step, slice(0, 48)), rows))

    @pl.when(step == FF // CHUNK - 1)
    def _():
        blk = blk_ref[0]
        unit, inverse = normalize(middle[...])
        grad = back[...]
        gain_term[...] = jnp.sum(grad * unit, axis=0, keepdims=True)
        total = dy[...].astype(F32) + norm_back(grad, unit, inverse, gains[1:2, :])
        d_middle[...] = total
        low = total.astype(BF)
        d_branch[...] = low
        stage[...] = dot_nt(w_out[...], low).astype(BF).reshape(HEADS, HD, R)
        out_cut(dot(o_turned[...], jnp.where(core == 0, low[:, 384:768], low[:, 0:384])).astype(BF), b_out)
        for d, out in enumerate((p0, p1, p2, p3)):
            j = lax.rem(blk + d, 4)
            for g in range(3):
                out[64 * g : 64 * g + 64, :] = stage[4 * g + j]


def ff_grad_kernel(place_ref, active, d_up, second, cot, o_turned, d_branch, a_out, b_out, pad):
    first = place_ref[3] == 0
    pad[R - 8 : R, :] = jnp.zeros((8, D), F32)
    pad[0:ROWS, :] = cot[0].astype(F32)
    dy = pad[...].astype(BF)
    second_turned = second[...].T

    def half(ref, i):
        return jnp.where(first, ref[:, 768 * i : 768 * i + 384], ref[:, 768 * i + 384 : 768 * i + 768])

    out_cut(dot(o_turned[...], half(d_branch, 0)).astype(BF), b_out)
    for pair in ((0, 1), (2, 3)):
        up = dot(second_turned, jnp.concatenate([half(d_up, i) for i in pair], axis=1))
        down = dot(jnp.concatenate([half(active, i).T for i in pair], axis=0), dy)
        for n, i in enumerate(pair):
            up_cut(up[:, 384 * n : 384 * n + 384], lambda yy, z, rows: put_block(a_out, (yy, i, z), rows))
            down_cut(down[384 * n : 384 * n + 384], lambda yy, xx, rows: put_block(b_out, (yy, xx, i, slice(0, 48)), rows))


def core_sum_kernel(place_ref, a_mine, b_mine, a_got, b_got, a0, a1, a2, a3, b0, b1, b2, b3):
    x, y = place_ref[1], place_ref[2]
    for d, (a_out, b_out) in enumerate(((a0, b0), (a1, b1), (a2, b2), (a3, b3))):
        xx, yy = lax.rem(x + d, 4), lax.rem(y + d, 4)
        for n in range(4):
            a_out[n] = (a_mine[n, xx].astype(F32) + a_got[n, xx].astype(F32)).astype(BF)
            b_out[n] = (b_mine[yy, n].astype(F32) + b_got[yy, n].astype(F32)).astype(BF)


def total_of(parts):
    return (parts[0].astype(F32) + parts[2].astype(F32)) + (parts[1].astype(F32) + parts[3].astype(F32))


TINY = 96
GROUP = 112
PART_A = 144
PART_B = 192
PARTS = PART_A + PART_B


def put(buffer, at, block):
    rows, lanes = block.shape
    for t in range(lanes // 128):
        buffer[at + rows * t : at + rows * t + rows, :] = block[:, 128 * t : 128 * t + 128]


def put_small(buffer, at, value):
    high = value.astype(BF)
    low = (value - high.astype(F32)).astype(BF)
    put(buffer, at, jnp.concatenate([high, low], axis=0))


def get_small(buffer, at):
    parts = []
    for t in range(6):
        part = buffer[at + 16 * t : at + 16 * t + 16, :].astype(F32)
        parts.append(part[0:8] + part[8:16])
    return jnp.concatenate(parts, axis=1)


def take(buffer, at, rows):
    return jnp.concatenate([buffer[at + rows * t : at + rows * t + rows, :] for t in range(3)], axis=1)


def cut_kernel(place_ref, a0, a1, a2, a3, b0, b1, b2, b3, keep, got, y0, y1, y2, y3, x0, x1, x2, x3):
    x, y = place_ref[1], place_ref[2]
    for d, (y_out, x_out) in enumerate(((y0, x0), (y1, x1), (y2, x2), (y3, x3))):
        yy, xx = lax.rem(y + d, 4), lax.rem(x + d, 4)
        a_sum = total_of([r[yy] for r in (a0, a1, a2, a3)]).astype(BF)
        heads = (keep[yy].astype(F32) + got[yy].astype(F32)).astype(BF)
        for i in range(4):
            put(y_out, PART_A * i, a_sum[i])
            y_out[4 * PART_A + GROUP * i : 4 * PART_A + GROUP * i + GROUP, :] = heads[i]
        x_out[...] = total_of([r[xx] for r in (b0, b1, b2, b3)]).astype(BF)


def block_kernel(place_ref, y0, y1, y2, y3, x0, x1, x2, x3, small, o0, o1, o2, o3):
    z = place_ref[0]
    for d, out in enumerate((o0, o1, o2, o3)):
        i = lax.rem(z + d, 4)
        start = pl.multiple_of(PART_A * i, 16)
        out[0:PART_A, :] = total_of([r[pl.ds(start, PART_A), :] for r in (y0, y1, y2, y3)]).astype(BF)
        put(out, PART_A, total_of([r[i] for r in (x0, x1, x2, x3)]).astype(BF))
        start = pl.multiple_of(4 * PART_A + GROUP * i, 16)
        at = PART_A + PART_B
        out[at : at + GROUP, :] = total_of([r[pl.ds(start, GROUP), :] for r in (y0, y1, y2, y3)]).astype(BF)
        put_small(out, at + GROUP, small[...])


def own_kernel(place_ref, z0, z1, z2, z3, heads, bulk):
    parts = (z0, z1, z2, z3)
    for d, r in enumerate(parts):
        heads[GROUP * d : GROUP * d + GROUP, :] = r[PARTS : PARTS + GROUP, :]
    put_small(heads, 4 * GROUP, total_of([get_small(r, PARTS + GROUP) for r in parts]))
    bulk[...] = total_of([r[0:PARTS, :] for r in parts]).astype(BF)


def row_kernel(place_ref, y0, y1, y2, y3, out):
    for d, r in enumerate((y0, y1, y2, y3)):
        out[PARTS * d : PARTS * d + PARTS, :] = r[...]


def head_row_kernel(place_ref, x0, x1, x2, x3, out):
    parts = (x0, x1, x2, x3)
    out[0 : 4 * GROUP, :] = total_of([r[0 : 4 * GROUP, :] for r in parts]).astype(BF)
    put_small(out, 4 * GROUP, total_of([get_small(r, 4 * GROUP) for r in parts]))


ALL_TINY = 16 * GROUP
ALL_BULK = ALL_TINY + TINY
ALL = ALL_BULK + 16 * PARTS


def stack_kernel(place_ref, y0, y1, y2, y3, x0, x1, x2, x3, out):
    parts = (y0, y1, y2, y3)
    put_small(out, ALL_TINY, total_of([get_small(r, 4 * GROUP) for r in parts]))
    for d, (r, b) in enumerate(zip(parts, (x0, x1, x2, x3))):
        out[4 * GROUP * d : 4 * GROUP * d + 4 * GROUP, :] = r[0 : 4 * GROUP, :]
        out[ALL_BULK + 4 * PARTS * d : ALL_BULK + 4 * PARTS * d + 4 * PARTS, :] = b[...]


def finish_kernel(place_ref, mine, other, grad_qkv, grad_out, grad_up, grad_down, gains, passes, pair, turned):
    z, x, y, core = place_ref[0], place_ref[1], place_ref[2], place_ref[3]

    @pl.when(pl.program_id(0) == 0)
    def _():
        pair[core] = mine[...]
        pair[1 - core] = other[...]
        small = get_small(mine, ALL_TINY) + get_small(other, ALL_TINY)
        turned[...] = small.T
        part = turned[pl.ds(pl.multiple_of(192 * z, 8), 192), :].T
        gains[...] = part[0:2, :]
        passes[...] = part[2:7, :]

    def rows(c, at, count):
        return pair[c, pl.ds(pl.multiple_of(at, 16), count), :].astype(F32)

    for step in range(2):
        @pl.when(pl.program_id(0) == step)
        def _():
            for c in range(2):
                for xx in range(4):
                    dx = lax.rem(x + 4 - xx, 4)
                    for yy in range(4):
                        dy = lax.rem(y + 4 - yy, 4)
                        at = ALL_BULK + 4 * PARTS * dx + PARTS * dy
                        if yy // 2 == step:
                            a, r = rows(c, at, PART_A), 48 * (yy % 2)
                            for t in range(3):
                                col = 384 * (2 * xx + c) + 128 * t
                                grad_up[r : r + 48, col : col + 128] = a[48 * t : 48 * t + 48]
                        n = 4 * yy + xx
                        if c == step or n // 6 == step:
                            b, r = rows(c, at + PART_A, PART_B), 48 * (2 * yy + xx // 2)
                            for t in range(3):
                                if c == step:
                                    col = 384 * (xx % 2) + 128 * t
                                    grad_down[r : r + 48, col : col + 128] = b[64 * t : 64 * t + 48]
                                if n // 6 == step:
                                    col = 384 * c + 128 * t
                                    grad_out[16 * (n % 6) : 16 * (n % 6) + 16, col : col + 128] = b[64 * t + 48 : 64 * t + 64]
                for yy in range(4):
                    dy = lax.rem(y + 4 - yy, 4)
                    for j in range(4):
                        dz = lax.rem(z + 4 - j, 4)
                        piece = rows(c, 4 * GROUP * dy + GROUP * dz, GROUP)
                        for at, *halves in units(4 * c + yy):
                            for side, (r, n) in enumerate(halves):
                                if r // 96 == step:
                                    col = D * (n % 3) + 64 * (4 * (n // 3) + j)
                                    block = piece[at : at + 16, 64 * side : 64 * side + 64]
                                    grad_qkv[r % 96 : r % 96 + 16, col : col + 64] = block


def layer_out_kernel(place_ref, middle, active, w_down, out, total):
    step = pl.program_id(0)

    @pl.when(step == 0)
    def _():
        total[...] = middle[...]

    total[...] += dot(active[...], w_down[...])

    @pl.when(step == FF // CHUNK - 1)
    def _():
        out[0] = total[0:ROWS, :].astype(BF)


def input_grad_kernel(blk_ref, a0, a1, a2, a3, w0, w1, w2, w3, w4, w5, out, stage):
    blk = blk_ref[0]
    for d, piece in enumerate((a0, a1, a2, a3)):
        s = lax.rem(blk + 4 - d, 4)
        for n in range(6):
            stage[n, s] = piece[64 * n : 64 * n + 64, :]
    total = jnp.zeros((D, R), F32)
    for n, weight in enumerate((w0, w1, w2, w3, w4, w5)):
        total = total + dot(weight[...], stage[n].reshape(256, R))
    out[...] = total


def last_kernel(
    blk_ref, count_ref, c0, c1, c2, c3, so_far, hidden, d_middle, gain_term, gains, wq, wk, wv, grad_stream, small, stage
):
    blk = blk_ref[0]
    for d, piece in enumerate((c0, c1, c2, c3)):
        s = lax.rem(blk + 4 - d, 4)
        for part in range(3):
            stage[part, s] = piece[64 * part : 64 * part + 64, :]
    turned = so_far[...]
    for part, weight in enumerate((wq, wk, wv)):
        turned = turned + dot(weight[...], stage[part].reshape(256, R))
    grad = turned.T
    unit, inverse = normalize(hidden[...])
    total = d_middle[...] + norm_back(grad, unit, inverse, gains[0:1, :])
    grad_stream[0] = total[0:ROWS, :]
    row = lax.broadcasted_iota(jnp.int32, (R, 1), 0)
    which = jnp.where(row < ROWS, pass_index(blk, count_ref[0]), -1)
    small[0:1, :] = jnp.sum(grad * unit, axis=0, keepdims=True)
    small[1:2, :] = gain_term[...]
    for r in range(PASSES):
        small[2 + r : 3 + r, :] = jnp.sum(jnp.where(which == r, total, 0.0), axis=0, keepdims=True)
    small[7:8, :] = jnp.zeros((1, D), F32)


def shift(values, axis, d):
    if axis == "z":
        return lax.ppermute(values, "blk", [(i, (i + d) % 4) for i in range(4)])
    pairs = []
    for b in range(32):
        y, x, core = b // 8, (b // 2) % 4, b % 2
        if axis == "y":
            y = (y + d) % 4
        elif axis == "x":
            x = (x + d) % 4
        else:
            core = (core + d) % 2
        pairs.append((b, 8 * y + 2 * x + core))
    return lax.ppermute(values, "batch", pairs)


def spread_pieces(pieces, axis):
    two, three, one = (shift(pieces[d], axis, d) for d in (2, 3, 1))
    return (pieces[0], one, two, three)


def all_of(value, axis):
    return spread_pieces((value,) * 4, axis)


def after(value, *others):
    return lax.optimization_barrier((value,) + others)[0]


def far(value):
    return pltpu.with_memory_space_constraint(value, pltpu.HBM)


def weight_spec(column):
    return pl.BlockSpec((D, 256), lambda *_, column=column: (0, column))


def on_device(stream, cotangent, passes, w_qkv, w_out, w_up, w_down, ln_gains, pass_embed):
    z = lax.axis_index("blk").astype(jnp.int32)
    batch = lax.axis_index("batch").astype(jnp.int32)
    place = jnp.stack([z, batch // 2 % 4, batch // 8, batch % 2])
    gains = ln_gains.T
    embed = pass_embed.T
    piece = shape((192, R))
    full = shape((R, D))

    def arrived(*values):
        nonlocal place
        place = lax.optimization_barrier((place,) + values)[0]

    def ordered(outs):
        nonlocal place
        *outs, first = outs
        place, first = lax.optimization_barrier((place, first))
        return (*outs, first)

    hidden, *early, normed = ordered(pl.pallas_call(
        first_kernel,
        grid=(1,),
        in_specs=[SM, SM, VM, VM, VM, weight_spec(0), weight_spec(3), weight_spec(6)],
        out_specs=[VM] * 6,
        out_shape=[kept((R, D), F32), piece, piece, piece, piece, full],
        scratch_shapes=[pltpu.VMEM((4, 192, R), BF)],
        compiler_params=room(24),
        name="ln_qkv",
    )(place, passes, far(stream), far(embed), far(gains), *([far(w_qkv)] * 3)))
    *sent, turned = ordered(pl.pallas_call(
        second_kernel,
        grid=(1,),
        in_specs=[SM, VM] + [weight_spec(c) for c in (1, 4, 7, 2, 5, 8)],
        out_specs=[VM] * 9,
        out_shape=[piece] * 8 + [kept((D, R))],
        scratch_shapes=[pltpu.VMEM((2, 4, 192, R), BF)],
        compiler_params=room(24),
        name="qkv_rest",
    )(place, normed, *([far(w_qkv)] * 6)))
    heads = [spread_pieces(early, "z"), spread_pieces(sent[0:4], "z")]
    last_group = [sent[4], shift(sent[5], "z", 1), sent[6], sent[7]]

    wholes, attended, spreads, sent = [], [], [], []
    for g in range(3):
        *parts, whole, result, spread = ordered(run(
            lambda *refs, g=g: attend_kernel(g == 2, *refs),
            "attend",
            24,
            [shape((192 if g == 2 else HD, R))] * 4
            + [kept((4, 192, R)), kept((4, HD, R), F32), kept((4, 1, R), F32)],
            (place, *heads[g], *(sent if g == 2 else ())),
            [
                pltpu.VMEM((4, 128, R), BF),
                pltpu.VMEM((4, 128, R), BF),
                pltpu.VMEM((4, HD, R), BF),
                pltpu.VMEM((4, R, 128), BF),
                pltpu.VMEM((4, R, R), F32),
                pltpu.VMEM((4, HD, R), BF),
            ],
        ))
        if g == 0:
            last_group[2], last_group[3] = (shift(after(last_group[d], place), "z", d) for d in (2, 3))
            heads.append(last_group)
        wholes.append(whole)
        attended.append(result)
        spreads.append(spread)
        sent += parts
    sent = sent[8:]
    back_o = spread_pieces(sent, "z")
    d_active = ordered((pl.pallas_call(
        active_grad_kernel,
        grid=(FF // CHUNK,),
        in_specs=[SM, VM, pl.BlockSpec((CHUNK, D), lambda f: (f, 0))],
        out_specs=pl.BlockSpec((R, CHUNK), lambda f: (0, f)),
        out_shape=shape((R, FF), F32),
        scratch_shapes=[pltpu.VMEM((R, D), BF), pltpu.VMEM((R, D), F32)],
        compiler_params=room(16),
        name="active_grad",
    )(place, far(cotangent), far(w_down)),))[0]
    near = after(turned, place, *back_o)
    near = (shift(near, "z", 1), shift(near, "z", 3))

    active, d_up, second, middle, o_turned, d_branch, d_middle, *sent, a_other, b_other, gain_term = ordered(pl.pallas_call(
        ff_kernel,
        grid=(FF // CHUNK,),
        in_specs=[SM] + [VM] * 4 + [VM, VM, VM, VM]
        + [pl.BlockSpec((D, CHUNK), lambda f: (0, f)), pl.BlockSpec((R, CHUNK), lambda f: (0, f))],
        out_specs=[VM] * 14,
        out_shape=[shape((R, FF)), shape((R, FF)), full, shape((R, D), F32), shape((D, R)), full, kept((R, D), F32)]
        + [kept((192, R))] + [piece] * 3 + [shape((4, 4, 4, 48, 384)), shape((4, 4, 4, 64, 384)), shape((1, D), F32)],
        scratch_shapes=[pltpu.VMEM((R, D), BF), pltpu.VMEM((R, D), F32), pltpu.VMEM((HEADS, HD, R), BF), pltpu.VMEM((D, R), BF)],
        compiler_params=room(26),
        name="ff",
    )(place, *back_o, hidden, cotangent, gains, w_out, far(w_up), d_active))
    *sent, a_other, b_other = lax.optimization_barrier((*sent, a_other, b_other, *near))[:6]
    d_o = spread_pieces(sent, "z")

    got = (shift(a_other, "core", 1), shift(b_other, "core", 1))
    own = ordered(run(
        ff_grad_kernel,
        "ff_grad",
        32,
        [shape((4, 4, 4, 48, 384)), shape((4, 4, 4, 64, 384))],
        (place, active, d_up, second, far(cotangent), o_turned, d_branch),
        [pltpu.VMEM((R, D), F32)],
    ))
    sent = ordered(run(
        core_sum_kernel,
        "core_sum",
        24,
        [kept((4, 4, 48, 384))] + [shape((4, 4, 48, 384))] * 3 + [kept((4, 4, 64, 384))] + [shape((4, 4, 64, 384))] * 3,
        (place, *own, *got),
    ))
    arrived(*d_o)
    distant = shift(after(turned, *d_o, place), "z", 2)
    a_sent, b_sent = sent[0:4], sent[4:8]
    a_parts = [a_sent[0], shift(a_sent[1], "x", 1), None, shift(a_sent[3], "x", 3)]
    b_parts = [b_sent[0], shift(b_sent[1], "y", 1), None, shift(b_sent[3], "y", 3)]

    def attend_back(which):
        count = len(which)
        group = pl.BlockSpec((64 * count, R), lambda _: (which[0] // count, 0))
        operands = [t for g in which for t in (wholes[g], attended[g], spreads[g])]
        return ordered(pl.pallas_call(
            lambda *refs: attend_back_kernel(count, *refs),
            grid=(1,),
            in_specs=[SM] + [VM] * (3 * count) + [group] * 4,
            out_specs=[VM] * 5,
            out_shape=[kept((192 * count, R))] + [shape((192 * count, R))] * 3 + [kept((count, 4, 192, R))],
            scratch_shapes=[
                pltpu.VMEM((count, 4, 128, R), BF),
                pltpu.VMEM((count, 4, 128, R), BF),
                pltpu.VMEM((count, 4, HD, R), BF),
                pltpu.VMEM((count, 4, R, 128), BF),
                pltpu.VMEM((count, 4, R, 128), BF),
                pltpu.VMEM((count, 4, R, HD), BF),
                pltpu.VMEM((count, 4, HD, R), BF),
                pltpu.VMEM((count, 4, R, HD), BF),
                pltpu.VMEM((count, 4, 1, R), F32),
                pltpu.VMEM((count, 4, HD, R), F32),
            ],
            compiler_params=room(32 if count == 2 else 24),
            name="attend_back",
        )(place, *(far(t) for t in operands), *(far(t) for t in d_o)))

    *sent, made_first = attend_back((0, 1))
    first_pieces = spread_pieces(sent, "z")
    a_parts[2] = shift(after(a_sent[2], place), "x", 2)
    b_parts[2] = shift(after(b_sent[2], place), "y", 2)
    arrived(a_parts[1], a_parts[3], b_parts[1], b_parts[3], distant)
    *sent, made_last = attend_back((2,))
    keep, send = ordered(run(
        head_grad_kernel,
        "head_grad",
        32,
        [shape((4, 4, GROUP, 128))] * 2,
        (place, far(turned), far(near[0]), far(distant), far(near[1]), far(made_first), far(made_last)),
        [pltpu.VMEM((4, 640, R), BF), pltpu.VMEM((D, 640), F32), pltpu.VMEM((8, 4, GROUP, 128), BF)],
    ))
    arrived(*first_pieces, a_parts[2], b_parts[2])
    *sent, send = lax.optimization_barrier((*sent, send, *first_pieces, a_parts[2], b_parts[2]))[:5]
    last_pieces = spread_pieces(sent, "z")
    got = shift(send, "core", 1)

    sent = ordered(run(
        cut_kernel,
        "sum_first",
        24,
        [shape((4 * PART_A + 4 * GROUP, 128))] * 4 + [shape((4, 64, 384))] * 4,
        (place, *a_parts, *b_parts, keep, got),
    ))
    so_far = ordered((pl.pallas_call(
        input_grad_kernel,
        grid=(1,),
        in_specs=[SM] + [VM] * 4 + [weight_spec(c) for c in (0, 3, 6, 1, 4, 7)],
        out_specs=VM,
        out_shape=shape((D, R), F32),
        scratch_shapes=[pltpu.VMEM((6, 4, HD, R), BF)],
        compiler_params=room(24),
        name="input_grad",
    )(place, *first_pieces, *([far(w_qkv)] * 6)),))[0]
    own_y, *others = lax.optimization_barrier((*sent, place))[:8]
    y_parts, x_parts = spread_pieces([own_y, *others[0:3]], "y"), spread_pieces(others[3:7], "x")
    grad_stream, small = ordered(pl.pallas_call(
        last_kernel,
        grid=(1,),
        in_specs=[SM, SM] + [VM] * 9 + [weight_spec(c) for c in (2, 5, 8)],
        out_specs=[VM, VM],
        out_shape=[kept((1, ROWS, D), F32), shape((8, D), F32)],
        scratch_shapes=[pltpu.VMEM((3, 4, HD, R), BF)],
        compiler_params=room(24),
        name="ln_back",
    )(place, passes, *last_pieces, so_far, hidden, d_middle, gain_term, gains, *([far(w_qkv)] * 3)))
    sent = ordered(run(
        block_kernel,
        "sum_second",
        16,
        [shape((PART_A + PART_B + GROUP + TINY, 128))] * 4,
        (place, *y_parts, *x_parts, small),
    ))
    z_parts = spread_pieces(sent, "z")
    layer_out = ordered((pl.pallas_call(
        layer_out_kernel,
        grid=(FF // CHUNK,),
        in_specs=[SM, VM, pl.BlockSpec((R, CHUNK), lambda f: (0, f)), pl.BlockSpec((CHUNK, D), lambda f: (f, 0))],
        out_specs=VM,
        out_shape=kept((1, ROWS, D)),
        scratch_shapes=[pltpu.VMEM((R, D), F32)],
        compiler_params=room(16),
        name="layer_out",
    )(place, middle, active, far(w_down)),))[0]
    head, bulk = ordered(run(
        own_kernel, "sum_blocks", 16, [shape((4 * GROUP + TINY, 128)), shape((PARTS, 128))], (place, *z_parts)
    ))
    bulks = all_of(bulk, "y")
    heads_x = all_of(head, "x")
    row = ordered(run(row_kernel, "stack_rows", 16, [shape((4 * PARTS, 128))], (place, *bulks)))[0]
    rows = [row, shift(row, "x", 1), None, shift(row, "x", 3)]
    head = ordered(run(head_row_kernel, "sum_heads", 16, [shape((4 * GROUP + TINY, 128))], (place, *heads_x)))[0]
    rows[2] = shift(after(row, place), "x", 2)
    heads_y = all_of(head, "y")
    buffer = ordered(run(stack_kernel, "stack", 16, [shape((ALL, 128))], (place, *heads_y, *rows)))[0]
    def half(count, lanes):
        return pl.BlockSpec((count, lanes), lambda i: (i, 0))

    *results, grad_gains, grad_pass = pl.pallas_call(
        finish_kernel,
        grid=(2,),
        in_specs=[SM, VM, VM],
        out_specs=[half(96, 3 * D), half(96, D), half(96, FF), half(384, D), VM, VM],
        out_shape=[
            kept((192, 3 * D), F32),
            kept((192, D), F32),
            kept((192, FF), F32),
            kept((D, D), F32),
            shape((2, 192), F32),
            shape((PASSES, 192), F32),
        ],
        scratch_shapes=[pltpu.VMEM((2, ALL, 128), BF), pltpu.VMEM((D, 8), F32)],
        compiler_params=room(32),
        name="finish",
    )(place, buffer, shift(buffer, "core", 1))
    return (layer_out, grad_stream, *results, grad_gains.T, grad_pass.T)


def solution(mesh):
    tokens = P("batch", "blk", None)
    in_specs = (tokens, tokens, P("batch"), P(), P(), P(), P(), P(), P())
    out_specs = (tokens, tokens) + (P("blk", None),) * 6
    return jax.shard_map(on_device, mesh=mesh, in_specs=in_specs, out_specs=out_specs, check_vma=False)
```

```python
import jax
import jax.numpy as jnp
from jax import lax
from jax.experimental import pallas as pl
from jax.experimental.pallas import tpu as pltpu
from jax.sharding import PartitionSpec as P

D = 768
HEADS = 12
HD = 64
FF = 3072
PASSES = 5
ROWS = 510
R = 512
EPS = 1e-05
NEG = -1e30
BF = jnp.bfloat16
F32 = jnp.float32
VM = pl.BlockSpec(memory_space=pltpu.VMEM)
SM = pl.BlockSpec(memory_space=pltpu.SMEM)
HB = pl.BlockSpec(memory_space=pl.ANY)
MIB = 1024 * 1024


def room(mib):
    return pltpu.CompilerParams(vmem_limit_bytes=mib * MIB)


def run(kernel, name, mib, outs, operands, scratch=(), scalars=1):
    return pl.pallas_call(
        kernel,
        in_specs=[SM] * scalars + [VM] * (len(operands) - scalars),
        out_specs=[VM] * len(outs),
        out_shape=outs,
        scratch_shapes=list(scratch),
        compiler_params=room(mib),
        name=name,
    )(*operands)


def shape(dims, kind=BF):
    return jax.ShapeDtypeStruct(dims, kind)


def kept(dims, kind=BF):
    return pltpu.HBM(dims, kind)


def dot(left, right):
    return jnp.dot(left, right, preferred_element_type=F32)


def dot_nt(left, right):
    return lax.dot_general(left, right, (((1,), (1,)), ((), ())), preferred_element_type=F32)


def normalize(values):
    mean = jnp.mean(values, axis=-1, keepdims=True)
    centred = values - mean
    inverse = lax.rsqrt(jnp.mean(centred * centred, axis=-1, keepdims=True) + EPS)
    return centred * inverse, inverse


def norm_back(grad, unit, inverse, gain):
    scaled = grad * gain
    first = jnp.mean(scaled, axis=-1, keepdims=True)
    second = jnp.mean(scaled * unit, axis=-1, keepdims=True)
    return inverse * (scaled - first - unit * second)


def pass_index(blk, count):
    row = lax.broadcasted_iota(jnp.int32, (R, 1), 0) + blk * ROWS
    turns = jnp.floor((row.astype(F32) + 0.5) / count.astype(F32)).astype(jnp.int32)
    return row - turns * count


def pieces_out(stage, outs, blk):
    for d, out in enumerate(outs):
        out[...] = stage[lax.rem(blk + d, 4)]


def project(normed, weights, stage, outs, blk):
    for part, weight in enumerate(weights):
        got = dot(normed, weight[...])
        if part == 0:
            got = got.astype(BF) * jnp.asarray(HD ** (-0.5), BF)
        turned = got.astype(BF).T
        for j in range(4):
            stage[j, 64 * part : 64 * part + 64, :] = turned[64 * j : 64 * j + 64]
    pieces_out(stage, outs, blk)


def project(normed, weights, stage):
    for part, weight in enumerate(weights):
        got = dot(normed, weight[...])
        if part == 0:
            got = got.astype(BF) * jnp.asarray(HD ** (-0.5), BF)
        flipped = got.astype(BF).T
        for j in range(4):
            stage[j, 64 * part : 64 * part + 64, :] = flipped[64 * j : 64 * j + 64]


def first_kernel(blk_ref, count_ref, stream, embed, gains, wq, wk, wv, hidden, p0, p1, p2, p3, normed, stage):
    blk = blk_ref[0]
    hidden[R - 8 : R, :] = jnp.zeros((8, D), F32)
    hidden[0:ROWS, :] = stream[0].astype(F32)
    which = pass_index(blk, count_ref[0])
    added = embed[0:1, :]
    for r in range(1, PASSES):
        added = jnp.where(which == r, embed[r : r + 1, :], added)
    values = hidden[...] + added
    hidden[...] = values
    unit, _ = normalize(values)
    row = lax.broadcasted_iota(jnp.int32, (R, 1), 0)
    low = jnp.where(row < ROWS, unit * gains[0:1, :], 0.0).astype(BF)
    normed[...] = low
    project(low, (wq, wk, wv), stage)
    for d, out in enumerate((p0, p1, p2, p3)):
        out[...] = stage[lax.rem(blk + d, 4)]


def second_kernel(blk_ref, normed, wq1, wk1, wv1, wq2, wk2, wv2, p0, p1, p2, p3, q0, q1, q2, q3, turned, stage):
    blk = blk_ref[0]
    turned[...] = normed[...].T
    for n, (weights, outs) in enumerate((((wq1, wk1, wv1), (p0, p1, p2, p3)), ((wq2, wk2, wv2), (q0, q1, q2, q3)))):
        project(normed[...], weights, stage.at[n])
        for d, out in enumerate(outs):
            out[...] = stage[n, lax.rem(blk + d, 4)]


def load_heads(whole, q_rows, k_rows, v_rows, k_cols):
    for s in range(4):
        q_rows[s, 0:64, :] = whole[s, 0:64, :]
        k_rows[s, 0:64, :] = whole[s, 64:128, :]
        v_rows[s] = whole[s, 128:192, :]
    row = lax.broadcasted_iota(jnp.int32, (64, R), 0)
    col = lax.broadcasted_iota(jnp.int32, (64, R), 1)
    one = jnp.where(row == 0, 1.0, 0.0).astype(BF)
    off = jnp.where((row == 0) & (col >= ROWS), NEG, 0.0).astype(BF)
    for s in range(4):
        q_rows[s, 64:128, :] = one
        k_rows[s, 64:128, :] = off
    for s in range(4):
        k_cols[s] = k_rows[s].T


HALF = R // 2


def causal(keys, queries):
    key = lax.broadcasted_iota(jnp.int32, (keys, queries), 0)
    query = lax.broadcasted_iota(jnp.int32, (keys, queries), 1)
    return key <= query


def attend_kernel(last, blk_ref, r0, r1, r2, r3, *rest):
    earlier, rest = (rest[:8], rest[8:]) if last else ((), rest)
    p0, p1, p2, p3, whole, attended, spread, q_rows, k_rows, v_rows, k_cols, scores, stage = rest
    blk = blk_ref[0]
    for d, piece in enumerate((r0, r1, r2, r3)):
        whole[lax.rem(blk + 4 - d, 4)] = piece[...]
    load_heads(whole, q_rows, k_rows, v_rows, k_cols)
    for i in range(4):
        low = jnp.where(causal(HALF, R), dot(k_cols[i, 0:HALF, :], q_rows[i]), NEG)
        high = jnp.where(causal(HALF, HALF), dot(k_cols[i, HALF:R, :], q_rows[i, :, HALF:R]), NEG)
        top = jnp.max(low, axis=0, keepdims=True)
        right = jnp.maximum(top[:, HALF:R], jnp.max(high, axis=0, keepdims=True))
        top = jnp.concatenate([top[:, 0:HALF], right], axis=1)
        for j in range(i):
            got = dot(k_cols[j], q_rows[i])
            scores[j] = got
            top = jnp.maximum(top, jnp.max(got, axis=0, keepdims=True))
        low = jnp.exp(low - top)
        high = jnp.exp(high - top[:, HALF:R])
        total = jnp.sum(low, axis=0, keepdims=True)
        summed = dot(v_rows[i, :, 0:HALF], low.astype(BF))
        right = total[:, HALF:R] + jnp.sum(high, axis=0, keepdims=True)
        total = jnp.concatenate([total[:, 0:HALF], right], axis=1)
        right = summed[:, HALF:R] + dot(v_rows[i, :, HALF:R], high.astype(BF))
        summed = jnp.concatenate([summed[:, 0:HALF], right], axis=1)
        for j in range(i):
            raised = jnp.exp(scores[j] - top)
            total = total + jnp.sum(raised, axis=0, keepdims=True)
            summed = summed + dot(v_rows[j], raised.astype(BF))
        result = summed / total
        attended[i] = result
        spread[i] = top + jnp.log(total)
        stage[i] = result.astype(BF)
    at = 128 if last else 0
    for d, out in enumerate((p0, p1, p2, p3)):
        out[at : at + 64, :] = stage[lax.rem(blk + d, 4)]
        if last:
            out[0:64, :] = earlier[d][...]
            out[64:128, :] = earlier[4 + d][...]


def attend_back_head(blk, whole, back, attended, spread, outs, scratch):
    q_rows, k_rows, v_rows, k_cols, q_cols, v_cols, o_rows, o_cols, delta, dq = scratch
    load_heads(whole, q_rows, k_rows, v_rows, k_cols)
    for d, piece in enumerate(back):
        o_rows[lax.rem(blk + 4 - d, 4)] = piece
    for s in range(4):
        q_cols[s] = q_rows[s].T
        v_cols[s] = v_rows[s].T
        o_cols[s] = o_rows[s].T
        delta[s] = jnp.sum(o_rows[s].astype(F32) * attended[s], axis=0, keepdims=True)
        dq[s] = jnp.zeros((HD, R), F32)
    for j in range(4):
        dk = jnp.zeros((R, 2 * HD), F32)
        dv = jnp.zeros((R, HD), F32)
        for i in range(j, 4):
            got = dot(k_cols[j], q_rows[i])
            if i == j:
                got = jnp.where(causal(R, R), got, NEG)
            probs = jnp.exp(got - spread[i])
            d_probs = dot(v_cols[j], o_rows[i])
            d_scores = (probs * (d_probs - delta[i])).astype(BF)
            dv = dv + dot(probs.astype(BF), o_cols[i])
            dk = dk + dot(d_scores, q_cols[i])
            dq[i] = dq[i] + dot(k_rows[j, 0:64, :], d_scores)
        outs[j, 0:64, :] = (dq[j] * HD ** (-0.5)).astype(BF)
        outs[j, 64:128, :] = dk[:, 0:64].astype(BF).T
        outs[j, 128:192, :] = dv.astype(BF).T


def attend_back_kernel(count, blk_ref, *refs):
    blk = blk_ref[0]
    sources = [refs[3 * h : 3 * h + 3] for h in range(count)]
    back, rest = refs[3 * count : 3 * count + 4], refs[3 * count + 4 :]
    pieces, outs, scratch = rest[0:4], rest[4], rest[5:]
    for h, (whole, attended, spread) in enumerate(sources):
        grads = [piece[64 * h : 64 * h + 64, :] for piece in back]
        attend_back_head(blk, whole, grads, attended, spread, outs.at[h], [ref.at[h] for ref in scratch])
        for d, out in enumerate(pieces):
            out[192 * h : 192 * h + 192, :] = outs[h, lax.rem(blk + d, 4)]


def units(piece):
    for n in range(7):
        u = 7 * piece + n
        if u < 48:
            yield 16 * n, (16 * (u // 4), 2 * (u % 4)), (16 * (u // 4), 2 * (u % 4) + 1)
        elif u < 54:
            yield 16 * n, (32 * (u - 48), 8), (32 * (u - 48) + 16, 8)


def head_grad_kernel(place_ref, t0, t1, t2, t3, e01, e2, keep, send, sides, made, pieces):
    blk, core = place_ref[0], place_ref[3]
    total = jnp.zeros((D, 640), F32)
    for d, piece in enumerate((t0, t1, t2, t3)):
        s = lax.rem(blk + 4 - d, 4)
        for g, side in enumerate((e01.at[0], e01.at[1], e2.at[0])):
            sides[d, 192 * g : 192 * g + 192, :] = side[s]
        sides[d, 576:640, :] = jnp.zeros((64, R), BF)
        total = total + dot_nt(piece[...], sides[d])
    made[...] = total
    pieces[...] = jnp.zeros((8, 4, GROUP, 128), BF)
    for k in range(8):
        for at, (row, left), (row_right, right) in units(k):
            for i in range(4):
                r = 192 * i + row
                if right == left:
                    halves = (made[r : r + 16, 512:576], made[r + 16 : r + 32, 512:576])
                    block = jnp.concatenate(halves, axis=1)
                else:
                    block = made[r : r + 16, 64 * left : 64 * left + 128]
                pieces[k, i, at : at + 16, :] = block.astype(BF)
    for q in range(4):
        keep[q] = pieces[4 * core + q]
        send[q] = pieces[4 * (1 - core) + q]


def gelu_both(value):
    c = (2.0 / jnp.pi) ** 0.5
    square = value * value
    t = jnp.tanh(c * value * (1.0 + 0.044715 * square))
    cdf = 0.5 * (1.0 + t)
    slope = cdf + (0.5 * c) * value * (1.0 - t * t) * (1.0 + 3.0 * 0.044715 * square)
    return value * cdf, slope


CHUNK = 768


def active_grad_kernel(place_ref, cot, w_down, out, dy, pad):
    @pl.when(pl.program_id(0) == 0)
    def _():
        pad[R - 8 : R, :] = jnp.zeros((8, D), F32)
        pad[0:ROWS, :] = cot[0].astype(F32)
        dy[...] = pad[...].astype(BF)

    out[...] = dot_nt(dy[...], w_down[...])


def up_cut(values, store):
    for z in range(4):
        for yy in range(4):
            store(yy, z, values[192 * z + 48 * yy : 192 * z + 48 * yy + 48, :])


def down_cut(values, store):
    for yy in range(4):
        for xx in range(4):
            r, col = 48 * (2 * yy + xx // 2), 384 * (xx % 2)
            store(yy, xx, values[r : r + 48, col : col + 384])


def out_cut(values, out):
    for i in range(4):
        for n in range(16):
            rows = values[192 * i + 16 * n : 192 * i + 16 * n + 16, :] if n < 12 else jnp.zeros((16, 384), BF)
            out[n // 4, n % 4, i, 48:64] = rows


def put_block(out, at, rows):
    out[at] = rows.astype(BF)


def ff_kernel(
    blk_ref, r0, r1, r2, r3, hidden, cot, gains, w_out, w_up, d_active,
    active, d_up, second, middle, o_turned, d_branch, d_middle, p0, p1, p2, p3, a_out, b_out, gain_term,
    dy, back, stage, second_turned,
):
    step = pl.program_id(0)
    core = blk_ref[3]

    @pl.when(step == 0)
    def _():
        blk = blk_ref[0]
        for d, piece in enumerate((r0, r1, r2, r3)):
            s = lax.rem(blk + 4 - d, 4)
            for g in range(3):
                stage[4 * g + s] = piece[64 * g : 64 * g + 64, :]
        o_rows = stage[...].reshape(D, R)
        o_turned[...] = o_rows
        values = hidden[...] + dot(o_rows.T, w_out[...])
        middle[...] = values
        unit, _ = normalize(values)
        second[...] = (unit * gains[1:2, :]).astype(BF)
        back[R - 8 : R, :] = jnp.zeros((8, D), F32)
        back[0:ROWS, :] = cot[0].astype(F32)
        dy[...] = back[...].astype(BF)
        back[...] = jnp.zeros((R, D), F32)
        second_turned[...] = second[...].T

    upward = dot(second[...], w_up[...])
    act, slope = gelu_both(upward)
    act = act.astype(BF)
    at = pl.ds(pl.multiple_of(step * CHUNK, 128), CHUNK)
    active[:, at] = act
    d_upward = (d_active[...] * slope).astype(BF)
    d_up[:, at] = d_upward
    back[...] += dot_nt(d_upward, w_up[...])

    first = core == 0
    other_up = jnp.where(first, d_upward[:, 384:768], d_upward[:, 0:384])
    other_act = jnp.where(first, act[:, 384:768], act[:, 0:384])
    up_cut(dot(second_turned[...], other_up), lambda yy, z, rows: put_block(a_out, (yy, step, z), rows))
    down_cut(dot(other_act.T, dy[...]), lambda yy, xx, rows: put_block(b_out, (yy, xx, step, slice(0, 48)), rows))

    @pl.when(step == FF // CHUNK - 1)
    def _():
        blk = blk_ref[0]
        unit, inverse = normalize(middle[...])
        grad = back[...]
        gain_term[...] = jnp.sum(grad * unit, axis=0, keepdims=True)
        total = dy[...].astype(F32) + norm_back(grad, unit, inverse, gains[1:2, :])
        d_middle[...] = total
        low = total.astype(BF)
        d_branch[...] = low
        stage[...] = dot_nt(w_out[...], low).astype(BF).reshape(HEADS, HD, R)
        out_cut(dot(o_turned[...], jnp.where(core == 0, low[:, 384:768], low[:, 0:384])).astype(BF), b_out)
        for d, out in enumerate((p0, p1, p2, p3)):
            j = lax.rem(blk + d, 4)
            for g in range(3):
                out[64 * g : 64 * g + 64, :] = stage[4 * g + j]


def ff_grad_kernel(place_ref, active, d_up, second, cot, o_turned, d_branch, a_out, b_out, pad):
    first = place_ref[3] == 0
    pad[R - 8 : R, :] = jnp.zeros((8, D), F32)
    pad[0:ROWS, :] = cot[0].astype(F32)
    dy = pad[...].astype(BF)
    second_turned = second[...].T

    def half(ref, i):
        return jnp.where(first, ref[:, 768 * i : 768 * i + 384], ref[:, 768 * i + 384 : 768 * i + 768])

    out_cut(dot(o_turned[...], half(d_branch, 0)).astype(BF), b_out)
    for pair in ((0, 1), (2, 3)):
        up = dot(second_turned, jnp.concatenate([half(d_up, i) for i in pair], axis=1))
        down = dot(jnp.concatenate([half(active, i).T for i in pair], axis=0), dy)
        for n, i in enumerate(pair):
            up_cut(up[:, 384 * n : 384 * n + 384], lambda yy, z, rows: put_block(a_out, (yy, i, z), rows))
            down_cut(down[384 * n : 384 * n + 384], lambda yy, xx, rows: put_block(b_out, (yy, xx, i, slice(0, 48)), rows))


def core_sum_kernel(place_ref, a_mine, b_mine, a_got, b_got, a0, a1, a2, a3, b0, b1, b2, b3):
    x, y = place_ref[1], place_ref[2]
    for d, (a_out, b_out) in enumerate(((a0, b0), (a1, b1), (a2, b2), (a3, b3))):
        xx, yy = lax.rem(x + d, 4), lax.rem(y + d, 4)
        for n in range(4):
            a_out[n] = (a_mine[n, xx].astype(F32) + a_got[n, xx].astype(F32)).astype(BF)
            b_out[n] = (b_mine[yy, n].astype(F32) + b_got[yy, n].astype(F32)).astype(BF)


def total_of(parts):
    return (parts[0].astype(F32) + parts[2].astype(F32)) + (parts[1].astype(F32) + parts[3].astype(F32))


TINY = 96
GROUP = 112
PART_A = 144
PART_B = 192
PARTS = PART_A + PART_B


def put(buffer, at, block):
    rows, lanes = block.shape
    for t in range(lanes // 128):
        buffer[at + rows * t : at + rows * t + rows, :] = block[:, 128 * t : 128 * t + 128]


def put_small(buffer, at, value):
    high = value.astype(BF)
    low = (value - high.astype(F32)).astype(BF)
    put(buffer, at, jnp.concatenate([high, low], axis=0))


def get_small(buffer, at):
    parts = []
    for t in range(6):
        part = buffer[at + 16 * t : at + 16 * t + 16, :].astype(F32)
        parts.append(part[0:8] + part[8:16])
    return jnp.concatenate(parts, axis=1)


def take(buffer, at, rows):
    return jnp.concatenate([buffer[at + rows * t : at + rows * t + rows, :] for t in range(3)], axis=1)


def cut_kernel(place_ref, a0, a1, a2, a3, b0, b1, b2, b3, keep, got, y0, y1, y2, y3, x0, x1, x2, x3):
    x, y = place_ref[1], place_ref[2]
    for d, (y_out, x_out) in enumerate(((y0, x0), (y1, x1), (y2, x2), (y3, x3))):
        yy, xx = lax.rem(y + d, 4), lax.rem(x + d, 4)
        a_sum = total_of([r[yy] for r in (a0, a1, a2, a3)]).astype(BF)
        heads = (keep[yy].astype(F32) + got[yy].astype(F32)).astype(BF)
        for i in range(4):
            put(y_out, PART_A * i, a_sum[i])
            y_out[4 * PART_A + GROUP * i : 4 * PART_A + GROUP * i + GROUP, :] = heads[i]
        x_out[...] = total_of([r[xx] for r in (b0, b1, b2, b3)]).astype(BF)


def block_kernel(place_ref, y0, y1, y2, y3, x0, x1, x2, x3, small, o0, o1, o2, o3):
    z = place_ref[0]
    for d, out in enumerate((o0, o1, o2, o3)):
        i = lax.rem(z + d, 4)
        start = pl.multiple_of(PART_A * i, 16)
        out[0:PART_A, :] = total_of([r[pl.ds(start, PART_A), :] for r in (y0, y1, y2, y3)]).astype(BF)
        put(out, PART_A, total_of([r[i] for r in (x0, x1, x2, x3)]).astype(BF))
        start = pl.multiple_of(4 * PART_A + GROUP * i, 16)
        at = PART_A + PART_B
        out[at : at + GROUP, :] = total_of([r[pl.ds(start, GROUP), :] for r in (y0, y1, y2, y3)]).astype(BF)
        put_small(out, at + GROUP, small[...])


def own_kernel(place_ref, z0, z1, z2, z3, heads, bulk):
    parts = (z0, z1, z2, z3)
    for d, r in enumerate(parts):
        heads[GROUP * d : GROUP * d + GROUP, :] = r[PARTS : PARTS + GROUP, :]
    put_small(heads, 4 * GROUP, total_of([get_small(r, PARTS + GROUP) for r in parts]))
    bulk[...] = total_of([r[0:PARTS, :] for r in parts]).astype(BF)


def row_kernel(place_ref, y0, y1, y2, y3, out):
    for d, r in enumerate((y0, y1, y2, y3)):
        out[PARTS * d : PARTS * d + PARTS, :] = r[...]


def head_row_kernel(place_ref, x0, x1, x2, x3, out):
    parts = (x0, x1, x2, x3)
    out[0 : 4 * GROUP, :] = total_of([r[0 : 4 * GROUP, :] for r in parts]).astype(BF)
    put_small(out, 4 * GROUP, total_of([get_small(r, 4 * GROUP) for r in parts]))


ALL_TINY = 16 * GROUP
ALL_BULK = ALL_TINY + TINY
ALL = ALL_BULK + 16 * PARTS


def stack_kernel(place_ref, y0, y1, y2, y3, x0, x1, x2, x3, out):
    parts = (y0, y1, y2, y3)
    put_small(out, ALL_TINY, total_of([get_small(r, 4 * GROUP) for r in parts]))
    for d, (r, b) in enumerate(zip(parts, (x0, x1, x2, x3))):
        out[4 * GROUP * d : 4 * GROUP * d + 4 * GROUP, :] = r[0 : 4 * GROUP, :]
        out[ALL_BULK + 4 * PARTS * d : ALL_BULK + 4 * PARTS * d + 4 * PARTS, :] = b[...]


def finish_kernel(place_ref, mine, other, grad_qkv, grad_out, grad_up, grad_down, gains, passes, pair, turned):
    z, x, y, core = place_ref[0], place_ref[1], place_ref[2], place_ref[3]

    @pl.when(pl.program_id(0) == 0)
    def _():
        pair[core] = mine[...]
        pair[1 - core] = other[...]
        small = get_small(mine, ALL_TINY) + get_small(other, ALL_TINY)
        turned[...] = small.T
        part = turned[pl.ds(pl.multiple_of(192 * z, 8), 192), :].T
        gains[...] = part[0:2, :]
        passes[...] = part[2:7, :]

    def rows(c, at, count):
        return pair[c, pl.ds(pl.multiple_of(at, 16), count), :].astype(F32)

    for step in range(2):
        @pl.when(pl.program_id(0) == step)
        def _():
            for c in range(2):
                for xx in range(4):
                    dx = lax.rem(x + 4 - xx, 4)
                    for yy in range(4):
                        dy = lax.rem(y + 4 - yy, 4)
                        at = ALL_BULK + 4 * PARTS * dx + PARTS * dy
                        if yy // 2 == step:
                            a, r = rows(c, at, PART_A), 48 * (yy % 2)
                            for t in range(3):
                                col = 384 * (2 * xx + c) + 128 * t
                                grad_up[r : r + 48, col : col + 128] = a[48 * t : 48 * t + 48]
                        n = 4 * yy + xx
                        if c == step or n // 6 == step:
                            b, r = rows(c, at + PART_A, PART_B), 48 * (2 * yy + xx // 2)
                            for t in range(3):
                                if c == step:
                                    col = 384 * (xx % 2) + 128 * t
                                    grad_down[r : r + 48, col : col + 128] = b[64 * t : 64 * t + 48]
                                if n // 6 == step:
                                    col = 384 * c + 128 * t
                                    grad_out[16 * (n % 6) : 16 * (n % 6) + 16, col : col + 128] = b[64 * t + 48 : 64 * t + 64]
                for yy in range(4):
                    dy = lax.rem(y + 4 - yy, 4)
                    for j in range(4):
                        dz = lax.rem(z + 4 - j, 4)
                        piece = rows(c, 4 * GROUP * dy + GROUP * dz, GROUP)
                        for at, *halves in units(4 * c + yy):
                            for side, (r, n) in enumerate(halves):
                                if r // 96 == step:
                                    col = D * (n % 3) + 64 * (4 * (n // 3) + j)
                                    block = piece[at : at + 16, 64 * side : 64 * side + 64]
                                    grad_qkv[r % 96 : r % 96 + 16, col : col + 64] = block


def layer_out_kernel(place_ref, middle, active, w_down, out, total):
    step = pl.program_id(0)

    @pl.when(step == 0)
    def _():
        total[...] = middle[...]

    total[...] += dot(active[...], w_down[...])

    @pl.when(step == FF // CHUNK - 1)
    def _():
        out[0] = total[0:ROWS, :].astype(BF)


def input_grad_kernel(blk_ref, a0, a1, a2, a3, w0, w1, w2, w3, w4, w5, out, stage):
    blk = blk_ref[0]
    for d, piece in enumerate((a0, a1, a2, a3)):
        s = lax.rem(blk + 4 - d, 4)
        for n in range(6):
            stage[n, s] = piece[64 * n : 64 * n + 64, :]
    total = jnp.zeros((D, R), F32)
    for n, weight in enumerate((w0, w1, w2, w3, w4, w5)):
        total = total + dot(weight[...], stage[n].reshape(256, R))
    out[...] = total


def last_kernel(
    blk_ref, count_ref, c0, c1, c2, c3, so_far, hidden, d_middle, gain_term, gains, wq, wk, wv, grad_stream, small, stage
):
    blk = blk_ref[0]
    for d, piece in enumerate((c0, c1, c2, c3)):
        s = lax.rem(blk + 4 - d, 4)
        for part in range(3):
            stage[part, s] = piece[64 * part : 64 * part + 64, :]
    turned = so_far[...]
    for part, weight in enumerate((wq, wk, wv)):
        turned = turned + dot(weight[...], stage[part].reshape(256, R))
    grad = turned.T
    unit, inverse = normalize(hidden[...])
    total = d_middle[...] + norm_back(grad, unit, inverse, gains[0:1, :])
    grad_stream[0] = total[0:ROWS, :]
    row = lax.broadcasted_iota(jnp.int32, (R, 1), 0)
    which = jnp.where(row < ROWS, pass_index(blk, count_ref[0]), -1)
    small[0:1, :] = jnp.sum(grad * unit, axis=0, keepdims=True)
    small[1:2, :] = gain_term[...]
    for r in range(PASSES):
        small[2 + r : 3 + r, :] = jnp.sum(jnp.where(which == r, total, 0.0), axis=0, keepdims=True)
    small[7:8, :] = jnp.zeros((1, D), F32)


def shift(values, axis, d):
    if axis == "z":
        return lax.ppermute(values, "blk", [(i, (i + d) % 4) for i in range(4)])
    pairs = []
    for b in range(32):
        y, x, core = b // 8, (b // 2) % 4, b % 2
        if axis == "y":
            y = (y + d) % 4
        elif axis == "x":
            x = (x + d) % 4
        else:
            core = (core + d) % 2
        pairs.append((b, 8 * y + 2 * x + core))
    return lax.ppermute(values, "batch", pairs)


def spread_pieces(pieces, axis):
    two, three, one = (shift(pieces[d], axis, d) for d in (2, 3, 1))
    return (pieces[0], one, two, three)


def all_of(value, axis):
    return spread_pieces((value,) * 4, axis)


def after(value, *others):
    return lax.optimization_barrier((value,) + others)[0]


def far(value):
    return pltpu.with_memory_space_constraint(value, pltpu.HBM)


def weight_spec(column):
    return pl.BlockSpec((D, 256), lambda *_, column=column: (0, column))


def on_device(stream, cotangent, passes, w_qkv, w_out, w_up, w_down, ln_gains, pass_embed):
    z = lax.axis_index("blk").astype(jnp.int32)
    batch = lax.axis_index("batch").astype(jnp.int32)
    place = jnp.stack([z, batch // 2 % 4, batch // 8, batch % 2])
    gains = ln_gains.T
    embed = pass_embed.T
    piece = shape((192, R))
    full = shape((R, D))

    def arrived(*values):
        nonlocal place
        place = lax.optimization_barrier((place,) + values)[0]

    def ordered(outs):
        nonlocal place
        *outs, first = outs
        place, first = lax.optimization_barrier((place, first))
        return (*outs, first)

    hidden, *early, normed = ordered(pl.pallas_call(
        first_kernel,
        grid=(1,),
        in_specs=[SM, SM, VM, VM, VM, weight_spec(0), weight_spec(3), weight_spec(6)],
        out_specs=[VM] * 6,
        out_shape=[kept((R, D), F32), piece, piece, piece, piece, full],
        scratch_shapes=[pltpu.VMEM((4, 192, R), BF)],
        compiler_params=room(24),
        name="ln_qkv",
    )(place, passes, far(stream), far(embed), far(gains), *([far(w_qkv)] * 3)))
    *sent, turned = ordered(pl.pallas_call(
        second_kernel,
        grid=(1,),
        in_specs=[SM, VM] + [weight_spec(c) for c in (1, 4, 7, 2, 5, 8)],
        out_specs=[VM] * 9,
        out_shape=[piece] * 8 + [kept((D, R))],
        scratch_shapes=[pltpu.VMEM((2, 4, 192, R), BF)],
        compiler_params=room(24),
        name="qkv_rest",
    )(place, normed, *([far(w_qkv)] * 6)))
    heads = [spread_pieces(early, "z"), spread_pieces(sent[0:4], "z")]
    last_group = [sent[4], shift(sent[5], "z", 1), sent[6], sent[7]]

    wholes, attended, spreads, sent = [], [], [], []
    for g in range(3):
        *parts, whole, result, spread = ordered(run(
            lambda *refs, g=g: attend_kernel(g == 2, *refs),
            "attend",
            24,
            [shape((192 if g == 2 else HD, R))] * 4
            + [kept((4, 192, R)), kept((4, HD, R), F32), kept((4, 1, R), F32)],
            (place, *heads[g], *(sent if g == 2 else ())),
            [
                pltpu.VMEM((4, 128, R), BF),
                pltpu.VMEM((4, 128, R), BF),
                pltpu.VMEM((4, HD, R), BF),
                pltpu.VMEM((4, R, 128), BF),
                pltpu.VMEM((4, R, R), F32),
                pltpu.VMEM((4, HD, R), BF),
            ],
        ))
        if g == 0:
            last_group[2], last_group[3] = (shift(after(last_group[d], place), "z", d) for d in (2, 3))
            heads.append(last_group)
        wholes.append(whole)
        attended.append(result)
        spreads.append(spread)
        sent += parts
    sent = sent[8:]
    back_o = spread_pieces(sent, "z")
    d_active = ordered((pl.pallas_call(
        active_grad_kernel,
        grid=(FF // CHUNK,),
        in_specs=[SM, VM, pl.BlockSpec((CHUNK, D), lambda f: (f, 0))],
        out_specs=pl.BlockSpec((R, CHUNK), lambda f: (0, f)),
        out_shape=shape((R, FF), F32),
        scratch_shapes=[pltpu.VMEM((R, D), BF), pltpu.VMEM((R, D), F32)],
        compiler_params=room(16),
        name="active_grad",
    )(place, far(cotangent), far(w_down)),))[0]
    near = after(turned, place, *back_o)
    near = (shift(near, "z", 1), shift(near, "z", 3))

    active, d_up, second, middle, o_turned, d_branch, d_middle, *sent, a_other, b_other, gain_term = ordered(pl.pallas_call(
        ff_kernel,
        grid=(FF // CHUNK,),
        in_specs=[SM] + [VM] * 4 + [VM, VM, VM, VM]
        + [pl.BlockSpec((D, CHUNK), lambda f: (0, f)), pl.BlockSpec((R, CHUNK), lambda f: (0, f))],
        out_specs=[VM] * 14,
        out_shape=[shape((R, FF)), shape((R, FF)), full, shape((R, D), F32), shape((D, R)), full, kept((R, D), F32)]
        + [kept((192, R))] + [piece] * 3 + [shape((4, 4, 4, 48, 384)), shape((4, 4, 4, 64, 384)), shape((1, D), F32)],
        scratch_shapes=[pltpu.VMEM((R, D), BF), pltpu.VMEM((R, D), F32), pltpu.VMEM((HEADS, HD, R), BF), pltpu.VMEM((D, R), BF)],
        compiler_params=room(26),
        name="ff",
    )(place, *back_o, hidden, cotangent, gains, w_out, far(w_up), d_active))
    *sent, a_other, b_other = lax.optimization_barrier((*sent, a_other, b_other, *near))[:6]
    d_o = spread_pieces(sent, "z")

    got = (shift(a_other, "core", 1), shift(b_other, "core", 1))
    own = ordered(run(
        ff_grad_kernel,
        "ff_grad",
        32,
        [shape((4, 4, 4, 48, 384)), shape((4, 4, 4, 64, 384))],
        (place, active, d_up, second, far(cotangent), o_turned, d_branch),
        [pltpu.VMEM((R, D), F32)],
    ))
    sent = ordered(run(
        core_sum_kernel,
        "core_sum",
        24,
        [kept((4, 4, 48, 384))] + [shape((4, 4, 48, 384))] * 3 + [kept((4, 4, 64, 384))] + [shape((4, 4, 64, 384))] * 3,
        (place, *own, *got),
    ))
    arrived(*d_o)
    distant = shift(after(turned, *d_o, place), "z", 2)
    a_sent, b_sent = sent[0:4], sent[4:8]
    a_parts = [a_sent[0], shift(a_sent[1], "x", 1), None, shift(a_sent[3], "x", 3)]
    b_parts = [b_sent[0], shift(b_sent[1], "y", 1), None, shift(b_sent[3], "y", 3)]

    def attend_back(which):
        count = len(which)
        group = pl.BlockSpec((64 * count, R), lambda _: (which[0] // count, 0))
        operands = [t for g in which for t in (wholes[g], attended[g], spreads[g])]
        return ordered(pl.pallas_call(
            lambda *refs: attend_back_kernel(count, *refs),
            grid=(1,),
            in_specs=[SM] + [VM] * (3 * count) + [group] * 4,
            out_specs=[VM] * 5,
            out_shape=[kept((192 * count, R))] + [shape((192 * count, R))] * 3 + [kept((count, 4, 192, R))],
            scratch_shapes=[
                pltpu.VMEM((count, 4, 128, R), BF),
                pltpu.VMEM((count, 4, 128, R), BF),
                pltpu.VMEM((count, 4, HD, R), BF),
                pltpu.VMEM((count, 4, R, 128), BF),
                pltpu.VMEM((count, 4, R, 128), BF),
                pltpu.VMEM((count, 4, R, HD), BF),
                pltpu.VMEM((count, 4, HD, R), BF),
                pltpu.VMEM((count, 4, R, HD), BF),
                pltpu.VMEM((count, 4, 1, R), F32),
                pltpu.VMEM((count, 4, HD, R), F32),
            ],
            compiler_params=room(32 if count == 2 else 24),
            name="attend_back",
        )(place, *(far(t) for t in operands), *(far(t) for t in d_o)))

    *sent, made_first = attend_back((0, 1))
    first_pieces = spread_pieces(sent, "z")
    a_parts[2] = shift(after(a_sent[2], place), "x", 2)
    b_parts[2] = shift(after(b_sent[2], place), "y", 2)
    arrived(a_parts[1], a_parts[3], b_parts[1], b_parts[3], distant)
    *sent, made_last = attend_back((2,))
    keep, send = ordered(run(
        head_grad_kernel,
        "head_grad",
        32,
        [shape((4, 4, GROUP, 128))] * 2,
        (place, far(turned), near[0], distant, near[1], far(made_first), far(made_last)),
        [pltpu.VMEM((4, 640, R), BF), pltpu.VMEM((D, 640), F32), pltpu.VMEM((8, 4, GROUP, 128), BF)],
    ))
    arrived(*first_pieces, a_parts[2], b_parts[2])
    *sent, send = lax.optimization_barrier((*sent, send, *first_pieces, a_parts[2], b_parts[2]))[:5]
    last_pieces = spread_pieces(sent, "z")
    got = shift(send, "core", 1)

    sent = ordered(run(
        cut_kernel,
        "sum_first",
        24,
        [shape((4 * PART_A + 4 * GROUP, 128))] * 4 + [shape((4, 64, 384))] * 4,
        (place, *a_parts, *b_parts, keep, got),
    ))
    so_far = ordered((pl.pallas_call(
        input_grad_kernel,
        grid=(1,),
        in_specs=[SM] + [VM] * 4 + [weight_spec(c) for c in (0, 3, 6, 1, 4, 7)],
        out_specs=VM,
        out_shape=shape((D, R), F32),
        scratch_shapes=[pltpu.VMEM((6, 4, HD, R), BF)],
        compiler_params=room(24),
        name="input_grad",
    )(place, *first_pieces, *([far(w_qkv)] * 6)),))[0]
    own_y, *others = lax.optimization_barrier((*sent, place))[:8]
    y_parts, x_parts = spread_pieces([own_y, *others[0:3]], "y"), spread_pieces(others[3:7], "x")
    grad_stream, small = ordered(pl.pallas_call(
        last_kernel,
        grid=(1,),
        in_specs=[SM, SM] + [VM] * 9 + [weight_spec(c) for c in (2, 5, 8)],
        out_specs=[VM, VM],
        out_shape=[kept((1, ROWS, D), F32), shape((8, D), F32)],
        scratch_shapes=[pltpu.VMEM((3, 4, HD, R), BF)],
        compiler_params=room(24),
        name="ln_back",
    )(place, passes, *last_pieces, so_far, hidden, d_middle, gain_term, gains, *([far(w_qkv)] * 3)))
    sent = ordered(run(
        block_kernel,
        "sum_second",
        16,
        [shape((PART_A + PART_B + GROUP + TINY, 128))] * 4,
        (place, *y_parts, *x_parts, small),
    ))
    z_parts = spread_pieces(sent, "z")
    layer_out = ordered((pl.pallas_call(
        layer_out_kernel,
        grid=(FF // CHUNK,),
        in_specs=[SM, VM, pl.BlockSpec((R, CHUNK), lambda f: (0, f)), pl.BlockSpec((CHUNK, D), lambda f: (f, 0))],
        out_specs=VM,
        out_shape=kept((1, ROWS, D)),
        scratch_shapes=[pltpu.VMEM((R, D), F32)],
        compiler_params=room(16),
        name="layer_out",
    )(place, middle, active, far(w_down)),))[0]
    head, bulk = ordered(run(
        own_kernel, "sum_blocks", 16, [shape((4 * GROUP + TINY, 128)), shape((PARTS, 128))], (place, *z_parts)
    ))
    bulks = all_of(bulk, "y")
    heads_x = all_of(head, "x")
    row = ordered(run(row_kernel, "stack_rows", 16, [shape((4 * PARTS, 128))], (place, *bulks)))[0]
    rows = [row, shift(row, "x", 1), None, shift(row, "x", 3)]
    head = ordered(run(head_row_kernel, "sum_heads", 16, [shape((4 * GROUP + TINY, 128))], (place, *heads_x)))[0]
    rows[2] = shift(after(row, place), "x", 2)
    heads_y = all_of(head, "y")
    buffer = ordered(run(stack_kernel, "stack", 16, [shape((ALL, 128))], (place, *heads_y, *rows)))[0]
    def half(count, lanes):
        return pl.BlockSpec((count, lanes), lambda i: (i, 0))

    *results, grad_gains, grad_pass = pl.pallas_call(
        finish_kernel,
        grid=(2,),
        in_specs=[SM, VM, VM],
        out_specs=[half(96, 3 * D), half(96, D), half(96, FF), half(384, D), VM, VM],
        out_shape=[
            kept((192, 3 * D), F32),
            kept((192, D), F32),
            kept((192, FF), F32),
            kept((D, D), F32),
            shape((2, 192), F32),
            shape((PASSES, 192), F32),
        ],
        scratch_shapes=[pltpu.VMEM((2, ALL, 128), BF), pltpu.VMEM((D, 8), F32)],
        compiler_params=room(32),
        name="finish",
    )(place, buffer, shift(buffer, "core", 1))
    return (layer_out, grad_stream, *results, grad_gains.T, grad_pass.T)


def solution(mesh):
    tokens = P("batch", "blk", None)
    in_specs = (tokens, tokens, P("batch"), P(), P(), P(), P(), P(), P())
    out_specs = (tokens, tokens) + (P("blk", None),) * 6
    return jax.shard_map(on_device, mesh=mesh, in_specs=in_specs, out_specs=out_specs, check_vma=False)
```
